32 devices in a mesh: wide: 8 (over y, x, core), narrow: 4 (over z).
Axes of the slice: x: 2, y: 2, z: 4, core: 2. Of those that a mesh axis runs over, the one named last changes fastest.
Arguments:
- tokens: bfloat16 [8192, 1152], P(('wide', 'narrow')), may hold values from -6 to 6
- condition: bfloat16 [32, 1152], P('wide'), may hold values from -6 to 6
- segment: int32 [8192], P('wide'), may hold values from 0 to 4, as said below
- w_ada: bfloat16 [1152, 6912], P(None, 'narrow'), may hold values from -0.1875 to 0.1875
- b_ada: bfloat16 [6912], P('narrow'), may hold values from -3 to 3
- w_qkv: bfloat16 [1152, 3, 1152], P(None, None, 'narrow'), may hold values from -0.1875 to 0.1875
- w_proj: bfloat16 [1152, 1152], P(None, 'narrow'), may hold values from -0.75 to 0.75
- w_up: bfloat16 [1152, 4608], P(None, 'narrow'), may hold values from -0.1875 to 0.1875
- w_down: bfloat16 [4608, 1152], P('narrow'), may hold values from -0.09375 to 0.09375
- out_grad: bfloat16 [8192, 1152], P(('wide', 'narrow')), may hold values from -6 to 6
Outputs:
- mixed: bfloat16 [8192, 1152], P(('wide', 'narrow'))
- tokens_grad: bfloat16 [8192, 1152], P(('wide', 'narrow'))
- w_ada_grad: float32 [1152, 6912], P('wide', 'narrow')
- b_ada_grad: float32 [6912], P(('narrow', 'wide'))
- w_qkv_grad: float32 [1152, 3, 1152], P('wide', None, 'narrow')
- w_proj_grad: float32 [1152, 1152], P('wide', 'narrow')
- w_up_grad: float32 [1152, 4608], P('wide', 'narrow')
- w_down_grad: float32 [4608, 1152], P(('narrow', 'wide'))
The draws below stay inside these ranges and needn't reach their ends.
Inputs may be any that keep to these rules, and one draw needn't show every extreme that they name: `segment`: within each wide shard's 1024 rows its 4 image slots lie in order from row 0, each on consecutive rows, with 256 rows (unmasked) or 128 rows (kept tokens of a masked image); the value 4 marks the padding rows after the last image. In every draw some shard has only unmasked images and some shard has padding.
All inputs are finite; a program needn't handle non-finite values.
Results may differ from the reference program's by a relative error of at most 0.02.
Values may be sent and summed in bfloat16 or wider, within the bound.
A program may use at most 128 MiB of HBM per device.

```python
import jax
import jax.numpy as jnp
from jax import lax

D = 1152
HEADS = 16
FF = 4608
IMG_LEN = 256
IMG_DEV = 4
KEPT = 128
ROWS = 1024
TOKENS = 8192
IMAGES = 32
N_WIDE = 8


def draw_segment(key, part):
    key = jax.random.fold_in(key, 11)
    full_key, pick_key = jax.random.split(key)
    full_image = jax.random.randint(full_key, (N_WIDE, IMG_DEV), 0, 2)
    chosen = jax.random.randint(pick_key, (), 0, N_WIDE)
    shard_ids = jnp.arange(N_WIDE, dtype=jnp.int32)[:, None]
    image_ids = jnp.arange(IMG_DEV, dtype=jnp.int32)[None, :]
    full_image = jnp.where(shard_ids == chosen, 1, full_image)
    short_shard = (chosen + 1) % N_WIDE
    full_image = jnp.where((shard_ids == short_shard) & (image_ids == 0), 0, full_image)
    lengths = jnp.where(full_image == 1, IMG_LEN, KEPT).astype(jnp.int32)
    image_ends = jnp.cumsum(lengths, axis=1)
    row_ids = jnp.arange(ROWS, dtype=jnp.int32)
    segment = jnp.sum((row_ids[None, :, None] >= image_ends[:, None, :]).astype(jnp.int32), axis=-1)
    return segment.reshape(TOKENS).astype(jnp.int32)


def with_spikes(array, key, source, target, blocks, factor):
    def block_of(dim):
        return (jnp.arange(array.shape[dim]) // (array.shape[dim] // blocks)).reshape((-1,) + (1,) * (array.ndim - 1 - dim))

    near = jax.random.permutation(key, blocks)[block_of(target)]
    second = (block_of(target) + blocks // 2) % blocks
    return jnp.where((block_of(source) == near) | (block_of(source) == second), factor * array, array)


def levels(stream_key, shape, shards, smallest, largest):
    def one(axis_at, parts):
        steps = jax.random.uniform(jax.random.fold_in(jax.random.fold_in(stream_key, 6), axis_at), (parts,), jnp.float32, smallest / len(shards), largest / len(shards))
        return jnp.repeat(jnp.exp(steps), shape[axis_at] // parts).reshape((-1,) + (1,) * (len(shape) - axis_at - 1))

    gain = one(*shards[0])
    for cut in shards[1:]:
        gain = gain * one(*cut)
    return gain


def normal_values(rng, dims, scale, most, cuts=(), kind=jnp.bfloat16):
    array = scale * jax.random.normal(rng, dims, jnp.float32)
    if cuts:
        array = array * levels(rng, dims, cuts, -0.22, 0.18)
    return jnp.clip(array, -most, most).astype(kind)


def bell_draw_with(rng, shape, deviation, limit, cuts, heavy, kind=jnp.bfloat16):
    values = deviation * jax.random.normal(rng, shape, jnp.float32)
    if cuts:
        values = values * levels(rng, shape, cuts, -0.22, 0.18)
    return jnp.clip(with_spikes(values, jax.random.fold_in(rng, 3), *heavy), -limit, limit).astype(kind)


def setup_inputs(seed: int = 0) -> dict:
    key_of = jax.random.split(jax.random.key(seed), 11)
    tokens = bell_draw_with(key_of[0], (TOKENS, D), 1.0, 6.0, ((0, 32),), (0, 1, 32, 2.75))
    condition = normal_values(key_of[1], (IMAGES, D), 1.0, 6.0, ((0, 8),))
    segment = draw_segment(jax.random.fold_in(key_of[10], 71), 0)
    w_ada = normal_values(key_of[3], (D, 6 * D), D ** -0.5, 0.1875, ((1, 4),))
    b_ada = normal_values(key_of[4], (6 * D,), 0.5, 3.0, ((0, 4),))
    w_qkv = normal_values(key_of[5], (D, 3, D), D ** -0.5, 0.1875, ((2, 4),))
    w_proj = normal_values(key_of[6], (D, D), (D // 16) ** -0.5, 0.75, ((1, 4),))
    w_up = normal_values(key_of[7], (D, FF), D ** -0.5, 0.1875, ((1, 4),))
    w_down = normal_values(key_of[8], (FF, D), FF ** -0.5, 0.09375, ((0, 4),))
    out_grad = normal_values(key_of[9], (TOKENS, D), 1.0, 6.0, ((0, 32),))
    return {"tokens": tokens, "condition": condition, "segment": segment, "w_ada": w_ada, "b_ada": b_ada, "w_qkv": w_qkv, "w_proj": w_proj, "w_up": w_up, "w_down": w_down, "out_grad": out_grad}


norm_epsilon = 1e-06
masked_score = -1e+30
highest = lax.Precision.HIGHEST

@jax.custom_vjp
def low(v):
    return lax.optimization_barrier(v.astype(jnp.bfloat16)).astype(jnp.float32)

@jax.custom_vjp
def low_back(v):
    return v

def low_keep(v):
    return (low(v), None)

def low_pass(kept, grad):
    return (grad,)

def back_keep(v):
    return (v, None)

def back_low(kept, grad):
    return (low(grad),)
low.defvjp(low_keep, low_pass)
low_back.defvjp(back_keep, back_low)

def both_ways(value):
    return low(low_back(value))

def normalize(inputs):
    centred = inputs - lax.optimization_barrier(jnp.mean(inputs, axis=-1, keepdims=True))
    return centred * lax.rsqrt(lax.optimization_barrier(jnp.mean(centred * centred, axis=-1, keepdims=True)) + norm_epsilon)

def modulate(inputs, scale_rows, shift_rows):
    return normalize(inputs) * (1.0 + scale_rows) + shift_rows

def attend(queries, key_rows, value_rows, seg_rows, factor):
    row_total, head_count, head_size = queries.shape
    block_rows = min(512, row_total)
    blocks = row_total // block_rows

    def one_block(block_pair):
        query_block, seg_block = block_pair
        scores = low_back(jnp.einsum('qhe,khe->hqk', query_block, key_rows, precision=highest) * factor)
        allowed = (seg_block[:, None] == seg_rows[None, :])[None, :, :]
        scores = jnp.where(allowed, scores, masked_score)
        row_max = lax.optimization_barrier(jnp.max(scores, axis=-1, keepdims=True))
        weights = jnp.exp(scores - row_max)
        probability = weights / lax.optimization_barrier(jnp.sum(weights, axis=-1, keepdims=True))
        return jnp.einsum('hqk,khe->qhe', low(probability), value_rows, precision=highest)
    results = lax.map(jax.checkpoint(one_block), (queries.reshape(blocks, block_rows, head_count, head_size), seg_rows.reshape(blocks, block_rows)))
    return results.reshape(row_total, head_count, head_size)

def shard_forward(params, token_values, silu_rows, seg_rows):
    w_ada, b_ada, w_qkv, w_proj, w_up, w_down = params
    images = silu_rows.shape[0]
    row_total = token_values.shape[0]
    head_size = D // HEADS
    modulation = low_back(jnp.dot(silu_rows, w_ada, precision=highest) + b_ada)
    onehot = (seg_rows[:, None] == jnp.arange(images, dtype=jnp.int32)[None, :]).astype(jnp.float32)
    per_token = jnp.dot(onehot, modulation, precision=highest)
    shift_one, scale_one, gate_one, shift_two, scale_two, gate_two = jnp.split(per_token, 6, axis=1)
    hidden_one = low(modulate(token_values, scale_one, shift_one))
    projected = both_ways(jnp.einsum('gd,dcf->gcf', hidden_one, w_qkv, precision=highest))
    queries = projected[:, 0].reshape(row_total, HEADS, head_size)
    key_rows = projected[:, 1].reshape(row_total, HEADS, head_size)
    value_rows = projected[:, 2].reshape(row_total, HEADS, head_size)
    attended = attend(queries, key_rows, value_rows, seg_rows, head_size ** (-0.5))
    heads_out = both_ways(attended.reshape(row_total, D))
    attn_branch = low_back(jnp.einsum('gi,oi->go', heads_out, w_proj, precision=highest))
    middle = token_values + gate_one * attn_branch
    hidden_two = low(modulate(middle, scale_two, shift_two))
    up_values = low_back(jnp.dot(hidden_two, w_up, precision=highest))
    activated = low(jax.nn.gelu(up_values, approximate=True))
    mlp_branch = low_back(jnp.dot(activated, w_down, precision=highest))
    return middle + gate_two * mlp_branch

def reference(tokens, condition, segment, w_ada, b_ada, w_qkv, w_proj, w_up, w_down, out_grad):
    weights = tuple((matrix.astype(jnp.float32) for matrix in (w_ada, b_ada, w_qkv, w_proj, w_up, w_down)))
    silu_all = low(jax.nn.silu(condition.astype(jnp.float32))).reshape(N_WIDE, IMG_DEV, D)
    token_shards = tokens.astype(jnp.float32).reshape(N_WIDE, ROWS, D)
    seg_shards = segment.reshape(N_WIDE, ROWS)
    grad_shards = out_grad.astype(jnp.float32).reshape(N_WIDE, ROWS, D)

    def one_shard(running, shard_items):
        token_rows, silu_rows, seg_rows, grad_rows = shard_items

        def forward(params, inputs):
            return shard_forward(params, inputs, silu_rows, seg_rows)
        result, pullback = jax.vjp(forward, weights, token_rows)
        weight_grads, token_grads = pullback(grad_rows)
        running = jax.tree.map(lambda before, addend: before + addend, running, weight_grads)
        return (running, (result.astype(jnp.bfloat16), token_grads.astype(jnp.bfloat16)))
    start_grads = tuple((jnp.zeros_like(matrix) for matrix in weights))
    totals, outputs = lax.scan(one_shard, start_grads, (token_shards, silu_all, seg_shards, grad_shards))
    mixed, tokens_grad = outputs
    w_ada_grad, b_ada_grad, w_qkv_grad, w_proj_grad, w_up_grad, w_down_grad = totals
    return (mixed.reshape(TOKENS, D), tokens_grad.reshape(TOKENS, D), w_ada_grad, b_ada_grad, w_qkv_grad, w_proj_grad, w_up_grad, w_down_grad)
```

```python
import functools
import math

import jax
import jax.numpy as jnp
from jax import lax
from jax.experimental import pallas as pl
from jax.experimental.pallas import tpu as pltpu
from jax.sharding import PartitionSpec as P

D = 1152
HEAD = 72
HEADS_LOCAL = 4
QUARTER = 288
HALF = 576
BLK = 144
SUB_A = 80
SEG = 128
OWN = 256
GROUP = 512
ATT = 640
NEG = -1e30
EPS = 1e-6
FACTOR = HEAD ** -0.5
GELU_ONE = math.sqrt(2.0 / math.pi)
GELU_TWO = 0.044715

f32, bf16 = jnp.float32, jnp.bfloat16
MESH = pl.DeviceIdType.MESH
NN = (((1,), (0,)), ((), ()))
NT = (((1,), (1,)), ((), ()))
TN = (((0,), (0,)), ((), ()))
WINDOWS = ((0, 128), (0, 256), (128, 128), (128, 256))


def dot(a, b, dims):
    return lax.dot_general(a, b, dims, preferred_element_type=f32)


def rows_at(start, size, align=16):
    return pl.ds(pl.multiple_of(start, align), size)


def mean_row(v):
    return jnp.sum(v, axis=-1, keepdims=True) * (1.0 / D)


def norm_parts(v):
    centred = v - mean_row(v)
    scale = lax.rsqrt(mean_row(centred * centred) + EPS)
    return centred * scale, scale


def norm_back(normal, scale, e):
    return scale * (e - mean_row(e) - normal * mean_row(e * normal))


def head_mask(hd, rows):
    start, width = WINDOWS[hd]
    low = HEAD * hd - start
    lane = lax.broadcasted_iota(jnp.int32, (rows, width), 1)
    return (lane >= low) & (lane < low + HEAD)


class Names:
    def __init__(self):
        self.ids = {}

    def __call__(self, *name):
        return self.ids.setdefault(name, len(self.ids))


SEMS = 160


def kernel(
    gather_wide, step,
    seg, cond, bada, tok_h, og_h, wada_h, wqkv_h, wproj_h, wup_h, wdown_h,
    mixed_o, tg_o, gw_o, mod_o, wada_o, bada_o,
    wt, crecv, frecv, srecv, zrecv, tok, og, h1, qkv, heads, lse_t, attp, attr, h2, mlpg, big,
    mlpp, mlpr, seco, secr, mgrad, attg, hgrad, facc, firstr, modblk, modrecv, silu_all, msum, mgr, mall, silu8,
    ssem, rsem, lsem,
):
    w = lax.axis_index("wide")
    n = lax.axis_index("narrow")
    b = w // step
    bits = (b % 2, (b // 2) % 2, b // 4)
    low, high = n % 2, n // 2

    def narrow_to(mask):
        m = n
        if mask & 1:
            m = m + 1 - 2 * low
        if mask & 2:
            m = m + 2 - 4 * high
        return (w, m)

    def wide_to(mask):
        m = w
        for k in range(3):
            if mask & (1 << k):
                m = m + step * (1 << k) * (1 - 2 * bits[k])
        return (m, n)

    def block_of(mask):
        m = b
        for k in range(3):
            if mask & (1 << k):
                m = m + (1 << k) * (1 - 2 * bits[k])
        return m

    names = Names()

    def remote(name, src, dst, dev):
        k = names(*name)
        return pltpu.make_async_remote_copy(
            src_ref=src, dst_ref=dst, send_sem=ssem.at[k], recv_sem=rsem.at[k], device_id=dev, device_id_type=MESH
        )

    sends = {}

    def send(name, src, dst, dev):
        copy = remote(name, src, dst, dev)
        copy.start()
        sends[name] = copy

    def recv(name, landing):
        remote(name, landing, landing, narrow_to(1)).wait_recv()

    def sent(prefix):
        for name in [s for s in sends if s[: len(prefix)] == prefix]:
            sends.pop(name).wait_send()

    locals_ = Names()

    def load(name, src, dst):
        copy = pltpu.make_async_copy(src, dst, lsem.at[locals_(name)])
        copy.start()
        return copy

    off = 128 * high
    own_at = off + OWN * low
    other_at = off + OWN * (1 - low)
    halo_at = GROUP * (1 - high)
    halo_there = GROUP * high

    load_a = load("a", wqkv_h, wt.at[0, pl.ds(0, 3 * QUARTER)])
    load_b = load("b", wproj_h, wt.at[0, pl.ds(3 * QUARTER, QUARTER)])
    load_m = load("m", wada_h, big.at[pl.ds(0, 3 * HALF)])
    load_t = load("t", tok_h, tok.at[rows_at(own_at, OWN)])
    load_u = load("u", wup_h, wt.at[1])
    load_d = load("d", wdown_h, wt.at[2])
    load_g = load("g", og_h, og.at[rows_at(OWN * low, OWN)])

    barrier = pltpu.get_barrier_semaphore()
    partners = [narrow_to(m) for m in (1, 2, 3)] + [wide_to(m) for m in (range(1, 8) if gather_wide else (1, 2, 4))]
    for dev in partners:
        pl.semaphore_signal(barrier, inc=1, device_id=dev, device_id_type=MESH)
    pl.semaphore_wait(barrier, len(partners))

    def block_rows(mask, part=None):
        base = block_of(mask) * BLK
        if part is None:
            return rows_at(base, BLK)
        return rows_at(base, SUB_A) if part == 0 else rows_at(base + SUB_A, BLK - SUB_A)

    def ag_z(m):
        r = block_rows(0)
        send(("ag", m, "z"), wt.at[m, r], wt.at[3 + m, r], narrow_to(2))

    def ag_one(m):
        recv(("ag", m, "z"), wt.at[3 + m, block_rows(0)])
        for part, axis in ((0, 2), (1, 4)):
            r = block_rows(0, part)
            send(("ag", m, "1", part), wt.at[3 + m, r], wt.at[3 + m, r], wide_to(axis))

    def ag_two(m):
        for part, axis, other in ((0, 2, 4), (1, 4, 2)):
            recv(("ag", m, "1", part), wt.at[3 + m, block_rows(axis, part)])
            for i, mask in enumerate((0, axis)):
                r = block_rows(mask, part)
                send(("ag", m, "2", part, i), wt.at[3 + m, r], wt.at[3 + m, r], wide_to(other))

    def ag_three(m):
        for part, axis, other in ((0, 2, 4), (1, 4, 2)):
            for i, mask in enumerate((other, 6)):
                recv(("ag", m, "2", part, i), wt.at[3 + m, block_rows(mask, part)])
        for i, mask in enumerate((0, 2, 4, 6)):
            r = block_rows(mask)
            send(("ag", m, "3", i), wt.at[3 + m, r], wt.at[3 + m, r], wide_to(1))

    def ag_end(m):
        for i, mask in enumerate((1, 3, 5, 7)):
            recv(("ag", m, "3", i), wt.at[3 + m, block_rows(mask)])

    load_a.wait()
    load_b.wait()
    ag_z(0)
    send(("tok",), tok_h, tok.at[rows_at(own_at, OWN)], narrow_to(1))
    halo_first = remote(
        ("halo", 0), tok_h.at[rows_at(128 * (1 - high), SEG)], tok.at[rows_at(halo_there, SEG)], narrow_to(2)
    )
    halo_second = remote(
        ("halo", 1), tok.at[rows_at(halo_at, SEG)], tok.at[rows_at(halo_at, SEG)], narrow_to(1)
    )
    halo_source = low != high

    @pl.when(halo_source)
    def _():
        halo_first.start()

    c = cond[...].astype(f32)
    silu = (c / (1.0 + jnp.exp(-c))).astype(bf16).astype(f32)
    silu8[...] = jnp.zeros((16, D), f32)
    silu8[0:4, :] = silu
    if gather_wide:
        silu_all[b] = silu8[0:8, :]
        for mask in range(1, 8):
            send(("silu", mask), silu8.at[pl.ds(0, 8)], silu_all.at[b], wide_to(mask))
    load_m.wait()
    silu_low = silu8[...].astype(bf16)
    row8 = lax.broadcasted_iota(jnp.int32, (8, HALF), 0)
    for i in range(3):
        part = dot(silu_low, big[HALF * i : HALF * (i + 1), :], NT)[0:8, :] + bada[i : i + 1, :]
        modrecv[3 * n + i, :, 0:HALF] = jnp.where(row8 < 4, part, 0.0)
        modrecv[3 * n + i, :, HALF:ATT] = jnp.zeros((8, ATT - HALF), f32)
    for mask in (1, 2, 3):
        mine = modrecv.at[pl.ds(3 * n, 3)]
        send(("mod", mask), mine, mine, narrow_to(mask))
    load_u.wait()
    ag_z(1)
    load_d.wait()
    ag_z(2)
    load_g.wait()
    send(("og",), og_h, og.at[rows_at(OWN * low, OWN)], narrow_to(1))
    for mask in (1, 2, 3):
        m = narrow_to(mask)[1]
        recv(("mod", mask), modrecv.at[pl.ds(3 * m, 3)])
    for k in range(6):
        first = modrecv[2 * k]
        second = pltpu.roll(modrecv[2 * k + 1], 64, 1)
        modblk[k, :, 0:512] = first[:, 0:512]
        modblk[k, :, 512:640] = first[:, 512:640] + second[:, 0:128]
        modblk[k, :, 640:D] = second[:, 128:640]

    def mod_row(k, shard_block):
        return modblk[k, pl.ds(seg[shard_block * SEG], 1), :]

    def first_norm(base, size):
        def body(t, carry):
            r = rows_at(base + t * 32, 32, 32)
            block = 3 * high + (base + t * 32) // SEG
            normal, _ = norm_parts(tok[r, :].astype(f32))
            h1[r, :] = (normal * (1.0 + mod_row(1, block)) + mod_row(0, block)).astype(bf16)
            return carry

        lax.fori_loop(0, size // 32, body, 0)

    load_t.wait()
    first_norm(own_at, OWN)
    ag_one(0)
    recv(("tok",), tok.at[rows_at(other_at, OWN)])
    first_norm(other_at, OWN)

    @pl.when(jnp.logical_not(halo_source))
    def _():
        halo_first.wait_recv()
        halo_second.start()

    @pl.when(halo_source)
    def _():
        halo_second.wait_recv()
        halo_first.wait_send()

    first_norm(halo_at, SEG)

    @pl.when(jnp.logical_not(halo_source))
    def _():
        halo_second.wait_send()

    ag_two(0)

    def project(s):
        def body(i, carry):
            qkv[s, i] = dot(h1[...], wt[3 * s, rows_at(QUARTER * i, 384), :], NT).astype(bf16)
            return carry

        lax.fori_loop(0, 3, body, 0)

    def key_bias(j, k0, count):
        mine = seg[SEG * (j + 3 * high)]
        return [jnp.where(seg[SEG * (k0 + i + 3 * high)] == mine, 0.0, NEG) for i in range(count)]

    def attend(s, j, k0, count):
        r = rows_at(j * SEG, SEG, SEG)
        keys = slice(k0 * SEG, (k0 + count) * SEG)
        bias = key_bias(j, k0, count)
        out = [jnp.zeros((SEG, 128), f32) for _ in range(3)]
        lse = jnp.zeros((SEG, 128), f32)
        lane = lax.broadcasted_iota(jnp.int32, (SEG, 128), 1)
        for hd, (a, width) in enumerate(WINDOWS):
            mask = head_mask(hd, SEG)
            q = jnp.where(mask, qkv[s, 0, r, a : a + width].astype(f32), 0.0).astype(bf16)
            scores = dot(q, qkv[s, 1, keys, a : a + width], NT) * FACTOR
            scores = jnp.concatenate(
                [scores[:, i * SEG : (i + 1) * SEG] + bias[i] for i in range(count)], axis=1
            )
            top = jnp.max(scores, axis=1, keepdims=True)
            weights = jnp.exp(scores - top)
            total = jnp.sum(weights, axis=1, keepdims=True)
            prob = (weights * (1.0 / total)).astype(bf16)
            res = jnp.where(mask, dot(prob, qkv[s, 2, keys, a : a + width], NN), 0.0)
            for i in range(width // 128):
                out[a // 128 + i] += res[:, i * 128 : (i + 1) * 128]
            lse = jnp.where(lane == hd, top + jnp.log(total), lse)
        for i in range(3):
            heads[s, r, i * 128 : (i + 1) * 128] = out[i].astype(bf16)
        lse_t[s, :, r] = lse.T[0:8, :]

    def for_blocks(fn):
        fn(0, 0, 2)
        fn(1, 0, 5)

        def body(j, carry):
            fn(j, 1, 4)
            return carry

        lax.fori_loop(2, 5, body, 0)

    project(0)
    ag_three(0)
    ag_one(1)
    for_blocks(functools.partial(attend, 0))
    ag_end(0)
    ag_two(1)
    project(1)
    ag_one(2)
    ag_three(1)
    for_blocks(functools.partial(attend, 1))
    ag_two(2)

    def order(i):
        return 1 - high if i == 0 else high

    for i in range(2):
        cc = order(i)
        src = rows_at(off + OWN * cc, OWN)
        dst = rows_at(OWN * cc, OWN)

        def body(t, carry):
            cols = pl.ds(pl.multiple_of(t * 384, 128), 384)
            part = dot(heads[0, src, 0:QUARTER], wt[0, 3 * QUARTER : D, cols], NN)
            part += dot(heads[1, src, 0:QUARTER], wt[3, 3 * QUARTER : D, cols], NN)
            attp[dst, cols] = part.astype(bf16)
            return carry

        lax.fori_loop(0, 3, body, 0)
        send(("att", i), attp.at[dst], attr.at[dst], narrow_to(1))

    ag_three(2)
    ag_end(1)
    ag_end(2)
    recv(("og",), og.at[rows_at(OWN * (1 - low), OWN)])

    for i in range(2):
        cc = order(i)
        chunk = rows_at(OWN * cc, OWN)
        recv(("att", i), attr.at[chunk])

        def second_norm(t, carry):
            r = rows_at(OWN * cc + t * 32, 32, 32)
            ra = rows_at(off + OWN * cc + t * 32, 32, 32)
            block = 4 * high + 2 * cc + t // 4
            branch = attp[r, :].astype(f32) + attr[r, :].astype(f32)
            middle = tok[ra, :].astype(f32) + mod_row(2, block) * branch
            normal, _ = norm_parts(middle)
            h2[r, :] = (normal * (1.0 + mod_row(4, block)) + mod_row(3, block)).astype(bf16)
            mlpg[r, :] = (mod_row(5, block) * og[r, :].astype(f32)).astype(bf16)
            return carry

        lax.fori_loop(0, OWN // 32, second_norm, 0)

        def units(k, carry):
            s, t = k // 3, k % 3
            cols = pl.ds(pl.multiple_of(t * 384, 128), 384)
            up = dot(h2[chunk, :], wt[3 * s + 1, :, cols], NN)
            grad = dot(mlpg[chunk, :], wt[3 * s + 2, cols, :], NT)
            square = up * up
            th = jnp.tanh(GELU_ONE * (up + GELU_TWO * up * square))
            half_one = 0.5 * (1.0 + th)
            act = up * half_one
            slope = half_one + 0.5 * up * (1.0 - th * th) * (GELU_ONE * (1.0 + 3.0 * GELU_TWO * square))
            big[rows_at(GROUP * s + OWN * cc, OWN), cols] = act.astype(bf16)
            big[rows_at(2 * GROUP + GROUP * s + OWN * cc, OWN), cols] = (grad * slope).astype(bf16)
            return carry

        lax.fori_loop(0, 6, units, 0)

        def inputs_back(t, carry):
            cols = pl.ds(pl.multiple_of(t * 384, 128), 384)
            part = dot(big[rows_at(2 * GROUP + OWN * cc, OWN), :], wt[1, cols, :], NT)
            part += dot(big[rows_at(3 * GROUP + OWN * cc, OWN), :], wt[4, cols, :], NT)
            seco[chunk, cols] = part.astype(bf16)
            return carry

        lax.fori_loop(0, 3, inputs_back, 0)
        send(("sec", i), seco.at[chunk], secr.at[chunk], narrow_to(1))

        def down(t, carry):
            cols = pl.ds(pl.multiple_of(t * 384, 128), 384)
            part = dot(big[rows_at(OWN * cc, OWN), :], wt[2, :, cols], NN)
            part += dot(big[rows_at(GROUP + OWN * cc, OWN), :], wt[5, :, cols], NN)
            mlpp[cc, :, cols] = part.astype(bf16)
            return carry

        lax.fori_loop(0, 3, down, 0)

    send(("mlp",), mlpp.at[1 - low], mlpr, narrow_to(1))
    sent(("ag",))

    def kept(mask):
        return rows_at(block_of(mask) * BLK, BLK)

    def axes(m):
        return (2, 4) if m in (0, 4, 2) else (4, 2)

    def rs_core(m):
        for i, mask in enumerate((0, 2, 4, 6)):
            send(("rs", m, "c", i), wt.at[m, kept(mask ^ 1)], crecv.at[m, pl.ds(i * BLK, BLK)], wide_to(1))

    def add_into(m, mask, ref, at):
        def body(t, carry):
            r = rows_at(block_of(mask) * BLK + t * 16, 16)
            wt[m, r, :] = (
                wt[m, r, :].astype(f32) + ref[m, rows_at(at + t * 16, 16), :].astype(f32)
            ).astype(bf16)
            return carry

        lax.fori_loop(0, BLK // 16, body, 0)

    def rs_one(m):
        first, second = axes(m)
        for i, mask in enumerate((0, 2, 4, 6)):
            recv(("rs", m, "c", i), crecv.at[m, pl.ds(i * BLK, BLK)])
        for mask in (first, 6, 0, second):
            add_into(m, mask, crecv, mask // 2 * BLK)
        for i, mask in enumerate((0, second)):
            send(("rs", m, "f", i), wt.at[m, kept(mask ^ first)], frecv.at[m, pl.ds(i * BLK, BLK)], wide_to(first))

    def rs_two(m):
        first, second = axes(m)
        for i, mask in enumerate((0, second)):
            recv(("rs", m, "f", i), frecv.at[m, pl.ds(i * BLK, BLK)])
            add_into(m, mask, frecv, i * BLK)
        send(("rs", m, "s"), wt.at[m, kept(second)], srecv.at[m], wide_to(second))

    def rs_three(m):
        recv(("rs", m, "s"), srecv.at[m])
        add_into(m, 0, srecv, 0)
        if m >= 3:
            send(("rs", m, "z"), wt.at[m, kept(0)], zrecv.at[m - 3], narrow_to(2))

    outs = []

    def rs_four(m):
        recv(("rs", m + 3, "z"), zrecv.at[m])

        def body(t, carry):
            r = rows_at(t * 16, 16)
            mine = wt[m, rows_at(block_of(0) * BLK + t * 16, 16), :].astype(f32)
            total = mine + zrecv[m, r, :].astype(f32)
            for i in range(3):
                facc[m, rows_at(i * BLK + t * 16, 16), :] = total[:, i * 384 : (i + 1) * 384]
            return carry

        lax.fori_loop(0, BLK // 16, body, 0)
        for i in range(3):
            outs.append(
                load(("out", m, i), facc.at[m, pl.ds(i * BLK, BLK)], gw_o.at[m, :, pl.ds(i * 384, 384)])
            )

    def down_grad(s):
        def body(t, carry):
            cols = pl.ds(pl.multiple_of(t * 128, 128), 128)
            part = dot(big[pl.ds(GROUP * s, GROUP), cols], mlpg[...], TN)
            wt[3 * s + 2, rows_at(t * 128, 128, 128), :] = part.astype(bf16)
            return carry

        lax.fori_loop(0, 9, body, 0)

    def up_grad(s):
        def body(t, carry):
            cols = pl.ds(pl.multiple_of(t * 128, 128), 128)
            part = dot(h2[:, cols], big[pl.ds(2 * GROUP + GROUP * s, GROUP), :], TN)
            wt[3 * s + 1, rows_at(t * 128, 128, 128), :] = part.astype(bf16)
            return carry

        lax.fori_loop(0, 9, body, 0)

    down_grad(1)
    rs_core(5)
    down_grad(0)
    rs_core(2)
    rs_one(5)
    up_grad(1)
    rs_core(4)
    rs_one(2)
    up_grad(0)
    rs_core(1)
    rs_one(4)

    msum[...] = jnp.zeros((2, 6, D), f32)
    for i in range(2):
        cc = order(i)
        chunk = rows_at(OWN * cc, OWN)
        recv(("sec", i), secr.at[chunk])

        def parts(t):
            r = rows_at(OWN * cc + t * 32, 32, 32)
            ra = rows_at(off + OWN * cc + t * 32, 32, 32)
            block = 4 * high + 2 * cc + t // 4
            branch = attp[r, :].astype(f32) + attr[r, :].astype(f32)
            gate = mod_row(2, block)
            normal, scale = norm_parts(tok[ra, :].astype(f32) + gate * branch)
            grad = seco[r, :].astype(f32) + secr[r, :].astype(f32)
            mid = og[r, :].astype(f32) + norm_back(normal, scale, grad * (1.0 + mod_row(4, block)))
            attg[ra, :] = (gate * mid).astype(bf16)
            return branch, normal, grad, mid

        @pl.when(cc == low)
        def _():
            def body(t, carry):
                branch, normal, grad, mid = parts(t)
                mgrad[rows_at(t * 32, 32, 32), :] = mid
                at = t // 4
                for k, v in ((2, mid * branch), (3, grad), (4, grad * normal)):
                    msum[at, k : k + 1, :] += jnp.sum(v, axis=0, keepdims=True)
                return carry

            lax.fori_loop(0, OWN // 32, body, 0)

        @pl.when(cc != low)
        def _():
            def body(t, carry):
                parts(t)
                return carry

            lax.fori_loop(0, OWN // 32, body, 0)

        if i == 0:
            r = rows_at(off + 384 * (1 - high) + 64 * low, 64)
            send(("ahalo", 0), attg.at[r], attg.at[rows_at(halo_there + 64 * low, 64)], narrow_to(2))
            rs_one(1)
            rs_two(5)
            rs_two(2)
            r = rows_at(halo_at + 64 * low, 64)
            recv(("ahalo", 0), attg.at[r])
            send(("ahalo", 1), attg.at[r], attg.at[r], narrow_to(1))

    recv(("ahalo", 1), attg.at[rows_at(halo_at + 64 * (1 - low), 64)])
    rs_two(4)

    recv(("mlp",), mlpr)

    def mix(t, carry):
        r = rows_at(OWN * low + t * 32, 32, 32)
        ra = rows_at(own_at + t * 32, 32, 32)
        rr = rows_at(t * 32, 32, 32)
        block = 4 * high + 2 * low + t // 4
        branch = attp[r, :].astype(f32) + attr[r, :].astype(f32)
        middle = tok[ra, :].astype(f32) + mod_row(2, block) * branch
        mlp = mlpp[low, rr, :].astype(f32) + mlpr[rr, :].astype(f32)
        mlpr[rr, :] = (middle + mod_row(5, block) * mlp).astype(bf16)
        msum[t // 4, 5:6, :] += jnp.sum(og[r, :].astype(f32) * mlp, axis=0, keepdims=True)
        return carry

    lax.fori_loop(0, OWN // 32, mix, 0)
    outs.append(load("mixed", mlpr, mixed_o))

    def attend_back(s, j, k0, count):
        r = rows_at(j * SEG, SEG, SEG)
        keys = slice(k0 * SEG, (k0 + count) * SEG)
        bias = key_bias(j, k0, count)
        out = [jnp.zeros((SEG, 128), f32) for _ in range(3)]
        for hd, (a, width) in enumerate(WINDOWS):
            mask = head_mask(hd, SEG)
            cols = slice(a, a + width)
            q = jnp.where(mask, qkv[s, 0, r, cols].astype(f32), 0.0).astype(bf16)
            hg = jnp.where(mask, hgrad[r, cols].astype(f32), 0.0).astype(bf16)
            scores = dot(qkv[s, 1, keys, cols], q, NT) * FACTOR
            scores = jnp.concatenate(
                [scores[i * SEG : (i + 1) * SEG, :] + bias[i] for i in range(count)], axis=0
            )
            prob = jnp.exp(scores - lse_t[s, hd : hd + 1, r])
            prob_grad = dot(qkv[s, 2, keys, cols], hg, NT)
            inner = jnp.sum(prob * prob_grad, axis=0, keepdims=True)
            score_grad = (prob * (prob_grad - inner)).astype(bf16)
            facc[1, keys, cols] += dot(score_grad, q, NN)
            facc[2, keys, cols] += dot(prob.astype(bf16), hg, NN)
            res = jnp.where(mask, dot(score_grad, qkv[s, 1, keys, cols], TN), 0.0)
            for i in range(width // 128):
                out[a // 128 + i] += res[:, i * 128 : (i + 1) * 128]
        for i in range(3):
            facc[0, r, i * 128 : (i + 1) * 128] = out[i]

    def pack(s):
        lane = lax.broadcasted_iota(jnp.int32, (64, 384), 1)

        def body(t, carry):
            ra = rows_at(off + t * 64, 64, 64)
            rg = rows_at(GROUP * s + t * 64, 64, 64)
            q = jnp.where(lane < QUARTER, facc[0, ra, :] * FACTOR, 0.0)
            k = pltpu.roll(jnp.where(lane < QUARTER, facc[1, ra, :] * FACTOR, 0.0), 32, 1)
            v = pltpu.roll(jnp.where(lane < QUARTER, facc[2, ra, :], 0.0), 64, 1)
            hd = pltpu.roll(heads[s, ra, :].astype(f32), 96, 1)
            tiles = [
                q[:, 0:128],
                q[:, 128:256],
                q[:, 256:384] + k[:, 0:128],
                k[:, 128:256],
                k[:, 256:384] + v[:, 0:128],
                v[:, 128:256],
                v[:, 256:384],
            ]
            for i, tile in enumerate(tiles):
                big[rg, i * 128 : (i + 1) * 128] = tile.astype(bf16)
            heads[s, ra, :] = hd.astype(bf16)
            return carry

        lax.fori_loop(0, GROUP // 64, body, 0)

    for s in range(2):
        hgrad[:, 0:QUARTER] = dot(attg[...], wt[3 * s, 3 * QUARTER : D, :], NT).astype(bf16)
        facc[...] = jnp.zeros((3, ATT, 384), f32)
        for_blocks(functools.partial(attend_back, s))
        pack(s)
        if s == 0:
            rs_two(1)
            rs_three(5)
            rs_three(2)

    def first_back(half, at):
        def body(t, carry):
            cols = pl.ds(pl.multiple_of(t * 384, 128), 384)
            part = dot(big[rows_at(OWN * half, OWN), 0 : 3 * QUARTER], wt[0, 0 : 3 * QUARTER, cols], NN)
            part += dot(big[rows_at(GROUP + OWN * half, OWN), 0 : 3 * QUARTER], wt[3, 0 : 3 * QUARTER, cols], NN)
            big[pl.ds(2 * GROUP + at, OWN), cols] = part.astype(bf16)
            return carry

        lax.fori_loop(0, 3, body, 0)

    first_back(1 - low, 0)
    send(("first",), big.at[pl.ds(2 * GROUP, OWN)], firstr, narrow_to(1))

    def attn_grad(s):
        def body(t, carry):
            cols = pl.ds(pl.multiple_of(t * 128, 128), 128)
            rg = rows_at(off, GROUP)
            part = dot(h1[rg, cols], big[pl.ds(GROUP * s, GROUP), 0:896], TN)
            proj = dot(attg[rg, cols], heads[s, rg, :], TN)
            r = rows_at(t * 128, 128, 128)
            wt[3 * s, r, 0:768] = part[:, 0:768].astype(bf16)
            wt[3 * s, r, 768:896] = (part[:, 768:896] + proj[:, 0:128]).astype(bf16)
            wt[3 * s, r, 896:D] = proj[:, 128:384].astype(bf16)
            return carry

        lax.fori_loop(0, 9, body, 0)

    first_back(low, OWN)
    attn_grad(1)
    rs_core(3)
    attn_grad(0)
    rs_core(0)
    rs_one(3)
    rs_one(0)
    rs_three(4)
    rs_three(1)

    recv(("first",), firstr)

    def tokens_back(t, carry):
        ra = rows_at(own_at + t * 32, 32, 32)
        rr = rows_at(t * 32, 32, 32)
        block = 4 * high + 2 * low + t // 4
        normal, scale = norm_parts(tok[ra, :].astype(f32))
        grad = big[rows_at(2 * GROUP + OWN + t * 32, 32, 32), :].astype(f32) + firstr[rr, :].astype(f32)
        res = mgrad[rr, :] + norm_back(normal, scale, grad * (1.0 + mod_row(1, block)))
        firstr[rr, :] = res.astype(bf16)
        for k, v in ((0, grad), (1, grad * normal)):
            msum[t // 4, k : k + 1, :] += jnp.sum(v, axis=0, keepdims=True)
        return carry

    lax.fori_loop(0, OWN // 32, tokens_back, 0)
    outs.append(load("tg", firstr, tg_o))

    sent(("mod",))
    row = lax.broadcasted_iota(jnp.int32, (8, D), 0)
    lane = lax.broadcasted_iota(jnp.int32, (8, ATT), 1)
    for k in range(6):
        total = jnp.zeros((8, D), f32)
        for i in range(2):
            slot = seg[SEG * (4 * high + 2 * low + i)]
            total += jnp.where((row == slot) & (row < 4), msum[i, k : k + 1, :], 0.0)
        modrecv[2 * k] = jnp.where(lane < HALF, total[:, 0:ATT], 0.0)
        modrecv[2 * k + 1] = jnp.where(lane < HALF, pltpu.roll(total[:, 512:D], HALF, 1), 0.0)
    for mask in (1, 2, 3):
        m = narrow_to(mask)[1]
        send(("mg", mask), modrecv.at[pl.ds(3 * m, 3)], mgr.at[mask - 1], narrow_to(mask))
    rs_two(3)
    rs_two(0)
    for mask in (1, 2, 3):
        recv(("mg", mask), mgr.at[mask - 1])
    total = modrecv[pl.ds(3 * n, 3)] + mgr[0] + mgr[1] + mgr[2]
    mall[b] = total.astype(bf16).astype(f32)
    if gather_wide:
        for mask in range(1, 8):
            send(("mall", mask), mall.at[b], mall.at[b], wide_to(mask))
    rs_three(3)
    rs_three(0)
    rs_four(1)
    rs_four(2)
    if gather_wide:
        for mask in range(1, 8):
            recv(("silu", mask), silu_all.at[block_of(mask)])
            recv(("mall", mask), mall.at[block_of(mask)])
        pick_row = lax.broadcasted_iota(jnp.int32, (BLK, D), 0) + b * BLK
        pick_col = lax.broadcasted_iota(jnp.int32, (BLK, D), 1)
        pick = jnp.where(pick_row == pick_col, 1.0, 0.0).astype(bf16)
        left = dot(pick, silu_all[...].reshape(64, D).astype(bf16), NT).astype(bf16)
        for i in range(3):
            right = mall[:, i].reshape(64, ATT)
            wada_o[i] = dot(left, right.astype(bf16), NN)
            bada_o[i : i + 1, :] = jnp.sum(right, axis=0, keepdims=True)
    mod_o[...] = mall[b]
    rs_four(0)
    for copy in outs:
        copy.wait()
    sent(())


def shards(N, tokens, condition, segment, w_ada, b_ada, w_qkv, w_proj, w_up, w_down, out_grad):
    step = N // 8
    gather_wide = N == 8
    anywhere = pl.BlockSpec(memory_space=pl.ANY)
    vmem = pl.BlockSpec(memory_space=pltpu.VMEM)
    smem = pl.BlockSpec(memory_space=pltpu.SMEM)
    shape = jax.ShapeDtypeStruct
    V = pltpu.VMEM
    out = pl.pallas_call(
        functools.partial(kernel, gather_wide, step),
        name="block",
        out_shape=(
            shape((OWN, D), bf16),
            shape((OWN, D), bf16),
            shape((3, BLK, D), f32),
            shape((3, 8, ATT), f32),
            shape((3, BLK, ATT), f32),
            shape((3, ATT), f32),
        ),
        in_specs=[smem, vmem, vmem] + [anywhere] * 7,
        out_specs=(anywhere, anywhere, anywhere, vmem, vmem, vmem),
        scratch_shapes=[
            V((6, D, D), bf16),
            V((6, 4 * BLK, D), bf16),
            V((6, 2 * BLK, D), bf16),
            V((6, BLK, D), bf16),
            V((3, BLK, D), bf16),
            V((ATT, D), bf16),
            V((GROUP, D), bf16),
            V((ATT, D), bf16),
            V((2, 3, ATT, 384), bf16),
            V((2, ATT, 384), bf16),
            V((2, 8, ATT), f32),
            V((GROUP, D), bf16),
            V((GROUP, D), bf16),
            V((GROUP, D), bf16),
            V((GROUP, D), bf16),
            V((4 * GROUP, D), bf16),
            V((2, OWN, D), bf16),
            V((OWN, D), bf16),
            V((GROUP, D), bf16),
            V((GROUP, D), bf16),
            V((OWN, D), f32),
            V((ATT, D), bf16),
            V((ATT, 384), bf16),
            V((3, ATT, 384), f32),
            V((OWN, D), bf16),
            V((6, 8, D), f32),
            V((12, 8, ATT), f32),
            V((8, 8, D), f32),
            V((2, 6, D), f32),
            V((3, 3, 8, ATT), f32),
            V((8, 3, 8, ATT), f32),
            V((16, D), f32),
            pltpu.SemaphoreType.DMA((SEMS,)),
            pltpu.SemaphoreType.DMA((SEMS,)),
            pltpu.SemaphoreType.DMA((24,)),
        ],
        compiler_params=pltpu.CompilerParams(
            collective_id=0, has_side_effects=True, vmem_limit_bytes=63 * 2**20
        ),
    )(
        segment,
        condition,
        b_ada.astype(f32).reshape(3, HALF),
        tokens,
        out_grad,
        w_ada.T,
        w_qkv.transpose(1, 2, 0).reshape(3 * QUARTER, D),
        w_proj.T,
        w_up,
        w_down,
    )
    mixed, tokens_grad, grads, mod, wada, bada = out
    if gather_wide:
        w_ada_grad = jnp.concatenate([wada[i, :, :HALF] for i in range(3)], axis=1)
        b_all = jnp.concatenate([bada[i, :HALF] for i in range(3)], axis=0)
    else:
        silu_low = jax.nn.silu(condition.astype(f32)).astype(bf16)
        mod_grad = jnp.concatenate([mod[i, :4, :HALF] for i in range(3)], axis=1).astype(bf16)
        silu_wide = lax.all_gather(silu_low, "wide", axis=0, tiled=True)
        mod_wide = lax.all_gather(mod_grad, "wide", axis=0, tiled=True)
        rows = D // N
        left = lax.dynamic_slice_in_dim(silu_wide, lax.axis_index("wide") * rows, rows, axis=1)
        w_ada_grad = jnp.einsum("id,ic->dc", left, mod_wide, preferred_element_type=f32)
        b_all = jnp.sum(mod_wide.astype(f32), axis=0)
        groups = [[i * step + r for r in range(step)] for i in range(8)]
        grads = lax.psum_scatter(grads, "wide", scatter_dimension=1, axis_index_groups=groups, tiled=True)
    part = b_all.shape[0] // N
    b_ada_grad = lax.dynamic_slice_in_dim(b_all, lax.axis_index("wide") * part, part)
    rows = D // N
    w_qkv_grad = grads[0, :, : 3 * QUARTER].reshape(rows, 3, QUARTER)
    return (
        mixed,
        tokens_grad,
        w_ada_grad,
        b_ada_grad,
        w_qkv_grad,
        grads[0, :, 3 * QUARTER :],
        grads[1],
        grads[2],
    )


def solution(mesh):
    placed = (
        P(("wide", "narrow"), None),
        P("wide", None),
        P("wide"),
        P(None, "narrow"),
        P("narrow"),
        P(None, None, "narrow"),
        P(None, "narrow"),
        P(None, "narrow"),
        P("narrow", None),
        P(("wide", "narrow"), None),
    )
    return jax.shard_map(
        functools.partial(shards, mesh.shape["wide"]),
        mesh=mesh,
        in_specs=placed,
        out_specs=(
            P(("wide", "narrow"), None),
            P(("wide", "narrow"), None),
            P("wide", "narrow"),
            P(("narrow", "wide")),
            P("wide", None, "narrow"),
            P("wide", "narrow"),
            P("wide", "narrow"),
            P(("narrow", "wide"), None),
        ),
        check_vma=False,
    )
```

```python
import functools
import math

import jax
import jax.numpy as jnp
from jax import lax
from jax.experimental import pallas as pl
from jax.experimental.pallas import tpu as pltpu
from jax.sharding import PartitionSpec as P

D = 1152
HEAD = 72
HEADS_LOCAL = 4
QUARTER = 288
HALF = 576
BLK = 144
SUB_A = 80
SEG = 128
OWN = 256
GROUP = 512
ATT = 640
NEG = -1e30
EPS = 1e-6
FACTOR = HEAD ** -0.5
GELU_ONE = math.sqrt(2.0 / math.pi)
GELU_TWO = 0.044715

f32, bf16 = jnp.float32, jnp.bfloat16
MESH = pl.DeviceIdType.MESH
NN = (((1,), (0,)), ((), ()))
NT = (((1,), (1,)), ((), ()))
TN = (((0,), (0,)), ((), ()))
PAIRS = ((0, (0, 1)), (128, (2, 3)))


def dot(a, b, dims):
    return lax.dot_general(a, b, dims, preferred_element_type=f32)


def rows_at(start, size, align=16):
    return pl.ds(pl.multiple_of(start, align), size)


def mean_row(v):
    return jnp.sum(v, axis=-1, keepdims=True) * (1.0 / D)


def norm_parts(v):
    centred = v - mean_row(v)
    scale = lax.rsqrt(mean_row(centred * centred) + EPS)
    return centred * scale, scale


def norm_back(normal, scale, e):
    return scale * (e - mean_row(e) - normal * mean_row(e * normal))


class Names:
    def __init__(self):
        self.ids = {}

    def __call__(self, *name):
        return self.ids.setdefault(name, len(self.ids))


SEMS = 122


def mark(name):
    pass


def kernel(
    gather_wide, step,
    seg, cond, bada, tok_h, og_h, wada_h, wqkv_h, wproj_h, wup_h, wdown_h,
    mixed_o, tg_o, gown_o, gfar_o, mall_o, silu_o,
    wt, crecv, frecv, srecv, zrecv, tok, og, h1, qkv, heads, lse_t, attp, attr, h2, mlpg, big,
    mlpp, mlpr, seco, secr, mgrad, attg, hgrad, facc, keys_t, dq_t, firstr, modblk, modrecv, silu_all, msum, mgs, mgr, mall, silu16, credit,
    ssem, rsem, lsem,
):
    w = lax.axis_index("wide")
    n = lax.axis_index("narrow")
    b = w // step
    bits = (b % 2, (b // 2) % 2, b // 4)
    low, high = n % 2, n // 2

    def narrow_to(mask):
        m = n
        if mask & 1:
            m = m + 1 - 2 * low
        if mask & 2:
            m = m + 2 - 4 * high
        return (w, m)

    def wide_to(mask):
        m = w
        for k in range(3):
            if mask & (1 << k):
                m = m + step * (1 << k) * (1 - 2 * bits[k])
        return (m, n)

    def block_of(mask):
        m = b
        for k in range(3):
            if mask & (1 << k):
                m = m + (1 << k) * (1 - 2 * bits[k])
        return m

    names = Names()

    def remote(name, src, dst, dev):
        k = names(*name)
        return pltpu.make_async_remote_copy(
            src_ref=src, dst_ref=dst, send_sem=ssem.at[k], recv_sem=rsem.at[k], device_id=dev, device_id_type=MESH
        )

    sends = {}

    def send(name, src, dst, dev):
        copy = remote(name, src, dst, dev)
        copy.start()
        sends[name] = copy

    def recv(name, landing):
        remote(name, landing, landing, narrow_to(1)).wait_recv()

    def sent(prefix):
        for name in [s for s in sends if s[: len(prefix)] == prefix]:
            sends.pop(name).wait_send()

    locals_ = Names()

    def load(name, src, dst):
        copy = pltpu.make_async_copy(src, dst, lsem.at[locals_(name)])
        copy.start()
        return copy

    off = 128 * high
    own_at = off + OWN * low
    other_at = off + OWN * (1 - low)
    halo_at = GROUP * (1 - high)
    halo_there = GROUP * high

    mark("loads")
    load_m = load("m", wada_h, big.at[pl.ds(0, 3 * HALF)])
    load_a = load("a", wqkv_h, wt.at[0, pl.ds(0, 3 * QUARTER)])
    load_b = load("b", wproj_h, wt.at[0, pl.ds(3 * QUARTER, QUARTER)])
    load_t = load("t", tok_h, tok.at[rows_at(own_at, OWN)])
    load_u = load("u", wup_h, wt.at[1])
    load_d = load("d", wdown_h, wt.at[2])
    load_g = load("g", og_h, og.at[rows_at(OWN * low, OWN)])
    barrier = pltpu.get_barrier_semaphore()
    partners = [narrow_to(m) for m in (1, 2, 3)] + [wide_to(m) for m in (range(1, 8) if gather_wide else (1, 2, 4))]
    for dev in partners:
        pl.semaphore_signal(barrier, inc=1, device_id=dev, device_id_type=MESH)

    c = cond[...].astype(f32)
    silu = (c / (1.0 + jnp.exp(-c))).astype(bf16).astype(f32)
    silu16[...] = jnp.zeros((16, D), f32)
    for i in range(3):
        silu16[4 * i : 4 * i + 4, :] = silu
    silu_low = silu16[...].astype(bf16)
    silu_all[b] = silu_low
    mark("wait_wada")
    load_m.wait()
    mark("mod_dots")
    third = lax.broadcasted_iota(jnp.int32, (16, HALF), 0) // 4
    part = jnp.zeros((16, HALF), f32)
    for i in range(3):
        value = dot(silu_low, big[HALF * i : HALF * (i + 1), :], NT) + bada[i : i + 1, :]
        part = jnp.where(third == i, value, part)
    modrecv[n, :, 0:HALF] = part
    modrecv[n, :, HALF:ATT] = jnp.zeros((16, ATT - HALF), f32)
    modblk[...] = jnp.zeros((6, 8, D), f32)
    mark("barrier")
    pl.semaphore_wait(barrier, len(partners))

    def allow(i):
        pl.semaphore_signal(credit.at[i], inc=1, device_id=narrow_to(2), device_id_type=MESH)

    def allowed(i):
        pl.semaphore_wait(credit.at[i], 1)

    def block_rows(mask, part=None):
        base = block_of(mask) * BLK
        if part is None:
            return rows_at(base, BLK)
        return rows_at(base, SUB_A) if part == 0 else rows_at(base + SUB_A, BLK - SUB_A)

    def ag_z(m):
        r = block_rows(0)
        send(("ag", m, "z"), wt.at[m, r], wt.at[3 + m, r], narrow_to(2))

    def ag_pass(m, name, mask, axis, part=None):
        r = block_rows(mask, part)
        send(("ag", m) + name, wt.at[3 + m, r], wt.at[3 + m, r], wide_to(axis))

    def ag_take(m, name, mask, part=None):
        recv(("ag", m) + name, wt.at[3 + m, block_rows(mask, part)])

    def ag_one(m):
        ag_take(m, ("z",), 0)
        ag_pass(m, ("x",), 0, 2)
        ag_pass(m, ("y",), 0, 4)
        ag_pass(m, ("c", 0), 0, 1)

    def ag_two(m):
        ag_take(m, ("x",), 2)
        ag_pass(m, ("xy",), 2, 4, 0)
        ag_take(m, ("y",), 4)
        ag_pass(m, ("yx",), 4, 2, 1)
        ag_pass(m, ("c", 2), 2, 1)
        ag_pass(m, ("c", 4), 4, 1)

    def ag_three(m):
        ag_take(m, ("xy",), 6, 0)
        ag_take(m, ("yx",), 6, 1)
        ag_pass(m, ("c", 6), 6, 1)

    def ag_end(m):
        for mask in (0, 2, 4, 6):
            ag_take(m, ("c", mask), mask ^ 1)

    mark("first_sends")
    for mask in (1, 2, 3):
        send(("mod", mask), modrecv.at[n], modrecv.at[n], narrow_to(mask))
    send(("tok",), tok_h, tok.at[rows_at(own_at, OWN)], narrow_to(1))
    halo_first = remote(
        ("halo", 0), tok_h.at[rows_at(128 * (1 - high), SEG)], tok.at[rows_at(halo_there, SEG)], narrow_to(2)
    )
    halo_second = remote(
        ("halo", 1), tok.at[rows_at(halo_at, SEG)], tok.at[rows_at(halo_at, SEG)], narrow_to(1)
    )
    halo_source = low != high

    @pl.when(halo_source)
    def _():
        halo_first.start()

    load_a.wait()
    load_b.wait()
    ag_z(0)
    mark("wait_mod")
    for mask in (1, 2, 3):
        m = narrow_to(mask)[1]
        recv(("mod", mask), modrecv.at[m])
    for k in range(6):
        halves = [modrecv[i // 3, i % 3 * 4 : i % 3 * 4 + 4, :] for i in (2 * k, 2 * k + 1)]
        first, second = halves[0], pltpu.roll(halves[1], 64, 1)
        modblk[k, 0:4, 0:512] = first[:, 0:512]
        modblk[k, 0:4, 512:640] = first[:, 512:640] + second[:, 0:128]
        modblk[k, 0:4, 640:D] = second[:, 128:640]

    def mod_row(k, shard_block):
        return modblk[k, pl.ds(seg[shard_block * SEG], 1), :]

    def first_norm(base, size):
        def body(t, carry):
            r = rows_at(base + t * 32, 32, 32)
            block = 3 * high + (base + t * 32) // SEG
            normal, _ = norm_parts(tok[r, :].astype(f32))
            h1[r, :] = (normal * (1.0 + mod_row(1, block)) + mod_row(0, block)).astype(bf16)
            return carry

        lax.fori_loop(0, size // 32, body, 0)

    mark("norm_own")
    load_t.wait()
    first_norm(own_at, OWN)
    mark("wait_halo")

    @pl.when(jnp.logical_not(halo_source))
    def _():
        halo_first.wait_recv()
        halo_second.start()

    mark("wait_tok")
    recv(("tok",), tok.at[rows_at(other_at, OWN)])
    allow(0)
    mark("norm_other")
    first_norm(other_at, OWN)
    mark("wait_ag_one_0")
    ag_one(0)
    mark("wait_halo_two")

    @pl.when(halo_source)
    def _():
        halo_second.wait_recv()
        halo_first.wait_send()

    mark("norm_halo")
    first_norm(halo_at, SEG)

    @pl.when(jnp.logical_not(halo_source))
    def _():
        halo_second.wait_send()

    def project(s):
        def body(i, carry):
            qkv[s, i] = dot(h1[...], wt[3 * s, rows_at(QUARTER * i, 384), :], NT).astype(bf16)
            return carry

        lax.fori_loop(0, 3, body, 0)

    def key_bias(j, k0, count):
        mine = seg[SEG * (j + 3 * high)]
        return [jnp.where(seg[SEG * (k0 + i + 3 * high)] == mine, 0.0, NEG) for i in range(count)]

    lane_pair = lax.broadcasted_iota(jnp.int32, (SEG, 256), 1)
    pair_masks = [
        [(lane_pair >= HEAD * hd - a) & (lane_pair < HEAD * (hd + 1) - a) for hd in hds] for a, hds in PAIRS
    ]

    def stacked(value, masks):
        value = value.astype(f32)
        return jnp.concatenate([jnp.where(m, value, 0.0).astype(bf16) for m in masks], axis=0)

    def attend(s, j, k0, count):
        r = rows_at(j * SEG, SEG, SEG)
        keys = slice(k0 * SEG, (k0 + count) * SEG)
        bias = key_bias(j, k0, count)
        out = [jnp.zeros((SEG, 128), f32) for _ in range(3)]
        lse = jnp.zeros((SEG, 128), f32)
        lane = lax.broadcasted_iota(jnp.int32, (SEG, 128), 1)
        for (a, hds), masks in zip(PAIRS, pair_masks):
            cols = slice(a, a + 256)
            scores = dot(stacked(qkv[s, 0, r, cols], masks), qkv[s, 1, keys, cols], NT) * FACTOR
            scores = jnp.concatenate(
                [scores[:, i * SEG : (i + 1) * SEG] + bias[i] for i in range(count)], axis=1
            )
            top = jnp.max(scores, axis=1, keepdims=True)
            weights = jnp.exp(scores - top)
            total = jnp.sum(weights, axis=1, keepdims=True)
            prob = (weights * (1.0 / total)).astype(bf16)
            res = dot(prob, qkv[s, 2, keys, cols], NN)
            log_total = top + jnp.log(total)
            for i, hd in enumerate(hds):
                part = jnp.where(masks[i], res[i * SEG : (i + 1) * SEG, :], 0.0)
                out[a // 128] += part[:, 0:128]
                out[a // 128 + 1] += part[:, 128:256]
                lse = jnp.where(lane == hd, log_total[i * SEG : (i + 1) * SEG, :], lse)
        for i in range(3):
            heads[s, r, i * 128 : (i + 1) * 128] = out[i].astype(bf16)
        lse_t[s, :, r] = lse.T[0:8, :]

    def for_blocks(fn, between=()):
        fn(0, 0, 2)
        for hook in between[0:1]:
            hook()
        fn(1, 0, 5)
        for hook in between[1:2]:
            hook()

        def body(j, carry):
            fn(j, 1, 4)
            return carry

        lax.fori_loop(2, 5, body, 0)

    mark("project_own")
    project(0)
    load_u.wait()
    load_d.wait()
    allowed(0)
    ag_z(1)
    ag_z(2)
    mark("wait_ag_two_0")
    ag_two(0)
    mark("attend_own")
    for_blocks(functools.partial(attend, 0), (lambda: None, lambda: ag_three(0)))
    load_g.wait()
    send(("og",), og_h, og.at[rows_at(OWN * low, OWN)], narrow_to(1))
    mark("wait_ag_end_0")
    ag_end(0)
    ag_one(1)
    mark("project_opp")
    project(1)
    mark("wait_ag_one_2")
    ag_one(2)
    mark("attend_opp")
    for_blocks(functools.partial(attend, 1), (lambda: None, lambda: ag_two(1)))
    mark("proj")
    def order(i):
        return 1 - high if i == 0 else high

    if gather_wide:
        for mask in range(1, 8):
            send(("silu", mask), silu_all.at[b], silu_all.at[b], wide_to(mask))
    for i in range(2):
        cc = order(i)
        src = rows_at(off + OWN * cc, OWN)
        dst = rows_at(OWN * cc, OWN)

        def body(t, carry):
            cols = pl.ds(pl.multiple_of(t * 384, 128), 384)
            part = dot(heads[0, src, 0:QUARTER], wt[0, 3 * QUARTER : D, cols], NN)
            part += dot(heads[1, src, 0:QUARTER], wt[3, 3 * QUARTER : D, cols], NN)
            attp[dst, cols] = part.astype(bf16)
            return carry

        lax.fori_loop(0, 3, body, 0)
        if i == 0:
            send(("att", i), attp.at[dst], attr.at[dst], narrow_to(1))

    mark("wait_ag_two_2")
    ag_two(2)
    ag_three(1)
    mark("wait_ag_three_2")
    ag_three(2)
    mark("wait_og")
    recv(("og",), og.at[rows_at(OWN * (1 - low), OWN)])

    mark("ffn")
    for i in range(2):
        cc = order(i)
        chunk = rows_at(OWN * cc, OWN)
        mark("wait_att")
        recv(("att", i), attr.at[chunk])
        if i == 0:
            dst = rows_at(OWN * order(1), OWN)
            send(("att", 1), attp.at[dst], attr.at[dst], narrow_to(1))

        mark("second_norm")
        def second_norm(t, carry):
            r = rows_at(OWN * cc + t * 32, 32, 32)
            ra = rows_at(off + OWN * cc + t * 32, 32, 32)
            block = 4 * high + 2 * cc + t // 4
            branch = attp[r, :].astype(f32) + attr[r, :].astype(f32)
            middle = tok[ra, :].astype(f32) + mod_row(2, block) * branch
            normal, _ = norm_parts(middle)
            h2[r, :] = (normal * (1.0 + mod_row(4, block)) + mod_row(3, block)).astype(bf16)
            mlpg[r, :] = (mod_row(5, block) * og[r, :].astype(f32)).astype(bf16)
            return carry

        lax.fori_loop(0, OWN // 32, second_norm, 0)
        if i == 0:
            mark("wait_ag_end")
            ag_end(1)
            ag_end(2)

        mark("units")
        def units(k, carry):
            s, t = k // 3, k % 3
            cols = pl.ds(pl.multiple_of(t * 384, 128), 384)
            up = dot(h2[chunk, :], wt[3 * s + 1, :, cols], NN)
            grad = dot(mlpg[chunk, :], wt[3 * s + 2, cols, :], NT)
            square = up * up
            th = jnp.tanh(GELU_ONE * (up + GELU_TWO * up * square))
            half_one = 0.5 * (1.0 + th)
            act = up * half_one
            slope = half_one + 0.5 * up * (1.0 - th * th) * (GELU_ONE * (1.0 + 3.0 * GELU_TWO * square))
            big[rows_at(GROUP * s + OWN * cc, OWN), cols] = act.astype(bf16)
            big[rows_at(2 * GROUP + GROUP * s + OWN * cc, OWN), cols] = (grad * slope).astype(bf16)
            return carry

        lax.fori_loop(0, 6, units, 0)

        mark("inputs_back")
        def inputs_back(t, carry):
            cols = pl.ds(pl.multiple_of(t * 384, 128), 384)
            part = dot(big[rows_at(2 * GROUP + OWN * cc, OWN), :], wt[1, cols, :], NT)
            part += dot(big[rows_at(3 * GROUP + OWN * cc, OWN), :], wt[4, cols, :], NT)
            seco[chunk, cols] = part.astype(bf16)
            return carry

        lax.fori_loop(0, 3, inputs_back, 0)
        send(("sec", i), seco.at[chunk], secr.at[chunk], narrow_to(1))

    mark("drain_ag")
    sent(("ag",))

    def kept(mask):
        return rows_at(block_of(mask) * BLK, BLK)

    def pieces(m):
        return ((pl.ds(0, 640), 2, 4), (pl.ds(640, 512), 4, 2))

    def rs_core(m):
        for i, mask in enumerate((0, 2, 4, 6)):
            send(("rs", m, "c", i), wt.at[m, kept(mask ^ 1)], crecv.at[m, pl.ds(i * BLK, BLK)], wide_to(1))

    def add_into(m, mask, ref, at, cols):
        def body(t, carry):
            r = rows_at(block_of(mask) * BLK + t * 16, 16)
            wt[m, r, cols] = (
                wt[m, r, cols].astype(f32) + ref[m, rows_at(at + t * 16, 16), cols].astype(f32)
            ).astype(bf16)
            return carry

        lax.fori_loop(0, BLK // 16, body, 0)

    def rs_one(m):
        for i, mask in enumerate((0, 2, 4, 6)):
            recv(("rs", m, "c", i), crecv.at[m, pl.ds(i * BLK, BLK)])
        for p, (cols, first, second) in enumerate(pieces(m)):
            for mask in (first, 6):
                add_into(m, mask, crecv, mask // 2 * BLK, cols)
            for i, mask in enumerate((0, second)):
                send(
                    ("rs", m, "f", p, i), wt.at[m, kept(mask ^ first), cols], frecv.at[m, pl.ds(i * BLK, BLK), cols],
                    wide_to(first),
                )
        for p, (cols, first, second) in enumerate(pieces(m)):
            for mask in (0, second):
                add_into(m, mask, crecv, mask // 2 * BLK, cols)

    def rs_two(m):
        for p, (cols, first, second) in enumerate(pieces(m)):
            recv(("rs", m, "f", p, 1), frecv.at[m, pl.ds(BLK, BLK), cols])
            add_into(m, second, frecv, BLK, cols)
            send(("rs", m, "s", p), wt.at[m, kept(second), cols], srecv.at[m, :, cols], wide_to(second))
        for p, (cols, first, second) in enumerate(pieces(m)):
            recv(("rs", m, "f", p, 0), frecv.at[m, pl.ds(0, BLK), cols])
            add_into(m, 0, frecv, 0, cols)

    outs = []

    def rs_three(m):
        for p, (cols, _, _) in enumerate(pieces(m)):
            recv(("rs", m, "s", p), srecv.at[m, :, cols])
            add_into(m, 0, srecv, 0, cols)
        if m >= 3:
            send(("rs", m, "z"), wt.at[m, kept(0)], zrecv.at[m - 3], narrow_to(2))
        else:
            outs.append(load(("own", m), wt.at[m, kept(0)], gown_o.at[m]))

    def rs_four(m):
        recv(("rs", m + 3, "z"), zrecv.at[m])
        outs.append(load(("far", m), zrecv.at[m], gfar_o.at[m]))

    def down(t, carry):
        cols = pl.ds(pl.multiple_of(t * 384, 128), 384)
        part = dot(big[0:GROUP, :], wt[2, :, cols], NN)
        part += dot(big[GROUP : 2 * GROUP, :], wt[5, :, cols], NN)
        mlpp[:, :, cols] = part.astype(bf16).reshape(2, OWN, 384)
        return carry

    def down_grad(s):
        def body(t, carry):
            cols = pl.ds(pl.multiple_of(t * 128, 128), 128)
            part = dot(big[pl.ds(GROUP * s, GROUP), cols], mlpg[...], TN)
            wt[3 * s + 2, rows_at(t * 128, 128, 128), :] = part.astype(bf16)
            return carry

        lax.fori_loop(0, 9, body, 0)

    def up_grad(s):
        def body(t, carry):
            cols = pl.ds(pl.multiple_of(t * 128, 128), 128)
            part = dot(h2[:, cols], big[pl.ds(2 * GROUP + GROUP * s, GROUP), :], TN)
            wt[3 * s + 1, rows_at(t * 128, 128, 128), :] = part.astype(bf16)
            return carry

        lax.fori_loop(0, 9, body, 0)

    mark("up_grad_1")
    up_grad(1)
    rs_core(4)
    msum[...] = jnp.zeros((2, 6, D), f32)
    for i in range(2):
        cc = order(i)
        chunk = rows_at(OWN * cc, OWN)
        mark("wait_sec")
        recv(("sec", i), secr.at[chunk])
        mark("second_norm_back")

        def parts(t):
            r = rows_at(OWN * cc + t * 32, 32, 32)
            ra = rows_at(off + OWN * cc + t * 32, 32, 32)
            block = 4 * high + 2 * cc + t // 4
            branch = attp[r, :].astype(f32) + attr[r, :].astype(f32)
            gate = mod_row(2, block)
            normal, scale = norm_parts(tok[ra, :].astype(f32) + gate * branch)
            grad = seco[r, :].astype(f32) + secr[r, :].astype(f32)
            mid = og[r, :].astype(f32) + norm_back(normal, scale, grad * (1.0 + mod_row(4, block)))
            attg[ra, :] = (gate * mid).astype(bf16)
            return branch, normal, grad, mid

        @pl.when(cc == low)
        def _():
            def body(t, carry):
                branch, normal, grad, mid = parts(t)
                mgrad[rows_at(t * 32, 32, 32), :] = mid
                at = t // 4
                for k, v in ((2, mid * branch), (3, grad), (4, grad * normal)):
                    msum[at, k : k + 1, :] += jnp.sum(v, axis=0, keepdims=True)
                return carry

            lax.fori_loop(0, OWN // 32, body, 0)

        @pl.when(cc != low)
        def _():
            def body(t, carry):
                parts(t)
                return carry

            lax.fori_loop(0, OWN // 32, body, 0)

        if i == 0:
            r = rows_at(off + 384 * (1 - high) + 64 * low, 64)
            send(("ahalo", 0), attg.at[r], attg.at[rows_at(halo_there + 64 * low, 64)], narrow_to(2))
            mark("rs_one_4")
            rs_one(4)
            mark("down")
            lax.fori_loop(0, 3, down, 0)
            mark("down_grad_1")
            down_grad(1)
            rs_core(5)
            mark("wait_halo_back")
            r = rows_at(halo_at + 64 * low, 64)
            recv(("ahalo", 0), attg.at[r])
            send(("ahalo", 1), attg.at[r], attg.at[r], narrow_to(1))

    mark("wait_halo_back_two")
    recv(("ahalo", 1), attg.at[rows_at(halo_at + 64 * (1 - low), 64)])
    send(("mlp",), mlpp.at[1 - low], mlpr, narrow_to(1))

    def mix(t, carry):
        r = rows_at(OWN * low + t * 32, 32, 32)
        ra = rows_at(own_at + t * 32, 32, 32)
        rr = rows_at(t * 32, 32, 32)
        block = 4 * high + 2 * low + t // 4
        branch = attp[r, :].astype(f32) + attr[r, :].astype(f32)
        middle = tok[ra, :].astype(f32) + mod_row(2, block) * branch
        mlp = mlpp[low, rr, :].astype(f32) + mlpr[rr, :].astype(f32)
        mlpr[rr, :] = (middle + mod_row(5, block) * mlp).astype(bf16)
        msum[t // 4, 5:6, :] += jnp.sum(og[r, :].astype(f32) * mlp, axis=0, keepdims=True)
        return carry

    def attend_back(s, j, k0, count):
        r = rows_at(j * SEG, SEG, SEG)
        keys = slice(k0 * SEG, (k0 + count) * SEG)
        bias = key_bias(j, k0, count)
        row = lax.broadcasted_iota(jnp.int32, (256, SEG), 0)
        for (a, hds), masks in zip(PAIRS, pair_masks):
            cols = slice(a, a + 256)
            q = stacked(qkv[s, 0, r, cols], masks)
            hg = stacked(hgrad[r, cols], masks)
            top = jnp.concatenate([lse_t[s, hd : hd + 1, r] for hd in hds], axis=1)
            scores = dot(qkv[s, 1, keys, cols], q, NT) * FACTOR
            prob = jnp.exp(
                jnp.concatenate(
                    [scores[i * SEG : (i + 1) * SEG, :] - (top - bias[i]) for i in range(count)], axis=0
                )
            )
            prob_grad = dot(qkv[s, 2, keys, cols], hg, NT)
            inner = jnp.sum(prob * prob_grad, axis=0, keepdims=True)
            score_grad = (prob * (prob_grad - inner)).astype(bf16)
            facc[0, keys, cols] += dot(score_grad, q, NN)
            facc[1, keys, cols] += dot(prob.astype(bf16), hg, NN)
            res = dot(keys_t[a : a + 256, keys], score_grad, NN)
            total = jnp.zeros((256, SEG), f32)
            for i, hd in enumerate(hds):
                mine = (row >= HEAD * hd - a) & (row < HEAD * (hd + 1) - a)
                total += jnp.where(mine, res[:, i * SEG : (i + 1) * SEG], 0.0)
            dq_t[a : a + 256, r] += total

    def pack(s):
        lane = lax.broadcasted_iota(jnp.int32, (128, 384), 1)

        def body(t, carry):
            ra = rows_at(off + t * 128, 128, 128)
            rg = rows_at(GROUP * s + t * 128, 128, 128)
            q = jnp.where(lane < QUARTER, dq_t[:, ra].T * FACTOR, 0.0)
            k = pltpu.roll(jnp.where(lane < QUARTER, facc[0, ra, :] * FACTOR, 0.0), 32, 1)
            v = pltpu.roll(jnp.where(lane < QUARTER, facc[1, ra, :], 0.0), 64, 1)
            hd = pltpu.roll(heads[s, ra, :].astype(f32), 96, 1)
            tiles = [
                q[:, 0:128],
                q[:, 128:256],
                q[:, 256:384] + k[:, 0:128],
                k[:, 128:256],
                k[:, 256:384] + v[:, 0:128],
                v[:, 128:256],
                v[:, 256:384],
            ]
            for i, tile in enumerate(tiles):
                big[rg, i * 128 : (i + 1) * 128] = tile.astype(bf16)
            heads[s, ra, :] = hd.astype(bf16)
            return carry

        lax.fori_loop(0, GROUP // 128, body, 0)

    def first_far(t, carry):
        half, cols = t // 3, pl.ds(pl.multiple_of(t % 3 * 384, 128), 384)
        part = dot(big[rows_at(GROUP + OWN * half, OWN), 0 : 3 * QUARTER], wt[3, 0 : 3 * QUARTER, cols], NN)
        high_part = part.astype(bf16)
        secr[rows_at(OWN * half, OWN), cols] = high_part
        mlpg[rows_at(OWN * half, OWN), cols] = (part - high_part.astype(f32)).astype(bf16)
        return carry

    def first_back(half, at):
        def body(t, carry):
            cols = pl.ds(pl.multiple_of(t * 384, 128), 384)
            part = dot(big[rows_at(OWN * half, OWN), 0 : 3 * QUARTER], wt[0, 0 : 3 * QUARTER, cols], NN)
            part += secr[rows_at(OWN * half, OWN), cols].astype(f32)
            part += mlpg[rows_at(OWN * half, OWN), cols].astype(f32)
            seco[pl.ds(at, OWN), cols] = part.astype(bf16)
            return carry

        lax.fori_loop(0, 3, body, 0)

    def attn_grad(s):
        def body(t, carry):
            cols = pl.ds(pl.multiple_of(t * 128, 128), 128)
            rg = rows_at(off, GROUP)
            part = dot(h1[rg, cols], big[pl.ds(GROUP * s, GROUP), 0:896], TN)
            proj = dot(attg[rg, cols], heads[s, rg, :], TN)
            r = rows_at(t * 128, 128, 128)
            wt[3 * s, r, 0:768] = part[:, 0:768].astype(bf16)
            wt[3 * s, r, 768:896] = (part[:, 768:896] + proj[:, 0:128]).astype(bf16)
            wt[3 * s, r, 896:D] = proj[:, 128:384].astype(bf16)
            return carry

        lax.fori_loop(0, 9, body, 0)

    def heads_back(s, between):
        mark("heads_grad")
        hgrad[:, 0:QUARTER] = dot(attg[...], wt[3 * s, 3 * QUARTER : D, :], NT).astype(bf16)
        facc[...] = jnp.zeros((2, ATT, 384), f32)
        dq_t[...] = jnp.zeros((384, ATT), f32)
        for i in range(5):
            keys_t[:, i * 128 : (i + 1) * 128] = qkv[s, 1, i * 128 : (i + 1) * 128, :].T
        mark("attend_back")
        for_blocks(functools.partial(attend_back, s), between)
        mark("pack")
        pack(s)

    mark("rs_one_5")
    rs_one(5)
    mark("down_grad_0")
    down_grad(0)
    rs_core(2)
    heads_back(1, (lambda: rs_two(4), lambda: rs_one(2)))
    mark("first_far")
    lax.fori_loop(0, 6, first_far, 0)
    mark("attn_grad_1")
    attn_grad(1)
    rs_core(3)
    mark("rs_three_4")
    rs_three(4)
    rs_two(5)
    mark("up_grad_0")
    up_grad(0)
    rs_core(1)
    mark("rs_one_3")
    rs_one(3)
    rs_two(2)
    heads_back(0, (lambda: rs_three(5), lambda: rs_one(1)))
    sent(("sec",))
    mark("first_back")
    first_back(1 - low, 0)
    send(("first",), seco.at[pl.ds(0, OWN)], firstr, narrow_to(1))
    mark("first_back_own")
    first_back(low, OWN)
    mark("rs_two_3")
    rs_two(3)
    mark("attn_grad_0")
    attn_grad(0)
    rs_core(0)
    mark("rs_three_21")
    rs_three(2)
    rs_two(1)
    mark("rs_one_0")
    rs_one(0)
    mark("wait_mlp")
    recv(("mlp",), mlpr)
    mark("mix")
    lax.fori_loop(0, OWN // 32, mix, 0)
    outs.append(load("mixed", mlpr, mixed_o))

    mark("wait_first")
    recv(("first",), firstr)
    allow(1)

    mark("tokens_back")
    def tokens_back(t, carry):
        ra = rows_at(own_at + t * 32, 32, 32)
        rr = rows_at(t * 32, 32, 32)
        block = 4 * high + 2 * low + t // 4
        normal, scale = norm_parts(tok[ra, :].astype(f32))
        grad = seco[rows_at(OWN + t * 32, 32, 32), :].astype(f32) + firstr[rr, :].astype(f32)
        res = mgrad[rr, :] + norm_back(normal, scale, grad * (1.0 + mod_row(1, block)))
        firstr[rr, :] = res.astype(bf16)
        for k, v in ((0, grad), (1, grad * normal)):
            msum[t // 4, k : k + 1, :] += jnp.sum(v, axis=0, keepdims=True)
        return carry

    lax.fori_loop(0, OWN // 32, tokens_back, 0)
    outs.append(load("tg", firstr, tg_o))

    mark("modgrad")
    sent(("mod",))
    row = lax.broadcasted_iota(jnp.int32, (8, D), 0)
    lane = lax.broadcasted_iota(jnp.int32, (8, ATT), 1)
    for k in range(6):
        total = jnp.zeros((8, D), f32)
        for i in range(2):
            slot = seg[SEG * (4 * high + 2 * low + i)]
            total += jnp.where((row == slot) & (row < 4), msum[i, k : k + 1, :], 0.0)
        for i, value in ((2 * k, total[:, 0:ATT]), (2 * k + 1, pltpu.roll(total[:, 512:D], HALF, 1))):
            modrecv[i // 3, i % 3 * 4 : i % 3 * 4 + 4, :] = jnp.where(lane < HALF, value, 0.0)[0:4, :]
    for i in range(4):
        modrecv[i, 12:16, :] = jnp.zeros((4, ATT), f32)
        mgs[i] = modrecv[i].astype(bf16)
    for mask in (1, 2, 3):
        m = narrow_to(mask)[1]
        send(("mg", mask), mgs.at[m], mgr.at[mask - 1], narrow_to(mask))
    mark("rs_three_3")
    allowed(1)
    rs_three(3)
    rs_three(1)
    mark("rs_two_0")
    rs_two(0)
    rs_four(2)
    rs_four(1)
    mark("wait_mg")
    for mask in (1, 2, 3):
        recv(("mg", mask), mgr.at[mask - 1])
    total = modrecv[n] + mgr[0].astype(f32) + mgr[1].astype(f32) + mgr[2].astype(f32)
    mall[b] = total.astype(bf16)
    if gather_wide:
        for mask in range(1, 8):
            send(("mall", mask), mall.at[b], mall.at[b], wide_to(mask))
    mark("rs_three_0")
    rs_three(0)
    mark("rs_four_0")
    rs_four(0)
    mark("wait_mall")
    if gather_wide:
        for mask in range(1, 8):
            recv(("silu", mask), silu_all.at[block_of(mask)])
            recv(("mall", mask), mall.at[block_of(mask)])
    outs.append(load("mall", mall, mall_o))
    outs.append(load("silu", silu_all, silu_o))
    mark("drain")
    for copy in outs:
        copy.wait()
    sent(())
    mark(None)


def finish(
    step, mixed_h, tg_h, gown_h, gfar_h, mall_h, silu_h,
    mixed_o, tg_o, wada_o, bada_o, gqkv_o, gproj_o, gup_o, gdown_o,
    gown, gfar, mall, silu, mixed, tg, wada, sums, bada, gqkv, gproj, gffn, sem,
):
    ids = Names()

    def move(src, dst):
        copy = pltpu.make_async_copy(src, dst, sem.at[ids(len(ids.ids))])
        copy.start()
        return copy

    ins = [move(mall_h, mall), move(silu_h, silu), move(gown_h, gown), move(gfar_h, gfar)]
    outs = []
    rows = [move(mixed_h, mixed), move(tg_h, tg)]
    rows[0].wait()
    outs.append(move(mixed, mixed_o))
    rows[1].wait()
    outs.append(move(tg, tg_o))
    b = lax.axis_index("wide") // step
    ins[0].wait()
    ins[1].wait()
    pick_row = lax.broadcasted_iota(jnp.int32, (BLK, D), 0) + b * BLK
    pick_col = lax.broadcasted_iota(jnp.int32, (BLK, D), 1)
    pick = jnp.where(pick_row == pick_col, 1.0, 0.0).astype(bf16)
    left = dot(pick, silu[...].reshape(128, D), NT).astype(bf16)
    third = lax.broadcasted_iota(jnp.int32, (BLK, 128), 1) % 16 // 4
    right = mall[...].reshape(128, ATT)
    for i in range(3):
        part = dot(jnp.where(third == i, left, 0), right, NN)
        total = dot(jnp.where(third[0:8] == i, 1.0, 0.0).astype(bf16), right, NN)
        if i == 1:
            part, total = pltpu.roll(part, 64, 1), pltpu.roll(total, 64, 1)
            wada[:, 512:640] += part[:, 0:128]
            wada[:, 640:D] = part[:, 128:640]
            sums[:, 512:640] += total[:, 0:128]
            sums[:, 640:D] = total[:, 128:640]
        else:
            at = i * HALF
            wada[:, at : at + HALF] = part[:, 0:HALF]
            sums[:, at : at + ATT] = total
            if i == 0:
                wada[:, HALF:640] = jnp.zeros((BLK, 64), f32)
    place = lax.axis_index("wide")
    bada[...] = pltpu.roll(sums[...], 14 * 128 - place * QUARTER // 4 * 3, 1)[:, 0:256]
    outs.append(move(wada, wada_o))
    outs.append(move(bada, bada_o))
    ins[2].wait()
    ins[3].wait()
    for m in range(3):
        total = gown[m].astype(f32) + gfar[m].astype(f32)
        if m == 0:
            gqkv[0] = total[:, 0:QUARTER]
            gqkv[1] = pltpu.roll(total[:, 256:640], 352, 1)[:, 0:QUARTER]
            gqkv[2] = pltpu.roll(total[:, 512:896], 320, 1)[:, 0:QUARTER]
            gproj[...] = pltpu.roll(total[:, 768:D], 288, 1)[:, 0:QUARTER]
            outs.append(move(gqkv, gqkv_o))
            outs.append(move(gproj, gproj_o))
        else:
            gffn[m - 1] = total
            outs.append(move(gffn.at[m - 1], (gup_o, gdown_o)[m - 1]))
    for copy in outs:
        copy.wait()


def shards(N, tokens, condition, segment, w_ada, b_ada, w_qkv, w_proj, w_up, w_down, out_grad):
    step = N // 8
    gather_wide = N == 8
    anywhere = pl.BlockSpec(memory_space=pl.ANY)
    hbm = pl.BlockSpec(memory_space=pltpu.HBM)
    vmem = pl.BlockSpec(memory_space=pltpu.VMEM)
    smem = pl.BlockSpec(memory_space=pltpu.SMEM)
    shape = jax.ShapeDtypeStruct
    V = pltpu.VMEM
    out = pl.pallas_call(
        functools.partial(kernel, gather_wide, step),
        name="block",
        out_shape=(
            shape((OWN, D), bf16),
            shape((OWN, D), bf16),
            shape((3, BLK, D), bf16),
            shape((3, BLK, D), bf16),
            shape((8, 16, ATT), bf16),
            shape((8, 16, D), bf16),
        ),
        in_specs=[smem, vmem, vmem] + [anywhere] * 7,
        out_specs=(anywhere,) * 6,
        scratch_shapes=[
            V((6, D, D), bf16),
            V((6, 4 * BLK, D), bf16),
            V((6, 2 * BLK, D), bf16),
            V((6, BLK, D), bf16),
            V((3, BLK, D), bf16),
            V((ATT, D), bf16),
            V((GROUP, D), bf16),
            V((ATT, D), bf16),
            V((2, 3, ATT, 384), bf16),
            V((2, ATT, 384), bf16),
            V((2, 8, ATT), f32),
            V((GROUP, D), bf16),
            V((GROUP, D), bf16),
            V((GROUP, D), bf16),
            V((GROUP, D), bf16),
            V((4 * GROUP, D), bf16),
            V((2, OWN, D), bf16),
            V((OWN, D), bf16),
            V((GROUP, D), bf16),
            V((GROUP, D), bf16),
            V((OWN, D), f32),
            V((ATT, D), bf16),
            V((ATT, 384), bf16),
            V((2, ATT, 384), f32),
            V((384, ATT), bf16),
            V((384, ATT), f32),
            V((OWN, D), bf16),
            V((6, 8, D), f32),
            V((4, 16, ATT), f32),
            V((8, 16, D), bf16),
            V((2, 6, D), f32),
            V((4, 16, ATT), bf16),
            V((3, 16, ATT), bf16),
            V((8, 16, ATT), bf16),
            V((16, D), f32),
            pltpu.SemaphoreType.REGULAR((2,)),
            pltpu.SemaphoreType.DMA((SEMS,)),
            pltpu.SemaphoreType.DMA((SEMS,)),
            pltpu.SemaphoreType.DMA((17,)),
        ],
        compiler_params=pltpu.CompilerParams(
            collective_id=0, has_side_effects=True, vmem_limit_bytes=63 * 2**20
        ),
    )(
        segment,
        condition,
        b_ada.astype(f32).reshape(3, HALF),
        tokens,
        out_grad,
        w_ada.T,
        w_qkv.transpose(1, 2, 0).reshape(3 * QUARTER, D),
        w_proj.T,
        w_up,
        w_down,
    )
    mixed, tokens_grad, gown, gfar, mall, silu = out
    mixed, tokens_grad, wada, bada, gqkv, gproj, gup, gdown = pl.pallas_call(
        functools.partial(finish, step),
        name="finish",
        out_shape=(
            shape((OWN, D), bf16),
            shape((OWN, D), bf16),
            shape((BLK, 3 * HALF), f32),
            shape((8, 256), f32),
            shape((3, BLK, QUARTER), f32),
            shape((BLK, QUARTER), f32),
            shape((BLK, D), f32),
            shape((BLK, D), f32),
        ),
        in_specs=[hbm] * 6,
        out_specs=(hbm,) * 8,
        scratch_shapes=[
            V((3, BLK, D), bf16),
            V((3, BLK, D), bf16),
            V((8, 16, ATT), bf16),
            V((8, 16, D), bf16),
            V((OWN, D), bf16),
            V((OWN, D), bf16),
            V((BLK, 3 * HALF), f32),
            V((8, 14 * 128), f32),
            V((8, 256), f32),
            V((3, BLK, QUARTER), f32),
            V((BLK, QUARTER), f32),
            V((2, BLK, D), f32),
            pltpu.SemaphoreType.DMA((16,)),
        ],
        compiler_params=pltpu.CompilerParams(vmem_limit_bytes=63 * 2**20),
    )(mixed, tokens_grad, gown, gfar, mall, silu)
    gqkv = gqkv.transpose(1, 0, 2)
    place = lax.axis_index("wide")
    if gather_wide:
        w_ada_grad, b_ada_grad = wada, bada[0, : 3 * HALF // N]
    else:
        silu_low = jax.nn.silu(condition.astype(f32)).astype(bf16)
        mine = lax.dynamic_index_in_dim(mall, place // step, keepdims=False)
        mod_grad = jnp.concatenate([mine[4 * i : 4 * i + 4, :HALF] for i in range(3)], axis=1)
        silu_wide = lax.all_gather(silu_low, "wide", axis=0, tiled=True)
        mod_wide = lax.all_gather(mod_grad, "wide", axis=0, tiled=True)
        left = lax.dynamic_slice_in_dim(silu_wide, place * (D // N), D // N, axis=1)
        w_ada_grad = jnp.einsum("id,ic->dc", left, mod_wide, preferred_element_type=f32)
        b_all = jnp.sum(mod_wide.astype(f32), axis=0)
        groups = [[i * step + r for r in range(step)] for i in range(8)]
        gqkv, gproj, gup, gdown = (
            lax.psum_scatter(g, "wide", scatter_dimension=0, axis_index_groups=groups, tiled=True)
            for g in (gqkv, gproj, gup, gdown)
        )
        part = b_all.shape[0] // N
        b_ada_grad = lax.dynamic_slice_in_dim(b_all, place * part, part)
    return (mixed, tokens_grad, w_ada_grad, b_ada_grad, gqkv, gproj, gup, gdown)


def solution(mesh):
    placed = (
        P(("wide", "narrow"), None),
        P("wide", None),
        P("wide"),
        P(None, "narrow"),
        P("narrow"),
        P(None, None, "narrow"),
        P(None, "narrow"),
        P(None, "narrow"),
        P("narrow", None),
        P(("wide", "narrow"), None),
    )
    return jax.shard_map(
        functools.partial(shards, mesh.shape["wide"]),
        mesh=mesh,
        in_specs=placed,
        out_specs=(
            P(("wide", "narrow"), None),
            P(("wide", "narrow"), None),
            P("wide", "narrow"),
            P(("narrow", "wide")),
            P("wide", None, "narrow"),
            P("wide", "narrow"),
            P("wide", "narrow"),
            P(("narrow", "wide"), None),
        ),
        check_vma=False,
    )
```

```python
import functools
import math

import jax
import jax.numpy as jnp
from jax import lax
from jax.experimental import pallas as pl
from jax.experimental.pallas import tpu as pltpu
from jax.sharding import PartitionSpec as P

D = 1152
HEAD = 72
HEADS_LOCAL = 4
QUARTER = 288
HALF = 576
BLK = 144
SUB_A = 80
SEG = 128
OWN = 256
GROUP = 512
ATT = 640
NEG = -1e30
EPS = 1e-6
FACTOR = HEAD ** -0.5
GELU_ONE = math.sqrt(2.0 / math.pi)
GELU_TWO = 0.044715

f32, bf16 = jnp.float32, jnp.bfloat16
MESH = pl.DeviceIdType.MESH
NN = (((1,), (0,)), ((), ()))
NT = (((1,), (1,)), ((), ()))
TN = (((0,), (0,)), ((), ()))
PAIRS = ((0, (0, 1)), (128, (2, 3)))


def dot(a, b, dims):
    return lax.dot_general(a, b, dims, preferred_element_type=f32)


def rows_at(start, size, align=16):
    return pl.ds(pl.multiple_of(start, align), size)


def mean_row(v):
    return jnp.sum(v, axis=-1, keepdims=True) * (1.0 / D)


def norm_parts(v):
    centred = v - mean_row(v)
    scale = lax.rsqrt(mean_row(centred * centred) + EPS)
    return centred * scale, scale


def norm_back(normal, scale, e):
    return scale * (e - mean_row(e) - normal * mean_row(e * normal))


def by_eight(v):
    return sum(v[i : i + 8, :] for i in range(0, v.shape[0], 8))


class Names:
    def __init__(self):
        self.ids = {}

    def __call__(self, *name):
        return self.ids.setdefault(name, len(self.ids))


SEMS = 122


def kernel(
    gather_wide, step,
    seg, cond, bada, tok_h, og_h, wada_h, wqkv_h, wproj_h, wup_h, wdown_h,
    mixed_o, tg_o, gown_o, gfar_o, mall_o, silu_o,
    wt, crecv, frecv, srecv, zrecv, tok, og, h1, qkv, heads, lse_t, attp, attr, h2, mlpg, big,
    mlpp, mlpr, seco, secr, mgrad, attg, hgrad, facc, keys_t, dq_t, firstr, modblk, modrecv, silu_all, msum, mgs, mgr, mall, silu16,
    ssem, rsem, lsem,
):
    w = lax.axis_index("wide")
    n = lax.axis_index("narrow")
    b = w // step
    bits = (b % 2, (b // 2) % 2, b // 4)
    low, high = n % 2, n // 2

    def narrow_to(mask):
        m = n
        if mask & 1:
            m = m + 1 - 2 * low
        if mask & 2:
            m = m + 2 - 4 * high
        return (w, m)

    def wide_to(mask):
        m = w
        for k in range(3):
            if mask & (1 << k):
                m = m + step * (1 << k) * (1 - 2 * bits[k])
        return (m, n)

    def block_of(mask):
        m = b
        for k in range(3):
            if mask & (1 << k):
                m = m + (1 << k) * (1 - 2 * bits[k])
        return m

    names = Names()

    def remote(name, src, dst, dev):
        k = names(*name)
        return pltpu.make_async_remote_copy(
            src_ref=src, dst_ref=dst, send_sem=ssem.at[k], recv_sem=rsem.at[k], device_id=dev, device_id_type=MESH
        )

    sends = {}

    def send(name, src, dst, dev):
        copy = remote(name, src, dst, dev)
        copy.start()
        sends[name] = copy

    def recv(name, landing):
        remote(name, landing, landing, narrow_to(1)).wait_recv()

    def sent(prefix):
        for name in [s for s in sends if s[: len(prefix)] == prefix]:
            sends.pop(name).wait_send()

    locals_ = Names()

    def load(name, src, dst):
        copy = pltpu.make_async_copy(src, dst, lsem.at[locals_(name)])
        copy.start()
        return copy

    off = 128 * high
    own_at = off + OWN * low
    other_at = off + OWN * (1 - low)
    halo_at = GROUP * (1 - high)
    halo_there = GROUP * high

    load_m = load("m", wada_h, big.at[pl.ds(0, 3 * HALF)])
    load_a = load("a", wqkv_h, wt.at[0, pl.ds(0, 3 * QUARTER)])
    load_b = load("b", wproj_h, wt.at[0, pl.ds(3 * QUARTER, QUARTER)])
    load_t = load("t", tok_h, tok.at[rows_at(own_at, OWN)])
    load_u = load("u", wup_h, wt.at[1])
    load_d = load("d", wdown_h, wt.at[2])
    load_g = load("g", og_h, og.at[rows_at(OWN * low, OWN)])
    barrier = pltpu.get_barrier_semaphore()
    partners = [narrow_to(m) for m in (1, 2, 3)] + [wide_to(m) for m in (range(1, 8) if gather_wide else (1, 2, 4))]
    for dev in partners:
        pl.semaphore_signal(barrier, inc=1, device_id=dev, device_id_type=MESH)

    c = cond[...].astype(f32)
    silu = (c / (1.0 + jnp.exp(-c))).astype(bf16).astype(f32)
    silu16[...] = jnp.zeros((16, D), f32)
    for i in range(3):
        silu16[4 * i : 4 * i + 4, :] = silu
    silu_low = silu16[...].astype(bf16)
    silu_all[b] = silu_low
    load_m.wait()
    third = lax.broadcasted_iota(jnp.int32, (16, HALF), 0) // 4
    part = jnp.zeros((16, HALF), f32)
    for i in range(3):
        value = dot(silu_low, big[HALF * i : HALF * (i + 1), :], NT) + bada[i : i + 1, :]
        part = jnp.where(third == i, value, part)
    modrecv[n, :, 0:HALF] = part
    modrecv[n, :, HALF:ATT] = jnp.zeros((16, ATT - HALF), f32)
    modblk[...] = jnp.zeros((6, 8, D), f32)
    pl.semaphore_wait(barrier, len(partners))

    def block_rows(mask, part=None):
        base = block_of(mask) * BLK
        if part is None:
            return rows_at(base, BLK)
        return rows_at(base, SUB_A) if part == 0 else rows_at(base + SUB_A, BLK - SUB_A)

    def ag_z(m):
        r = block_rows(0)
        send(("ag", m, "z"), wt.at[m, r], wt.at[3 + m, r], narrow_to(2))

    def ag_pass(m, name, mask, axis, part=None):
        r = block_rows(mask, part)
        send(("ag", m) + name, wt.at[3 + m, r], wt.at[3 + m, r], wide_to(axis))

    def ag_take(m, name, mask, part=None):
        recv(("ag", m) + name, wt.at[3 + m, block_rows(mask, part)])

    def ag_one(m):
        ag_take(m, ("z",), 0)
        ag_pass(m, ("x",), 0, 2)
        ag_pass(m, ("y",), 0, 4)
        ag_pass(m, ("c", 0), 0, 1)

    def ag_two(m):
        ag_take(m, ("x",), 2)
        ag_pass(m, ("xy",), 2, 4, 0)
        ag_take(m, ("y",), 4)
        ag_pass(m, ("yx",), 4, 2, 1)
        ag_pass(m, ("c", 2), 2, 1)
        ag_pass(m, ("c", 4), 4, 1)

    def ag_three(m):
        ag_take(m, ("xy",), 6, 0)
        ag_take(m, ("yx",), 6, 1)
        ag_pass(m, ("c", 6), 6, 1)

    def ag_end(m):
        for mask in (0, 2, 4, 6):
            ag_take(m, ("c", mask), mask ^ 1)

    for mask in (1, 2, 3):
        send(("mod", mask), modrecv.at[n], modrecv.at[n], narrow_to(mask))
    send(("tok",), tok_h, tok.at[rows_at(own_at, OWN)], narrow_to(1))
    halo_first = remote(
        ("halo", 0), tok_h.at[rows_at(128 * (1 - high), SEG)], tok.at[rows_at(halo_there, SEG)], narrow_to(2)
    )
    halo_second = remote(
        ("halo", 1), tok.at[rows_at(halo_at, SEG)], tok.at[rows_at(halo_at, SEG)], narrow_to(1)
    )
    halo_source = low != high

    @pl.when(halo_source)
    def _():
        halo_first.start()

    load_a.wait()
    load_b.wait()
    ag_z(0)
    for mask in (1, 2, 3):
        m = narrow_to(mask)[1]
        recv(("mod", mask), modrecv.at[m])
    for k in range(6):
        halves = [modrecv[i // 3, i % 3 * 4 : i % 3 * 4 + 4, :] for i in (2 * k, 2 * k + 1)]
        first, second = halves[0], pltpu.roll(halves[1], 64, 1)
        modblk[k, 0:4, 0:512] = first[:, 0:512]
        modblk[k, 0:4, 512:640] = first[:, 512:640] + second[:, 0:128]
        modblk[k, 0:4, 640:D] = second[:, 128:640]

    def mod_row(k, shard_block):
        return modblk[k, pl.ds(seg[shard_block * SEG], 1), :]

    def first_norm(base, size):
        def body(t, carry):
            r = rows_at(base + t * 32, 32, 32)
            block = 3 * high + (base + t * 32) // SEG
            normal, _ = norm_parts(tok[r, :].astype(f32))
            h1[r, :] = (normal * (1.0 + mod_row(1, block)) + mod_row(0, block)).astype(bf16)
            return carry

        lax.fori_loop(0, size // 32, body, 0)

    load_t.wait()
    first_norm(own_at, OWN)

    @pl.when(jnp.logical_not(halo_source))
    def _():
        halo_first.wait_recv()
        halo_second.start()

    ag_one(0)
    load_u.wait()
    ag_z(1)
    recv(("tok",), tok.at[rows_at(other_at, OWN)])
    load_g.wait()
    send(("og",), og_h, og.at[rows_at(OWN * low, OWN)], narrow_to(1))
    first_norm(other_at, OWN)

    @pl.when(halo_source)
    def _():
        halo_second.wait_recv()
        halo_first.wait_send()

    first_norm(halo_at, SEG)

    @pl.when(jnp.logical_not(halo_source))
    def _():
        halo_second.wait_send()

    def project(s):
        def body(i, carry):
            qkv[s, i] = dot(h1[...], wt[3 * s, rows_at(QUARTER * i, 384), :], NT).astype(bf16)
            return carry

        lax.fori_loop(0, 3, body, 0)

    def key_bias(j, k0, count):
        mine = seg[SEG * (j + 3 * high)]
        return [jnp.where(seg[SEG * (k0 + i + 3 * high)] == mine, 0.0, NEG) for i in range(count)]

    lane_pair = lax.broadcasted_iota(jnp.int32, (SEG, 256), 1)
    pair_masks = [
        [(lane_pair >= HEAD * hd - a) & (lane_pair < HEAD * (hd + 1) - a) for hd in hds] for a, hds in PAIRS
    ]

    def stacked(value, masks):
        value = value.astype(f32)
        return jnp.concatenate([jnp.where(m, value, 0.0).astype(bf16) for m in masks], axis=0)

    def attend(s, j, k0, count):
        r = rows_at(j * SEG, SEG, SEG)
        keys = slice(k0 * SEG, (k0 + count) * SEG)
        bias = key_bias(j, k0, count)
        out = [jnp.zeros((SEG, 128), f32) for _ in range(3)]
        lse = jnp.zeros((SEG, 128), f32)
        lane = lax.broadcasted_iota(jnp.int32, (SEG, 128), 1)
        for (a, hds), masks in zip(PAIRS, pair_masks):
            cols = slice(a, a + 256)
            scores = dot(stacked(qkv[s, 0, r, cols], masks), qkv[s, 1, keys, cols], NT) * FACTOR
            scores = jnp.concatenate(
                [scores[:, i * SEG : (i + 1) * SEG] + bias[i] for i in range(count)], axis=1
            )
            top = jnp.max(scores, axis=1, keepdims=True)
            weights = jnp.exp(scores - top)
            total = jnp.sum(weights, axis=1, keepdims=True)
            prob = (weights * (1.0 / total)).astype(bf16)
            res = dot(prob, qkv[s, 2, keys, cols], NN)
            log_total = top + jnp.log(total)
            for i, hd in enumerate(hds):
                part = jnp.where(masks[i], res[i * SEG : (i + 1) * SEG, :], 0.0)
                out[a // 128] += part[:, 0:128]
                out[a // 128 + 1] += part[:, 128:256]
                lse = jnp.where(lane == hd, log_total[i * SEG : (i + 1) * SEG, :], lse)
        for i in range(3):
            heads[s, r, i * 128 : (i + 1) * 128] = out[i].astype(bf16)
        lse_t[s, :, r] = lse.T[0:8, :]

    def for_blocks(fn, between=()):
        fn(0, 0, 2)
        for hook in between[0:1]:
            hook()
        fn(1, 0, 5)
        for hook in between[1:2]:
            hook()

        def body(j, carry):
            fn(j, 1, 4)
            return carry

        lax.fori_loop(2, 5, body, 0)

    project(0)
    load_d.wait()
    ag_z(2)
    ag_two(0)
    for_blocks(functools.partial(attend, 0), (lambda: None, lambda: ag_three(0)))
    ag_one(1)
    ag_end(0)
    project(1)
    for_blocks(functools.partial(attend, 1))
    ag_two(1)
    def order(i):
        return 1 - high if i == 0 else high

    if gather_wide:
        for mask in range(1, 8):
            send(("silu", mask), silu_all.at[b], silu_all.at[b], wide_to(mask))
    for i in range(2):
        cc = order(i)
        src = rows_at(off + OWN * cc, OWN)
        dst = rows_at(OWN * cc, OWN)

        def body(t, carry):
            cols = pl.ds(pl.multiple_of(t * 384, 128), 384)
            part = dot(heads[0, src, 0:QUARTER], wt[0, 3 * QUARTER : D, cols], NN)
            part += dot(heads[1, src, 0:QUARTER], wt[3, 3 * QUARTER : D, cols], NN)
            attp[dst, cols] = part.astype(bf16)
            return carry

        lax.fori_loop(0, 3, body, 0)
        if i == 0:
            send(("att", i), attp.at[dst], attr.at[dst], narrow_to(1))

    ag_three(1)
    ag_one(2)
    recv(("og",), og.at[rows_at(OWN * (1 - low), OWN)])

    for i in range(2):
        cc = order(i)
        chunk = rows_at(OWN * cc, OWN)
        recv(("att", i), attr.at[chunk])
        if i == 0:
            dst = rows_at(OWN * order(1), OWN)
            send(("att", 1), attp.at[dst], attr.at[dst], narrow_to(1))

        def second_norm(t, carry):
            r = rows_at(OWN * cc + t * 32, 32, 32)
            ra = rows_at(off + OWN * cc + t * 32, 32, 32)
            block = 4 * high + 2 * cc + t // 4
            branch = attp[r, :].astype(f32) + attr[r, :].astype(f32)
            middle = tok[ra, :].astype(f32) + mod_row(2, block) * branch
            normal, _ = norm_parts(middle)
            h2[r, :] = (normal * (1.0 + mod_row(4, block)) + mod_row(3, block)).astype(bf16)
            mlpg[r, :] = (mod_row(5, block) * og[r, :].astype(f32)).astype(bf16)
            return carry

        lax.fori_loop(0, OWN // 32, second_norm, 0)
        if i == 0:
            ag_two(2)
            ag_end(1)

        def units(k, carry):
            s, t = k // 3, k % 3
            cols = pl.ds(pl.multiple_of(t * 384, 128), 384)
            up = dot(h2[chunk, :], wt[3 * s + 1, :, cols], NN)
            grad = dot(mlpg[chunk, :], wt[3 * s + 2, cols, :], NT)
            square = up * up
            th = jnp.tanh(GELU_ONE * (up + GELU_TWO * up * square))
            half_one = 0.5 * (1.0 + th)
            act = up * half_one
            slope = half_one + 0.5 * up * (1.0 - th * th) * (GELU_ONE * (1.0 + 3.0 * GELU_TWO * square))
            big[rows_at(GROUP * s + OWN * cc, OWN), cols] = act.astype(bf16)
            big[rows_at(2 * GROUP + GROUP * s + OWN * cc, OWN), cols] = (grad * slope).astype(bf16)
            return carry

        lax.fori_loop(0, 3, units, 0)
        if i == 0:
            ag_three(2)
            ag_end(2)
        lax.fori_loop(3, 6, units, 0)

        def inputs_back(t, carry):
            cols = pl.ds(pl.multiple_of(t * 384, 128), 384)
            part = dot(big[rows_at(2 * GROUP + OWN * cc, OWN), :], wt[1, cols, :], NT)
            part += dot(big[rows_at(3 * GROUP + OWN * cc, OWN), :], wt[4, cols, :], NT)
            seco[chunk, cols] = part.astype(bf16)
            return carry

        lax.fori_loop(0, 3, inputs_back, 0)
        send(("sec", i), seco.at[chunk], secr.at[chunk], narrow_to(1))

    sent(("ag",))

    def kept(mask):
        return rows_at(block_of(mask) * BLK, BLK)

    def pieces(m):
        return ((pl.ds(0, 640), 2, 4), (pl.ds(640, 512), 4, 2))

    def rs_core(m):
        for i, mask in enumerate((0, 2, 4, 6)):
            send(("rs", m, "c", i), wt.at[m, kept(mask ^ 1)], crecv.at[m, pl.ds(i * BLK, BLK)], wide_to(1))

    def add_into(m, mask, ref, at, cols):
        def body(t, carry):
            r = rows_at(block_of(mask) * BLK + t * 48, 48)
            wt[m, r, cols] = wt[m, r, cols] + ref[m, rows_at(at + t * 48, 48), cols]
            return carry

        lax.fori_loop(0, BLK // 48, body, 0)

    def rs_one(m):
        for i, mask in enumerate((0, 2, 4, 6)):
            recv(("rs", m, "c", i), crecv.at[m, pl.ds(i * BLK, BLK)])
        for p, (cols, first, second) in enumerate(pieces(m)):
            for mask in (first, 6):
                add_into(m, mask, crecv, mask // 2 * BLK, cols)
            for i, mask in enumerate((0, second)):
                send(
                    ("rs", m, "f", p, i), wt.at[m, kept(mask ^ first), cols], frecv.at[m, pl.ds(i * BLK, BLK), cols],
                    wide_to(first),
                )
        for p, (cols, first, second) in enumerate(pieces(m)):
            for mask in (0, second):
                add_into(m, mask, crecv, mask // 2 * BLK, cols)

    def rs_two(m):
        for p, (cols, first, second) in enumerate(pieces(m)):
            recv(("rs", m, "f", p, 1), frecv.at[m, pl.ds(BLK, BLK), cols])
            add_into(m, second, frecv, BLK, cols)
            send(("rs", m, "s", p), wt.at[m, kept(second), cols], srecv.at[m, :, cols], wide_to(second))
        for p, (cols, first, second) in enumerate(pieces(m)):
            recv(("rs", m, "f", p, 0), frecv.at[m, pl.ds(0, BLK), cols])
            add_into(m, 0, frecv, 0, cols)

    outs = []

    def rs_three(m):
        for p, (cols, _, _) in enumerate(pieces(m)):
            recv(("rs", m, "s", p), srecv.at[m, :, cols])
            add_into(m, 0, srecv, 0, cols)
        if m >= 3:
            send(("rs", m, "z"), wt.at[m, kept(0)], zrecv.at[m - 3], narrow_to(2))
        else:
            outs.append(load(("own", m), wt.at[m, kept(0)], gown_o.at[m]))

    def rs_four(m):
        recv(("rs", m + 3, "z"), zrecv.at[m])
        outs.append(load(("far", m), zrecv.at[m], gfar_o.at[m]))

    def down(t, carry):
        cols = pl.ds(pl.multiple_of(t * 384, 128), 384)
        part = dot(big[0:GROUP, :], wt[2, :, cols], NN)
        part += dot(big[GROUP : 2 * GROUP, :], wt[5, :, cols], NN)
        mlpp[:, :, cols] = part.astype(bf16).reshape(2, OWN, 384)
        return carry

    def by_columns(fn, count, tail=None):
        def body(t, carry):
            fn(pl.ds(pl.multiple_of(t * 256, 128), 256))
            return carry

        lax.fori_loop(0, count, body, 0)
        if tail is not None:
            fn(pl.ds(tail, 128))

    def down_grad(s):
        def tile(cols):
            wt[3 * s + 2, :, cols] = dot(big[pl.ds(GROUP * s, GROUP), :], mlpg[:, cols], TN).astype(bf16)

        by_columns(tile, 4, 1024)

    def up_grad(s):
        def tile(cols):
            wt[3 * s + 1, :, cols] = dot(h2[...], big[pl.ds(2 * GROUP + GROUP * s, GROUP), cols], TN).astype(bf16)

        by_columns(tile, 4, 1024)

    up_grad(1)
    rs_core(4)
    msum[...] = jnp.zeros((2, 6, 8, D), f32)
    for i in range(2):
        cc = order(i)
        chunk = rows_at(OWN * cc, OWN)
        recv(("sec", i), secr.at[chunk])

        def parts(t):
            r = rows_at(OWN * cc + t * 32, 32, 32)
            ra = rows_at(off + OWN * cc + t * 32, 32, 32)
            block = 4 * high + 2 * cc + t // 4
            branch = attp[r, :].astype(f32) + attr[r, :].astype(f32)
            gate = mod_row(2, block)
            normal, scale = norm_parts(tok[ra, :].astype(f32) + gate * branch)
            grad = seco[r, :].astype(f32) + secr[r, :].astype(f32)
            mid = og[r, :].astype(f32) + norm_back(normal, scale, grad * (1.0 + mod_row(4, block)))
            attg[ra, :] = (gate * mid).astype(bf16)
            return branch, normal, grad, mid

        @pl.when(cc == low)
        def _():
            def body(t, carry):
                branch, normal, grad, mid = parts(t)
                mgrad[rows_at(t * 32, 32, 32), :] = mid
                at = t // 4
                for k, v in ((2, mid * branch), (3, grad), (4, grad * normal)):
                    msum[at, k] += by_eight(v)
                return carry

            lax.fori_loop(0, OWN // 32, body, 0)

        @pl.when(cc != low)
        def _():
            def body(t, carry):
                parts(t)
                return carry

            lax.fori_loop(0, OWN // 32, body, 0)

        if i == 0:
            r = rows_at(off + 384 * (1 - high) + 64 * low, 64)
            send(("ahalo", 0), attg.at[r], attg.at[rows_at(halo_there + 64 * low, 64)], narrow_to(2))
            rs_one(4)
            lax.fori_loop(0, 3, down, 0)
            down_grad(1)
            rs_core(5)
            down_grad(0)
            rs_core(2)
            rs_two(4)
            rs_one(5)
            r = rows_at(halo_at + 64 * low, 64)
            recv(("ahalo", 0), attg.at[r])
            send(("ahalo", 1), attg.at[r], attg.at[r], narrow_to(1))

    recv(("ahalo", 1), attg.at[rows_at(halo_at + 64 * (1 - low), 64)])
    send(("mlp",), mlpp.at[1 - low], mlpr, narrow_to(1))

    def mix(t, carry):
        r = rows_at(OWN * low + t * 32, 32, 32)
        ra = rows_at(own_at + t * 32, 32, 32)
        rr = rows_at(t * 32, 32, 32)
        block = 4 * high + 2 * low + t // 4
        branch = attp[r, :].astype(f32) + attr[r, :].astype(f32)
        middle = tok[ra, :].astype(f32) + mod_row(2, block) * branch
        mlp = mlpp[low, rr, :].astype(f32) + mlpr[rr, :].astype(f32)
        mlpr[rr, :] = (middle + mod_row(5, block) * mlp).astype(bf16)
        msum[t // 4, 5] += by_eight(og[r, :].astype(f32) * mlp)
        return carry

    def attend_back(s, j, k0, count):
        r = rows_at(j * SEG, SEG, SEG)
        keys = slice(k0 * SEG, (k0 + count) * SEG)
        bias = key_bias(j, k0, count)
        row = lax.broadcasted_iota(jnp.int32, (256, SEG), 0)
        for (a, hds), masks in zip(PAIRS, pair_masks):
            cols = slice(a, a + 256)
            q = stacked(qkv[s, 0, r, cols], masks)
            hg = stacked(hgrad[r, cols], masks)
            top = jnp.concatenate([lse_t[s, hd : hd + 1, r] for hd in hds], axis=1)
            scores = dot(qkv[s, 1, keys, cols], q, NT) * FACTOR
            prob = jnp.exp(
                jnp.concatenate(
                    [scores[i * SEG : (i + 1) * SEG, :] - (top - bias[i]) for i in range(count)], axis=0
                )
            )
            prob_grad = dot(qkv[s, 2, keys, cols], hg, NT)
            inner = jnp.sum(prob * prob_grad, axis=0, keepdims=True)
            score_grad = (prob * (prob_grad - inner)).astype(bf16)
            facc[0, keys, cols] += dot(score_grad, q, NN)
            facc[1, keys, cols] += dot(prob.astype(bf16), hg, NN)
            res = dot(keys_t[a : a + 256, keys], score_grad, NN)
            total = jnp.zeros((256, SEG), f32)
            for i, hd in enumerate(hds):
                mine = (row >= HEAD * hd - a) & (row < HEAD * (hd + 1) - a)
                total += jnp.where(mine, res[:, i * SEG : (i + 1) * SEG], 0.0)
            dq_t[a : a + 256, r] += total

    def pack(s):
        lane = lax.broadcasted_iota(jnp.int32, (128, 384), 1)

        def body(t, carry):
            ra = rows_at(off + t * 128, 128, 128)
            rg = rows_at(GROUP * s + t * 128, 128, 128)
            q = jnp.where(lane < QUARTER, dq_t[:, ra].T * FACTOR, 0.0)
            k = pltpu.roll(jnp.where(lane < QUARTER, facc[0, ra, :] * FACTOR, 0.0), 32, 1)
            v = pltpu.roll(jnp.where(lane < QUARTER, facc[1, ra, :], 0.0), 64, 1)
            hd = pltpu.roll(heads[s, ra, :].astype(f32), 96, 1)
            tiles = [
                q[:, 0:128],
                q[:, 128:256],
                q[:, 256:384] + k[:, 0:128],
                k[:, 128:256],
                k[:, 256:384] + v[:, 0:128],
                v[:, 128:256],
                v[:, 256:384],
            ]
            for i, tile in enumerate(tiles):
                big[rg, i * 128 : (i + 1) * 128] = tile.astype(bf16)
            heads[s, ra, :] = hd.astype(bf16)
            return carry

        lax.fori_loop(0, GROUP // 128, body, 0)

    def first_far(t, carry):
        half, cols = t // 3, pl.ds(pl.multiple_of(t % 3 * 384, 128), 384)
        part = dot(big[rows_at(GROUP + OWN * half, OWN), 0 : 3 * QUARTER], wt[3, 0 : 3 * QUARTER, cols], NN)
        high_part = part.astype(bf16)
        secr[rows_at(OWN * half, OWN), cols] = high_part
        mlpg[rows_at(OWN * half, OWN), cols] = (part - high_part.astype(f32)).astype(bf16)
        return carry

    def first_back(half, at):
        def body(t, carry):
            cols = pl.ds(pl.multiple_of(t * 384, 128), 384)
            part = dot(big[rows_at(OWN * half, OWN), 0 : 3 * QUARTER], wt[0, 0 : 3 * QUARTER, cols], NN)
            part += secr[rows_at(OWN * half, OWN), cols].astype(f32)
            part += mlpg[rows_at(OWN * half, OWN), cols].astype(f32)
            seco[pl.ds(at, OWN), cols] = part.astype(bf16)
            return carry

        lax.fori_loop(0, 3, body, 0)

    def attn_grad(s):
        rg = rows_at(off, GROUP)

        def tile(cols):
            wt[3 * s, :, cols] = dot(h1[rg, :], big[pl.ds(GROUP * s, GROUP), cols], TN).astype(bf16)

        by_columns(tile, 3)
        part = dot(h1[rg, :], big[pl.ds(GROUP * s, GROUP), 768:896], TN)
        part += dot(attg[rg, :], heads[s, rg, 0:128], TN)
        wt[3 * s, :, 768:896] = part.astype(bf16)
        wt[3 * s, :, 896:D] = dot(attg[rg, :], heads[s, rg, 128:384], TN).astype(bf16)

    def heads_back(s, between):
        hgrad[:, 0:QUARTER] = dot(attg[...], wt[3 * s, 3 * QUARTER : D, :], NT).astype(bf16)
        facc[...] = jnp.zeros((2, ATT, 384), f32)
        dq_t[...] = jnp.zeros((384, ATT), f32)
        for i in range(5):
            keys_t[:, i * 128 : (i + 1) * 128] = qkv[s, 1, i * 128 : (i + 1) * 128, :].T
        for_blocks(functools.partial(attend_back, s), between)
        pack(s)

    heads_back(1, (lambda: rs_three(4), lambda: rs_one(2)))
    rs_two(5)
    lax.fori_loop(0, 6, first_far, 0)
    rs_three(5)
    attn_grad(1)
    rs_core(3)
    rs_two(2)
    up_grad(0)
    rs_core(1)
    rs_one(3)
    heads_back(0, (lambda: None, lambda: rs_one(1)))
    rs_two(3)
    sent(("sec",))
    first_back(1 - low, 0)
    send(("first",), seco.at[pl.ds(0, OWN)], firstr, narrow_to(1))
    first_back(low, OWN)
    attn_grad(0)
    rs_core(0)
    recv(("mlp",), mlpr)
    lax.fori_loop(0, OWN // 32, mix, 0)
    outs.append(load("mixed", mlpr, mixed_o))
    rs_three(2)
    rs_one(0)
    rs_three(3)
    rs_two(1)

    recv(("first",), firstr)

    def tokens_back(t, carry):
        ra = rows_at(own_at + t * 32, 32, 32)
        rr = rows_at(t * 32, 32, 32)
        block = 4 * high + 2 * low + t // 4
        normal, scale = norm_parts(tok[ra, :].astype(f32))
        grad = seco[rows_at(OWN + t * 32, 32, 32), :].astype(f32) + firstr[rr, :].astype(f32)
        res = mgrad[rr, :] + norm_back(normal, scale, grad * (1.0 + mod_row(1, block)))
        firstr[rr, :] = res.astype(bf16)
        for k, v in ((0, grad), (1, grad * normal)):
            msum[t // 4, k] += by_eight(v)
        return carry

    lax.fori_loop(0, OWN // 32, tokens_back, 0)
    outs.append(load("tg", firstr, tg_o))

    sent(("mod",))
    row = lax.broadcasted_iota(jnp.int32, (8, D), 0)
    lane = lax.broadcasted_iota(jnp.int32, (8, ATT), 1)
    for k in range(6):
        total = jnp.zeros((8, D), f32)
        for i in range(2):
            slot = seg[SEG * (4 * high + 2 * low + i)]
            total += jnp.where((row == slot) & (row < 4), jnp.sum(msum[i, k], axis=0, keepdims=True), 0.0)
        for i, value in ((2 * k, total[:, 0:ATT]), (2 * k + 1, pltpu.roll(total[:, 512:D], HALF, 1))):
            modrecv[i // 3, i % 3 * 4 : i % 3 * 4 + 4, :] = jnp.where(lane < HALF, value, 0.0)[0:4, :]
    for i in range(4):
        modrecv[i, 12:16, :] = jnp.zeros((4, ATT), f32)
        mgs[i] = modrecv[i].astype(bf16)
    for mask in (1, 2, 3):
        m = narrow_to(mask)[1]
        send(("mg", mask), mgs.at[m], mgr.at[mask - 1], narrow_to(mask))
    rs_three(1)
    rs_two(0)
    rs_four(2)
    rs_four(1)
    for mask in (1, 2, 3):
        recv(("mg", mask), mgr.at[mask - 1])
    total = modrecv[n] + mgr[0].astype(f32) + mgr[1].astype(f32) + mgr[2].astype(f32)
    mall[b] = total.astype(bf16)
    if gather_wide:
        for mask in range(1, 8):
            send(("mall", mask), mall.at[b], mall.at[b], wide_to(mask))
    rs_three(0)
    rs_four(0)
    if gather_wide:
        for mask in range(1, 8):
            recv(("silu", mask), silu_all.at[block_of(mask)])
            recv(("mall", mask), mall.at[block_of(mask)])
    outs.append(load("mall", mall, mall_o))
    outs.append(load("silu", silu_all, silu_o))
    for copy in outs:
        copy.wait()
    sent(())


def finish(
    step, mixed_h, tg_h, gown_h, gfar_h, mall_h, silu_h,
    mixed_o, tg_o, wada_o, bada_o, gqkv_o, gproj_o, gup_o, gdown_o,
    gown, gfar, mall, silu, mixed, tg, wada, sums, bada, gqkv, gproj, gffn, sem,
):
    ids = Names()

    def move(src, dst):
        copy = pltpu.make_async_copy(src, dst, sem.at[ids(len(ids.ids))])
        copy.start()
        return copy

    ins = [move(mall_h, mall), move(silu_h, silu), move(gown_h, gown), move(gfar_h, gfar)]
    outs = []
    rows = [move(mixed_h, mixed), move(tg_h, tg)]
    rows[0].wait()
    outs.append(move(mixed, mixed_o))
    rows[1].wait()
    outs.append(move(tg, tg_o))
    b = lax.axis_index("wide") // step
    ins[0].wait()
    ins[1].wait()
    pick_row = lax.broadcasted_iota(jnp.int32, (BLK, D), 0) + b * BLK
    pick_col = lax.broadcasted_iota(jnp.int32, (BLK, D), 1)
    pick = jnp.where(pick_row == pick_col, 1.0, 0.0).astype(bf16)
    left = dot(pick, silu[...].reshape(128, D), NT).astype(bf16)
    third = lax.broadcasted_iota(jnp.int32, (BLK, 128), 1) % 16 // 4
    right = mall[...].reshape(128, ATT)
    for i in range(3):
        part = dot(jnp.where(third == i, left, 0), right, NN)
        total = dot(jnp.where(third[0:8] == i, 1.0, 0.0).astype(bf16), right, NN)
        if i == 1:
            part, total = pltpu.roll(part, 64, 1), pltpu.roll(total, 64, 1)
            wada[:, 512:640] += part[:, 0:128]
            wada[:, 640:D] = part[:, 128:640]
            sums[:, 512:640] += total[:, 0:128]
            sums[:, 640:D] = total[:, 128:640]
        else:
            at = i * HALF
            wada[:, at : at + HALF] = part[:, 0:HALF]
            sums[:, at : at + ATT] = total
            if i == 0:
                wada[:, HALF:640] = jnp.zeros((BLK, 64), f32)
    place = lax.axis_index("wide")
    bada[...] = pltpu.roll(sums[...], 14 * 128 - place * 216, 1)[0:1, 0:216]
    outs.append(move(wada, wada_o))
    outs.append(move(bada, bada_o))
    ins[2].wait()
    ins[3].wait()
    for m in range(3):
        total = gown[m].astype(f32) + gfar[m].astype(f32)
        if m == 0:
            gqkv[0] = total[:, 0:QUARTER]
            gqkv[1] = pltpu.roll(total[:, 256:640], 352, 1)[:, 0:QUARTER]
            gqkv[2] = pltpu.roll(total[:, 512:896], 320, 1)[:, 0:QUARTER]
            gproj[...] = pltpu.roll(total[:, 768:D], 288, 1)[:, 0:QUARTER]
            outs.append(move(gqkv, gqkv_o))
            outs.append(move(gproj, gproj_o))
        else:
            gffn[m - 1] = total
            outs.append(move(gffn.at[m - 1], (gup_o, gdown_o)[m - 1]))
    for copy in outs:
        copy.wait()


def shards(N, tokens, condition, segment, w_ada, b_ada, w_qkv, w_proj, w_up, w_down, out_grad):
    step = N // 8
    gather_wide = N == 8
    anywhere = pl.BlockSpec(memory_space=pl.ANY)
    hbm = pl.BlockSpec(memory_space=pltpu.HBM)
    vmem = pl.BlockSpec(memory_space=pltpu.VMEM)
    smem = pl.BlockSpec(memory_space=pltpu.SMEM)
    shape = jax.ShapeDtypeStruct
    V = pltpu.VMEM
    out = pl.pallas_call(
        functools.partial(kernel, gather_wide, step),
        name="block",
        out_shape=(
            shape((OWN, D), bf16),
            shape((OWN, D), bf16),
            shape((3, BLK, D), bf16),
            shape((3, BLK, D), bf16),
            shape((8, 16, ATT), bf16),
            shape((8, 16, D), bf16),
        ),
        in_specs=[smem, vmem, vmem] + [anywhere] * 7,
        out_specs=(anywhere,) * 6,
        scratch_shapes=[
            V((6, D, D), bf16),
            V((6, 4 * BLK, D), bf16),
            V((6, 2 * BLK, D), bf16),
            V((6, BLK, D), bf16),
            V((3, BLK, D), bf16),
            V((ATT, D), bf16),
            V((GROUP, D), bf16),
            V((ATT, D), bf16),
            V((2, 3, ATT, 384), bf16),
            V((2, ATT, 384), bf16),
            V((2, 8, ATT), f32),
            V((GROUP, D), bf16),
            V((GROUP, D), bf16),
            V((GROUP, D), bf16),
            V((GROUP, D), bf16),
            V((4 * GROUP, D), bf16),
            V((2, OWN, D), bf16),
            V((OWN, D), bf16),
            V((GROUP, D), bf16),
            V((GROUP, D), bf16),
            V((OWN, D), f32),
            V((ATT, D), bf16),
            V((ATT, 384), bf16),
            V((2, ATT, 384), f32),
            V((384, ATT), bf16),
            V((384, ATT), f32),
            V((OWN, D), bf16),
            V((6, 8, D), f32),
            V((4, 16, ATT), f32),
            V((8, 16, D), bf16),
            V((2, 6, 8, D), f32),
            V((4, 16, ATT), bf16),
            V((3, 16, ATT), bf16),
            V((8, 16, ATT), bf16),
            V((16, D), f32),
            pltpu.SemaphoreType.DMA((SEMS,)),
            pltpu.SemaphoreType.DMA((SEMS,)),
            pltpu.SemaphoreType.DMA((17,)),
        ],
        compiler_params=pltpu.CompilerParams(
            collective_id=0, has_side_effects=True, vmem_limit_bytes=63 * 2**20
        ),
    )(
        segment,
        condition,
        b_ada.astype(f32).reshape(3, HALF),
        tokens,
        out_grad,
        w_ada.T,
        w_qkv.transpose(1, 2, 0).reshape(3 * QUARTER, D),
        w_proj.T,
        w_up,
        w_down,
    )
    mixed, tokens_grad, gown, gfar, mall, silu = out
    mixed, tokens_grad, wada, bada, gqkv, gproj, gup, gdown = pl.pallas_call(
        functools.partial(finish, step),
        name="finish",
        out_shape=(
            shape((OWN, D), bf16),
            shape((OWN, D), bf16),
            shape((BLK, 3 * HALF), f32),
            shape((1, 216), f32),
            shape((3, BLK, QUARTER), f32),
            shape((BLK, QUARTER), f32),
            shape((BLK, D), f32),
            shape((BLK, D), f32),
        ),
        in_specs=[hbm] * 6,
        out_specs=(hbm,) * 8,
        scratch_shapes=[
            V((3, BLK, D), bf16),
            V((3, BLK, D), bf16),
            V((8, 16, ATT), bf16),
            V((8, 16, D), bf16),
            V((OWN, D), bf16),
            V((OWN, D), bf16),
            V((BLK, 3 * HALF), f32),
            V((8, 14 * 128), f32),
            V((1, 216), f32),
            V((3, BLK, QUARTER), f32),
            V((BLK, QUARTER), f32),
            V((2, BLK, D), f32),
            pltpu.SemaphoreType.DMA((16,)),
        ],
        compiler_params=pltpu.CompilerParams(vmem_limit_bytes=63 * 2**20),
    )(mixed, tokens_grad, gown, gfar, mall, silu)
    gqkv = gqkv.transpose(1, 0, 2)
    place = lax.axis_index("wide")
    if gather_wide:
        w_ada_grad, b_ada_grad = wada, bada.reshape(216)
    else:
        silu_low = jax.nn.silu(condition.astype(f32)).astype(bf16)
        mine = lax.dynamic_index_in_dim(mall, place // step, keepdims=False)
        mod_grad = jnp.concatenate([mine[4 * i : 4 * i + 4, :HALF] for i in range(3)], axis=1)
        silu_wide = lax.all_gather(silu_low, "wide", axis=0, tiled=True)
        mod_wide = lax.all_gather(mod_grad, "wide", axis=0, tiled=True)
        left = lax.dynamic_slice_in_dim(silu_wide, place * (D // N), D // N, axis=1)
        w_ada_grad = jnp.einsum("id,ic->dc", left, mod_wide, preferred_element_type=f32)
        b_all = jnp.sum(mod_wide.astype(f32), axis=0)
        groups = [[i * step + r for r in range(step)] for i in range(8)]
        gqkv, gproj, gup, gdown = (
            lax.psum_scatter(g, "wide", scatter_dimension=0, axis_index_groups=groups, tiled=True)
            for g in (gqkv, gproj, gup, gdown)
        )
        part = b_all.shape[0] // N
        b_ada_grad = lax.dynamic_slice_in_dim(b_all, place * part, part)
    return (mixed, tokens_grad, w_ada_grad, b_ada_grad, gqkv, gproj, gup, gdown)


def solution(mesh):
    placed = (
        P(("wide", "narrow"), None),
        P("wide", None),
        P("wide"),
        P(None, "narrow"),
        P("narrow"),
        P(None, None, "narrow"),
        P(None, "narrow"),
        P(None, "narrow"),
        P("narrow", None),
        P(("wide", "narrow"), None),
    )
    return jax.shard_map(
        functools.partial(shards, mesh.shape["wide"]),
        mesh=mesh,
        in_specs=placed,
        out_specs=(
            P(("wide", "narrow"), None),
            P(("wide", "narrow"), None),
            P("wide", "narrow"),
            P(("narrow", "wide")),
            P("wide", None, "narrow"),
            P("wide", "narrow"),
            P("wide", "narrow"),
            P(("narrow", "wide"), None),
        ),
        check_vma=False,
    )
```

```python
import functools
import math

import jax
import jax.numpy as jnp
from jax import lax
from jax.experimental import pallas as pl
from jax.experimental.pallas import tpu as pltpu
from jax.sharding import PartitionSpec as P

D = 1152
HEAD = 72
HEADS_LOCAL = 4
QUARTER = 288
HALF = 576
BLK = 144
SUB_A = 80
SEG = 128
OWN = 256
GROUP = 512
ATT = 640
NEG = -1e30
EPS = 1e-6
FACTOR = HEAD ** -0.5
GELU_ONE = math.sqrt(2.0 / math.pi)
GELU_TWO = 0.044715

f32, bf16 = jnp.float32, jnp.bfloat16
MESH = pl.DeviceIdType.MESH
NN = (((1,), (0,)), ((), ()))
NT = (((1,), (1,)), ((), ()))
TN = (((0,), (0,)), ((), ()))
PAIRS = ((0, (0, 1)), (128, (2, 3)))


def dot(a, b, dims):
    return lax.dot_general(a, b, dims, preferred_element_type=f32)


def rows_at(start, size, align=16):
    return pl.ds(pl.multiple_of(start, align), size)


def mean_row(v):
    return jnp.sum(v, axis=-1, keepdims=True) * (1.0 / D)


def norm_parts(v):
    centred = v - mean_row(v)
    scale = lax.rsqrt(mean_row(centred * centred) + EPS)
    return centred * scale, scale


def norm_back(normal, scale, e):
    return scale * (e - mean_row(e) - normal * mean_row(e * normal))


def by_eight(v):
    return sum(v[i : i + 8, :] for i in range(0, v.shape[0], 8))


class Names:
    def __init__(self):
        self.ids = {}

    def __call__(self, *name):
        return self.ids.setdefault(name, len(self.ids))


SEMS = 83


def kernel(
    gather_wide, step,
    seg, cond, bada, tok_h, og_h, wada_h, wqkv_h, wproj_h, wup_h, wdown_h,
    mixed_o, tg_o, gown_o, gfar_o, mall_o, silu_o,
    wt, crecv, frecv, srecv, zrecv, tok, og, h1, qkv, heads, lse_t, attp, attr, h2, mlpg, big,
    mlpp, mlpr, seco, secr, mgrad, attg, hgrad, facc, keys_t, dq_t, firstr, modblk, modrecv, silu_all, msum, mgs, mgr, mall, silu16,
    ssem, rsem, lsem,
):
    w = lax.axis_index("wide")
    n = lax.axis_index("narrow")
    b = w // step
    bits = (b % 2, (b // 2) % 2, b // 4)
    low, high = n % 2, n // 2

    def narrow_to(mask):
        m = n
        if mask & 1:
            m = m + 1 - 2 * low
        if mask & 2:
            m = m + 2 - 4 * high
        return (w, m)

    def wide_to(mask):
        m = w
        for k in range(3):
            if mask & (1 << k):
                m = m + step * (1 << k) * (1 - 2 * bits[k])
        return (m, n)

    def block_of(mask):
        m = b
        for k in range(3):
            if mask & (1 << k):
                m = m + (1 << k) * (1 - 2 * bits[k])
        return m

    names = Names()

    def remote(name, src, dst, dev):
        k = names(*name)
        return pltpu.make_async_remote_copy(
            src_ref=src, dst_ref=dst, send_sem=ssem.at[k], recv_sem=rsem.at[k], device_id=dev, device_id_type=MESH
        )

    sends = {}

    def send(name, src, dst, dev, group=None):
        remote(name, src, dst, dev).start()
        sends[name] = remote(name, src, dst, dev) if group is None else remote(name, group, group, dev)

    def recv(name, landing):
        remote(name, landing, landing, narrow_to(1)).wait_recv()

    def sent(prefix):
        for name in [s for s in sends if s[: len(prefix)] == prefix]:
            sends.pop(name).wait_send()

    locals_ = Names()

    def load(name, src, dst):
        copy = pltpu.make_async_copy(src, dst, lsem.at[locals_(name)])
        copy.start()
        return copy

    off = 128 * high
    own_at = off + OWN * low
    other_at = off + OWN * (1 - low)
    halo_at = GROUP * (1 - high)
    halo_there = GROUP * high

    load_m = load("m", wada_h, big.at[pl.ds(0, 3 * HALF)])
    load_a = load("a", wqkv_h, wt.at[0, pl.ds(0, 3 * QUARTER)])
    load_b = load("b", wproj_h, wt.at[0, pl.ds(3 * QUARTER, QUARTER)])
    load_t = load("t", tok_h, tok.at[rows_at(own_at, OWN)])
    load_u = load("u", wup_h, wt.at[1])
    load_d = load("d", wdown_h, wt.at[2])
    load_g = load("g", og_h, og.at[rows_at(OWN * low, OWN)])
    barrier = pltpu.get_barrier_semaphore()
    partners = [narrow_to(m) for m in (1, 2, 3)] + [wide_to(m) for m in (range(1, 8) if gather_wide else (1, 2, 4))]
    for dev in partners:
        pl.semaphore_signal(barrier, inc=1, device_id=dev, device_id_type=MESH)

    c = cond[...].astype(f32)
    silu = (c / (1.0 + jnp.exp(-c))).astype(bf16).astype(f32)
    silu16[...] = jnp.zeros((16, D), f32)
    for i in range(3):
        silu16[4 * i : 4 * i + 4, :] = silu
    silu_low = silu16[...].astype(bf16)
    silu_all[b] = silu_low
    load_m.wait()
    third = lax.broadcasted_iota(jnp.int32, (16, HALF), 0) // 4
    part = jnp.zeros((16, HALF), f32)
    for i in range(3):
        value = dot(silu_low, big[HALF * i : HALF * (i + 1), :], NT) + bada[i : i + 1, :]
        part = jnp.where(third == i, value, part)
    modrecv[n, :, 0:HALF] = part
    modrecv[n, :, HALF:ATT] = jnp.zeros((16, ATT - HALF), f32)
    modblk[...] = jnp.zeros((6, 8, D), f32)
    pl.semaphore_wait(barrier, len(partners))

    def block_rows(mask, part=None):
        base = block_of(mask) * BLK
        if part is None:
            return rows_at(base, BLK)
        return rows_at(base, SUB_A) if part == 0 else rows_at(base + SUB_A, BLK - SUB_A)

    def ag_z(m):
        r = block_rows(0)
        send(("ag", m, "z"), wt.at[m, r], wt.at[3 + m, r], narrow_to(2))

    def ag_pass(m, name, mask, axis, part=None):
        r = block_rows(mask, part)
        group = wt.at[3 + m, pl.ds(0, 4 * BLK)] if axis == 1 else None
        send(("ag", m) + name, wt.at[3 + m, r], wt.at[3 + m, r], wide_to(axis), group)

    def ag_take(m, name, mask, part=None):
        recv(("ag", m) + name, wt.at[3 + m, block_rows(mask, part)])

    def ag_one(m):
        ag_take(m, ("z",), 0)
        ag_pass(m, ("x",), 0, 2)
        ag_pass(m, ("y",), 0, 4)
        ag_pass(m, ("c",), 0, 1)

    def ag_two(m):
        ag_take(m, ("x",), 2)
        ag_pass(m, ("xy",), 2, 4, 0)
        ag_take(m, ("y",), 4)
        ag_pass(m, ("yx",), 4, 2, 1)
        ag_pass(m, ("c",), 2, 1)
        ag_pass(m, ("c",), 4, 1)

    def ag_three(m):
        ag_take(m, ("xy",), 6, 0)
        ag_take(m, ("yx",), 6, 1)
        ag_pass(m, ("c",), 6, 1)

    def ag_end(m):
        recv(("ag", m, "c"), wt.at[3 + m, pl.ds(0, 4 * BLK)])

    for mask in (1, 2, 3):
        send(("mod", mask), modrecv.at[n], modrecv.at[n], narrow_to(mask))
    send(("tok",), tok_h, tok.at[rows_at(own_at, OWN)], narrow_to(1))
    halo_first = remote(
        ("halo", 0), tok_h.at[rows_at(128 * (1 - high), SEG)], tok.at[rows_at(halo_there, SEG)], narrow_to(2)
    )
    halo_second = remote(
        ("halo", 1), tok.at[rows_at(halo_at, SEG)], tok.at[rows_at(halo_at, SEG)], narrow_to(1)
    )
    halo_source = low != high

    @pl.when(halo_source)
    def _():
        halo_first.start()

    load_a.wait()
    load_b.wait()
    ag_z(0)
    for mask in (1, 2, 3):
        m = narrow_to(mask)[1]
        recv(("mod", mask), modrecv.at[m])
    for k in range(6):
        halves = [modrecv[i // 3, i % 3 * 4 : i % 3 * 4 + 4, :] for i in (2 * k, 2 * k + 1)]
        first, second = halves[0], pltpu.roll(halves[1], 64, 1)
        modblk[k, 0:4, 0:512] = first[:, 0:512]
        modblk[k, 0:4, 512:640] = first[:, 512:640] + second[:, 0:128]
        modblk[k, 0:4, 640:D] = second[:, 128:640]

    def mod_row(k, shard_block):
        return modblk[k, pl.ds(seg[shard_block * SEG], 1), :]

    def first_norm(base, size):
        def body(t, carry):
            r = rows_at(base + t * 32, 32, 32)
            block = 3 * high + (base + t * 32) // SEG
            normal, _ = norm_parts(tok[r, :].astype(f32))
            h1[r, :] = (normal * (1.0 + mod_row(1, block)) + mod_row(0, block)).astype(bf16)
            return carry

        lax.fori_loop(0, size // 32, body, 0)

    load_t.wait()
    first_norm(own_at, OWN)

    @pl.when(jnp.logical_not(halo_source))
    def _():
        halo_first.wait_recv()
        halo_second.start()

    ag_one(0)
    load_u.wait()
    ag_z(1)
    recv(("tok",), tok.at[rows_at(other_at, OWN)])
    load_g.wait()
    send(("og",), og_h, og.at[rows_at(OWN * low, OWN)], narrow_to(1))
    first_norm(other_at, OWN)

    @pl.when(halo_source)
    def _():
        halo_second.wait_recv()
        halo_first.wait_send()

    first_norm(halo_at, SEG)

    @pl.when(jnp.logical_not(halo_source))
    def _():
        halo_second.wait_send()

    def project(s):
        def body(i, carry):
            qkv[s, i] = dot(h1[...], wt[3 * s, rows_at(QUARTER * i, 384), :], NT).astype(bf16)
            return carry

        lax.fori_loop(0, 3, body, 0)

    def key_bias(j, k0, count):
        mine = seg[SEG * (j + 3 * high)]
        return [jnp.where(seg[SEG * (k0 + i + 3 * high)] == mine, 0.0, NEG) for i in range(count)]

    lane_pair = lax.broadcasted_iota(jnp.int32, (SEG, 256), 1)
    pair_masks = [
        [(lane_pair >= HEAD * hd - a) & (lane_pair < HEAD * (hd + 1) - a) for hd in hds] for a, hds in PAIRS
    ]

    def stacked(value, masks):
        value = value.astype(f32)
        return jnp.concatenate([jnp.where(m, value, 0.0).astype(bf16) for m in masks], axis=0)

    def attend(s, j, k0, count):
        r = rows_at(j * SEG, SEG, SEG)
        keys = slice(k0 * SEG, (k0 + count) * SEG)
        bias = key_bias(j, k0, count)
        out = [jnp.zeros((SEG, 128), f32) for _ in range(3)]
        lse = jnp.zeros((SEG, 128), f32)
        lane = lax.broadcasted_iota(jnp.int32, (SEG, 128), 1)
        for (a, hds), masks in zip(PAIRS, pair_masks):
            cols = slice(a, a + 256)
            scores = dot(stacked(qkv[s, 0, r, cols], masks), qkv[s, 1, keys, cols], NT) * FACTOR
            scores = jnp.concatenate(
                [scores[:, i * SEG : (i + 1) * SEG] + bias[i] for i in range(count)], axis=1
            )
            top = jnp.max(scores, axis=1, keepdims=True)
            weights = jnp.exp(scores - top)
            total = jnp.sum(weights, axis=1, keepdims=True)
            prob = (weights * (1.0 / total)).astype(bf16)
            res = dot(prob, qkv[s, 2, keys, cols], NN)
            log_total = top + jnp.log(total)
            for i, hd in enumerate(hds):
                part = jnp.where(masks[i], res[i * SEG : (i + 1) * SEG, :], 0.0)
                out[a // 128] += part[:, 0:128]
                out[a // 128 + 1] += part[:, 128:256]
                lse = jnp.where(lane == hd, log_total[i * SEG : (i + 1) * SEG, :], lse)
        for i in range(3):
            heads[s, r, i * 128 : (i + 1) * 128] = out[i].astype(bf16)
        lse_t[s, :, r] = lse.T[0:8, :]

    def for_blocks(fn, between=()):
        fn(0, 0, 2)
        for hook in between[0:1]:
            hook()
        fn(1, 0, 5)
        for hook in between[1:2]:
            hook()

        def body(j, carry):
            fn(j, 1, 4)
            return carry

        lax.fori_loop(2, 5, body, 0)

    load_d.wait()
    ag_two(0)
    ag_z(2)
    project(0)
    ag_three(0)
    for_blocks(functools.partial(attend, 0))
    ag_one(1)
    ag_end(0)
    project(1)
    for_blocks(functools.partial(attend, 1))
    ag_two(1)
    def order(i):
        return 1 - high if i == 0 else high

    if gather_wide:
        for mask in range(1, 8):
            send(("silu",), silu_all.at[b], silu_all.at[b], wide_to(mask), silu_all.at[pl.ds(0, 7)])
    for i in range(2):
        cc = order(i)
        src = rows_at(off + OWN * cc, OWN)
        dst = rows_at(OWN * cc, OWN)

        def body(t, carry):
            cols = pl.ds(pl.multiple_of(t * 384, 128), 384)
            part = dot(heads[0, src, 0:QUARTER], wt[0, 3 * QUARTER : D, cols], NN)
            part += dot(heads[1, src, 0:QUARTER], wt[3, 3 * QUARTER : D, cols], NN)
            attp[dst, cols] = part.astype(bf16)
            return carry

        lax.fori_loop(0, 3, body, 0)
        if i == 0:
            send(("att", i), attp.at[dst], attr.at[dst], narrow_to(1))

    ag_three(1)
    ag_one(2)
    ag_two(2)
    recv(("og",), og.at[rows_at(OWN * (1 - low), OWN)])

    for i in range(2):
        cc = order(i)
        chunk = rows_at(OWN * cc, OWN)
        recv(("att", i), attr.at[chunk])
        if i == 0:
            dst = rows_at(OWN * order(1), OWN)
            send(("att", 1), attp.at[dst], attr.at[dst], narrow_to(1))

        def second_norm(t, carry):
            r = rows_at(OWN * cc + t * 32, 32, 32)
            ra = rows_at(off + OWN * cc + t * 32, 32, 32)
            block = 4 * high + 2 * cc + t // 4
            branch = attp[r, :].astype(f32) + attr[r, :].astype(f32)
            middle = tok[ra, :].astype(f32) + mod_row(2, block) * branch
            normal, _ = norm_parts(middle)
            h2[r, :] = (normal * (1.0 + mod_row(4, block)) + mod_row(3, block)).astype(bf16)
            mlpg[r, :] = (mod_row(5, block) * og[r, :].astype(f32)).astype(bf16)
            return carry

        lax.fori_loop(0, OWN // 32, second_norm, 0)
        if i == 0:
            ag_end(1)

        def units(k, carry):
            s, t = k // 3, k % 3
            cols = pl.ds(pl.multiple_of(t * 384, 128), 384)
            up = dot(h2[chunk, :], wt[3 * s + 1, :, cols], NN)
            grad = dot(mlpg[chunk, :], wt[3 * s + 2, cols, :], NT)
            square = up * up
            th = jnp.tanh(GELU_ONE * (up + GELU_TWO * up * square))
            half_one = 0.5 * (1.0 + th)
            act = up * half_one
            slope = half_one + 0.5 * up * (1.0 - th * th) * (GELU_ONE * (1.0 + 3.0 * GELU_TWO * square))
            big[rows_at(GROUP * s + OWN * cc, OWN), cols] = act.astype(bf16)
            big[rows_at(2 * GROUP + GROUP * s + OWN * cc, OWN), cols] = (grad * slope).astype(bf16)
            return carry

        if i == 0:
            lax.fori_loop(0, 3, units, 0)
            ag_three(2)
            ag_end(2)
            lax.fori_loop(3, 6, units, 0)
        else:
            lax.fori_loop(0, 6, units, 0)

        def inputs_back(t, carry):
            cols = pl.ds(pl.multiple_of(t * 384, 128), 384)
            part = dot(big[rows_at(2 * GROUP + OWN * cc, OWN), :], wt[1, cols, :], NT)
            part += dot(big[rows_at(3 * GROUP + OWN * cc, OWN), :], wt[4, cols, :], NT)
            seco[chunk, cols] = part.astype(bf16)
            return carry

        lax.fori_loop(0, 3, inputs_back, 0)
        send(("sec", i), seco.at[chunk], secr.at[chunk], narrow_to(1))

    sent(("ag",))

    def pieces(m):
        return ((pl.ds(0, 640), 2, 4), (pl.ds(640, 512), 4, 2))

    def part(m, mask, cols=slice(None), start=0, size=BLK):
        k = block_of(mask)
        if m == 3:
            return crecv.at[4 + k // 4, rows_at(k % 4 * BLK + start, size), cols]
        return wt.at[m, rows_at(k * BLK + start, size), cols]

    def rs_core(m):
        for i, mask in enumerate((0, 2, 4, 6)):
            send(("rs", m, "c"), part(m, mask ^ 1), crecv.at[m, pl.ds(i * BLK, BLK)], wide_to(1), crecv.at[m])

    def add_into(m, mask, ref, at, cols):
        def body(t, carry):
            mine = part(m, mask, cols, t * 48, 48)
            mine[...] = mine[...] + ref[m, rows_at(at + t * 48, 48), cols]
            return carry

        lax.fori_loop(0, BLK // 48, body, 0)

    def rs_one(m):
        recv(("rs", m, "c"), crecv.at[m])
        for p, (cols, first, second) in enumerate(pieces(m)):
            for mask in (first, 6):
                add_into(m, mask, crecv, mask // 2 * BLK, cols)
            for i, mask in enumerate((0, second)):
                send(
                    ("rs", m, "f", p, i), part(m, mask ^ first, cols), frecv.at[m, pl.ds(i * BLK, BLK), cols],
                    wide_to(first),
                )
        for p, (cols, first, second) in enumerate(pieces(m)):
            for mask in (0, second):
                add_into(m, mask, crecv, mask // 2 * BLK, cols)

    def rs_two(m):
        for p, (cols, first, second) in enumerate(pieces(m)):
            recv(("rs", m, "f", p, 1), frecv.at[m, pl.ds(BLK, BLK), cols])
            add_into(m, second, frecv, BLK, cols)
            send(("rs", m, "s", p), part(m, second, cols), srecv.at[m, :, cols], wide_to(second))
        for p, (cols, first, second) in enumerate(pieces(m)):
            recv(("rs", m, "f", p, 0), frecv.at[m, pl.ds(0, BLK), cols])
            add_into(m, 0, frecv, 0, cols)

    outs = []

    def rs_copy(m):
        return remote(("rs", m, "z"), part(m, 0), zrecv.at[m - 3], narrow_to(2))

    def rs_start(m, here):
        @pl.when(here)
        def _():
            rs_copy(m).start()

    def rs_three(m):
        for p, (cols, _, _) in enumerate(pieces(m)):
            recv(("rs", m, "s", p), srecv.at[m, :, cols])
            add_into(m, 0, srecv, 0, cols)
        if m >= 3:
            sends["rs", m, "z"] = rs_copy(m)
            if m > 3:
                rs_start(m, halo_source)
        else:
            outs.append(load(("own", m), part(m, 0), gown_o.at[m]))

    def rs_four(m):
        recv(("rs", m + 3, "z"), zrecv.at[m])
        outs.append(load(("far", m), zrecv.at[m], gfar_o.at[m]))

    def down(t, carry):
        cols = pl.ds(pl.multiple_of(t * 384, 128), 384)
        part = dot(big[0:GROUP, :], wt[2, :, cols], NN)
        part += dot(big[GROUP : 2 * GROUP, :], wt[5, :, cols], NN)
        mlpp[:, :, cols] = part.astype(bf16).reshape(2, OWN, 384)
        return carry

    def by_columns(fn, count=5):
        def body(t, carry):
            fn(pl.ds(pl.multiple_of(jnp.minimum(t * 256, D - 256), 128), 256))
            return carry

        lax.fori_loop(0, count, body, 0)

    def down_grad(s):
        def tile(cols):
            wt[3 * s + 2, :, cols] = dot(big[pl.ds(GROUP * s, GROUP), :], mlpg[:, cols], TN).astype(bf16)

        by_columns(tile)

    def up_grad(s):
        def tile(cols):
            wt[3 * s + 1, :, cols] = dot(h2[...], big[pl.ds(2 * GROUP + GROUP * s, GROUP), cols], TN).astype(bf16)

        by_columns(tile)

    up_grad(1)
    rs_core(4)
    msum[...] = jnp.zeros((2, 6, 8, D), f32)
    for i in range(2):
        cc = order(i)
        chunk = rows_at(OWN * cc, OWN)
        recv(("sec", i), secr.at[chunk])

        def parts(t):
            r = rows_at(OWN * cc + t * 32, 32, 32)
            ra = rows_at(off + OWN * cc + t * 32, 32, 32)
            block = 4 * high + 2 * cc + t // 4
            branch = attp[r, :].astype(f32) + attr[r, :].astype(f32)
            gate = mod_row(2, block)
            normal, scale = norm_parts(tok[ra, :].astype(f32) + gate * branch)
            grad = seco[r, :].astype(f32) + secr[r, :].astype(f32)
            mid = og[r, :].astype(f32) + norm_back(normal, scale, grad * (1.0 + mod_row(4, block)))
            attg[ra, :] = (gate * mid).astype(bf16)
            return branch, normal, grad, mid

        @pl.when(cc == low)
        def _():
            def body(t, carry):
                branch, normal, grad, mid = parts(t)
                mgrad[rows_at(t * 32, 32, 32), :] = mid
                at = t // 4
                for k, v in ((2, mid * branch), (3, grad), (4, grad * normal)):
                    msum[at, k] += by_eight(v)
                return carry

            lax.fori_loop(0, OWN // 32, body, 0)

        @pl.when(cc != low)
        def _():
            def body(t, carry):
                parts(t)
                return carry

            lax.fori_loop(0, OWN // 32, body, 0)

        if i == 0:
            r = rows_at(off + 384 * (1 - high) + 64 * low, 64)
            send(("ahalo", 0), attg.at[r], attg.at[rows_at(halo_there + 64 * low, 64)], narrow_to(2))
            rs_one(4)
            lax.fori_loop(0, 3, down, 0)
            down_grad(1)
            rs_core(5)
            down_grad(0)
            rs_core(2)
            rs_two(4)
            rs_one(5)
            r = rows_at(halo_at + 64 * low, 64)
            recv(("ahalo", 0), attg.at[r])
            send(("ahalo", 1), attg.at[r], attg.at[r], narrow_to(1))
            send(("mlp",), mlpp.at[1 - low], mlpr, narrow_to(1))

    def mix(t, carry):
        r = rows_at(OWN * low + t * 32, 32, 32)
        ra = rows_at(own_at + t * 32, 32, 32)
        rr = rows_at(t * 32, 32, 32)
        block = 4 * high + 2 * low + t // 4
        branch = attp[r, :].astype(f32) + attr[r, :].astype(f32)
        middle = tok[ra, :].astype(f32) + mod_row(2, block) * branch
        mlp = mlpp[low, rr, :].astype(f32) + mlpr[rr, :].astype(f32)
        mlpr[rr, :] = (middle + mod_row(5, block) * mlp).astype(bf16)
        msum[t // 4, 5] += by_eight(og[r, :].astype(f32) * mlp)
        return carry

    def attend_back(s, j, k0, count):
        r = rows_at(j * SEG, SEG, SEG)
        keys = slice(k0 * SEG, (k0 + count) * SEG)
        bias = key_bias(j, k0, count)
        row = lax.broadcasted_iota(jnp.int32, (256, SEG), 0)
        for (a, hds), masks in zip(PAIRS, pair_masks):
            cols = slice(a, a + 256)
            q = stacked(qkv[s, 0, r, cols], masks)
            hg = stacked(hgrad[r, cols], masks)
            top = jnp.concatenate([lse_t[s, hd : hd + 1, r] for hd in hds], axis=1)
            scores = dot(qkv[s, 1, keys, cols], q, NT) * FACTOR
            prob = jnp.exp(
                jnp.concatenate(
                    [scores[i * SEG : (i + 1) * SEG, :] - (top - bias[i]) for i in range(count)], axis=0
                )
            )
            prob_grad = dot(qkv[s, 2, keys, cols], hg, NT)
            inner = jnp.sum(prob * prob_grad, axis=0, keepdims=True)
            score_grad = (prob * (prob_grad - inner)).astype(bf16)
            facc[0, keys, cols] += dot(score_grad, q, NN)
            facc[1, keys, cols] += dot(prob.astype(bf16), hg, NN)
            res = dot(keys_t[a : a + 256, keys], score_grad, NN)
            total = jnp.zeros((256, SEG), f32)
            for i, hd in enumerate(hds):
                mine = (row >= HEAD * hd - a) & (row < HEAD * (hd + 1) - a)
                total += jnp.where(mine, res[:, i * SEG : (i + 1) * SEG], 0.0)
            dq_t[a : a + 256, r] += total

    def pack(s):
        lane = lax.broadcasted_iota(jnp.int32, (128, 384), 1)

        def body(t, carry):
            ra = rows_at(off + t * 128, 128, 128)
            rg = rows_at(GROUP * s + t * 128, 128, 128)
            q = jnp.where(lane < QUARTER, dq_t[:, ra].T * FACTOR, 0.0)
            k = pltpu.roll(jnp.where(lane < QUARTER, facc[0, ra, :] * FACTOR, 0.0), 32, 1)
            v = pltpu.roll(jnp.where(lane < QUARTER, facc[1, ra, :], 0.0), 64, 1)
            hd = pltpu.roll(heads[s, ra, :].astype(f32), 96, 1)
            tiles = [
                q[:, 0:128],
                q[:, 128:256],
                q[:, 256:384] + k[:, 0:128],
                k[:, 128:256],
                k[:, 256:384] + v[:, 0:128],
                v[:, 128:256],
                v[:, 256:384],
            ]
            for i, tile in enumerate(tiles):
                big[rg, i * 128 : (i + 1) * 128] = tile.astype(bf16)
            heads[s, ra, :] = hd.astype(bf16)
            return carry

        lax.fori_loop(0, GROUP // 128, body, 0)

    def first_back(half, at):
        def tile(cols):
            total = dot(big[rows_at(OWN * half, OWN), 0 : 3 * QUARTER], wt[0, 0 : 3 * QUARTER, cols], NN)
            total += dot(big[rows_at(GROUP + OWN * half, OWN), 0 : 3 * QUARTER], wt[3, 0 : 3 * QUARTER, cols], NN)
            seco[pl.ds(at, OWN), cols] = total.astype(bf16)

        by_columns(tile)

    def attn_grad(s):
        rg = rows_at(off, GROUP)

        def put(cols, value):
            value = value.astype(bf16)
            if s == 0:
                wt[0, :, cols] = value
            else:
                crecv[4, :, cols] = value[: 4 * BLK, :]
                crecv[5, :, cols] = value[4 * BLK :, :]

        def tile(cols):
            put(cols, dot(h1[rg, :], big[pl.ds(GROUP * s, GROUP), cols], TN))

        by_columns(tile, 3)
        value = dot(h1[rg, :], big[pl.ds(GROUP * s, GROUP), 768:896], TN)
        value += dot(attg[rg, :], heads[s, rg, 0:128], TN)
        put(slice(768, 896), value)
        put(slice(896, D), dot(attg[rg, :], heads[s, rg, 128:384], TN))

    def heads_rows(s, r):
        hgrad[r, 0:QUARTER] = dot(attg[r, :], wt[3 * s, 3 * QUARTER : D, :], NT).astype(bf16)

    def heads_back(s, early, middle):
        heads_rows(s, rows_at(off, GROUP))
        facc[...] = jnp.zeros((2, ATT, 384), f32)
        dq_t[...] = jnp.zeros((384, ATT), f32)
        for i in range(5):
            keys_t[:, i * 128 : (i + 1) * 128] = qkv[s, 1, i * 128 : (i + 1) * 128, :].T
        attend_back(s, 1, 0, 5)
        early()

        def body(j, carry):
            attend_back(s, j, 1, 4)
            return carry

        lax.fori_loop(2, 4, body, 0)
        middle()
        heads_rows(s, rows_at(halo_at, SEG))
        attend_back(s, 0, 0, 2)
        attend_back(s, 4, 1, 4)
        pack(s)

    def middle_far():
        recv(("ahalo", 1), attg.at[rows_at(halo_at + 64 * (1 - low), 64)])
        rs_start(4, jnp.logical_not(halo_source))
        rs_two(5)


    rs_three(4)
    heads_back(1, lambda: None, middle_far)
    rs_one(2)
    attn_grad(1)
    rs_core(3)
    rs_three(5)
    up_grad(0)
    rs_core(1)
    rs_one(3)
    rs_start(5, jnp.logical_not(halo_source))
    heads_back(0, lambda: None, lambda: None)
    rs_two(2)
    rs_one(1)
    sent(("sec",))
    first_back(1 - low, 0)
    send(("first",), seco.at[pl.ds(0, OWN)], firstr, narrow_to(1))
    first_back(low, OWN)
    rs_two(3)
    attn_grad(0)
    rs_core(0)
    rs_three(2)
    recv(("mlp",), mlpr)
    lax.fori_loop(0, OWN // 32, mix, 0)
    outs.append(load("mixed", mlpr, mixed_o))
    rs_one(0)
    rs_three(3)
    rs_two(1)

    recv(("first",), firstr)
    rs_start(3, jnp.logical_not(halo_source))

    def tokens_back(t, carry):
        ra = rows_at(own_at + t * 32, 32, 32)
        rr = rows_at(t * 32, 32, 32)
        block = 4 * high + 2 * low + t // 4
        normal, scale = norm_parts(tok[ra, :].astype(f32))
        grad = seco[rows_at(OWN + t * 32, 32, 32), :].astype(f32) + firstr[rr, :].astype(f32)
        res = mgrad[rr, :] + norm_back(normal, scale, grad * (1.0 + mod_row(1, block)))
        firstr[rr, :] = res.astype(bf16)
        for k, v in ((0, grad), (1, grad * normal)):
            msum[t // 4, k] += by_eight(v)
        return carry

    lax.fori_loop(0, OWN // 32, tokens_back, 0)
    outs.append(load("tg", firstr, tg_o))

    sent(("mod",))
    row = lax.broadcasted_iota(jnp.int32, (8, D), 0)
    lane = lax.broadcasted_iota(jnp.int32, (8, ATT), 1)
    for k in range(6):
        total = jnp.zeros((8, D), f32)
        for i in range(2):
            slot = seg[SEG * (4 * high + 2 * low + i)]
            total += jnp.where((row == slot) & (row < 4), jnp.sum(msum[i, k], axis=0, keepdims=True), 0.0)
        for i, value in ((2 * k, total[:, 0:ATT]), (2 * k + 1, pltpu.roll(total[:, 512:D], HALF, 1))):
            modrecv[i // 3, i % 3 * 4 : i % 3 * 4 + 4, :] = jnp.where(lane < HALF, value, 0.0)[0:4, :]
    for i in range(4):
        modrecv[i, 12:16, :] = jnp.zeros((4, ATT), f32)
        mgs[i] = modrecv[i].astype(bf16)
    for mask in (1, 2, 3):
        m = narrow_to(mask)[1]
        send(("mg", mask), mgs.at[m], mgr.at[mask - 1], narrow_to(mask))
    rs_three(1)
    rs_two(0)
    rs_four(2)
    rs_four(1)
    for mask in (1, 2, 3):
        recv(("mg", mask), mgr.at[mask - 1])
    rs_start(3, halo_source)
    total = modrecv[n] + mgr[0].astype(f32) + mgr[1].astype(f32) + mgr[2].astype(f32)
    mall[b] = total.astype(bf16)
    if gather_wide:
        for mask in range(1, 8):
            send(("mall",), mall.at[b], mall.at[b], wide_to(mask), mall.at[pl.ds(0, 7)])
    rs_three(0)
    rs_four(0)
    if gather_wide:
        recv(("silu",), silu_all.at[pl.ds(0, 7)])
        recv(("mall",), mall.at[pl.ds(0, 7)])
    outs.append(load("mall", mall, mall_o))
    outs.append(load("silu", silu_all, silu_o))
    for copy in outs:
        copy.wait()
    sent(())


def finish(
    step, mixed_h, tg_h, gown_h, gfar_h, mall_h, silu_h,
    mixed_o, tg_o, wada_o, bada_o, gqkv_o, gproj_o, gup_o, gdown_o,
    gown, gfar, mall, silu, mixed, tg, wada, sums, bada, gqkv, gproj, gffn, sem,
):
    ids = Names()

    def move(src, dst):
        copy = pltpu.make_async_copy(src, dst, sem.at[ids(len(ids.ids))])
        copy.start()
        return copy

    ins = [move(mall_h, mall), move(silu_h, silu), move(gown_h, gown), move(gfar_h, gfar)]
    outs = []
    rows = [move(mixed_h, mixed), move(tg_h, tg)]
    b = lax.axis_index("wide") // step
    ins[0].wait()
    ins[1].wait()
    pick_row = lax.broadcasted_iota(jnp.int32, (BLK, D), 0) + b * BLK
    pick_col = lax.broadcasted_iota(jnp.int32, (BLK, D), 1)
    pick = jnp.where(pick_row == pick_col, 1.0, 0.0).astype(bf16)
    left = dot(pick, silu[...].reshape(128, D), NT).astype(bf16)
    third = lax.broadcasted_iota(jnp.int32, (BLK, 128), 1) % 16 // 4
    right = mall[...].reshape(128, ATT)
    for i in range(3):
        part = dot(jnp.where(third == i, left, 0), right, NN)
        total = dot(jnp.where(third[0:8] == i, 1.0, 0.0).astype(bf16), right, NN)
        if i == 1:
            part, total = pltpu.roll(part, 64, 1), pltpu.roll(total, 64, 1)
            wada[:, 512:640] += part[:, 0:128]
            wada[:, 640:D] = part[:, 128:640]
            sums[:, 512:640] += total[:, 0:128]
            sums[:, 640:D] = total[:, 128:640]
        else:
            at = i * HALF
            wada[:, at : at + HALF] = part[:, 0:HALF]
            sums[:, at : at + ATT] = total
            if i == 0:
                wada[:, HALF:640] = jnp.zeros((BLK, 64), f32)
    place = lax.axis_index("wide")
    bada[...] = pltpu.roll(sums[...], 14 * 128 - place * 216, 1)[0:1, 0:216]
    outs.append(move(wada, wada_o))
    outs.append(move(bada, bada_o))
    ins[2].wait()
    ins[3].wait()
    for m in range(3):
        total = gown[m].astype(f32) + gfar[m].astype(f32)
        if m == 0:
            gqkv[0] = total[:, 0:QUARTER]
            gqkv[1] = pltpu.roll(total[:, 256:640], 352, 1)[:, 0:QUARTER]
            gqkv[2] = pltpu.roll(total[:, 512:896], 320, 1)[:, 0:QUARTER]
            gproj[...] = pltpu.roll(total[:, 768:D], 288, 1)[:, 0:QUARTER]
            outs.append(move(gqkv, gqkv_o))
            outs.append(move(gproj, gproj_o))
        else:
            gffn[m - 1] = total
            outs.append(move(gffn.at[m - 1], (gup_o, gdown_o)[m - 1]))
    rows[0].wait()
    outs.append(move(mixed, mixed_o))
    rows[1].wait()
    outs.append(move(tg, tg_o))
    for copy in outs:
        copy.wait()


def shards(N, tokens, condition, segment, w_ada, b_ada, w_qkv, w_proj, w_up, w_down, out_grad):
    step = N // 8
    gather_wide = N == 8
    anywhere = pl.BlockSpec(memory_space=pl.ANY)
    hbm = pl.BlockSpec(memory_space=pltpu.HBM)
    vmem = pl.BlockSpec(memory_space=pltpu.VMEM)
    smem = pl.BlockSpec(memory_space=pltpu.SMEM)
    shape = jax.ShapeDtypeStruct
    V = pltpu.VMEM
    out = pl.pallas_call(
        functools.partial(kernel, gather_wide, step),
        name="block",
        out_shape=(
            shape((OWN, D), bf16),
            shape((OWN, D), bf16),
            shape((3, BLK, D), bf16),
            shape((3, BLK, D), bf16),
            shape((8, 16, ATT), bf16),
            shape((8, 16, D), bf16),
        ),
        in_specs=[smem, vmem, vmem] + [anywhere] * 7,
        out_specs=(anywhere,) * 6,
        scratch_shapes=[
            V((6, D, D), bf16),
            V((6, 4 * BLK, D), bf16),
            V((6, 2 * BLK, D), bf16),
            V((6, BLK, D), bf16),
            V((3, BLK, D), bf16),
            V((ATT, D), bf16),
            V((GROUP, D), bf16),
            V((ATT, D), bf16),
            V((2, 3, ATT, 384), bf16),
            V((2, ATT, 384), bf16),
            V((2, 8, ATT), f32),
            V((GROUP, D), bf16),
            V((GROUP, D), bf16),
            V((GROUP, D), bf16),
            V((GROUP, D), bf16),
            V((4 * GROUP, D), bf16),
            V((2, OWN, D), bf16),
            V((OWN, D), bf16),
            V((GROUP, D), bf16),
            V((GROUP, D), bf16),
            V((OWN, D), f32),
            V((ATT, D), bf16),
            V((ATT, 384), bf16),
            V((2, ATT, 384), f32),
            V((384, ATT), bf16),
            V((384, ATT), f32),
            V((OWN, D), bf16),
            V((6, 8, D), f32),
            V((4, 16, ATT), f32),
            V((8, 16, D), bf16),
            V((2, 6, 8, D), f32),
            V((4, 16, ATT), bf16),
            V((3, 16, ATT), bf16),
            V((8, 16, ATT), bf16),
            V((16, D), f32),
            pltpu.SemaphoreType.DMA((SEMS,)),
            pltpu.SemaphoreType.DMA((SEMS,)),
            pltpu.SemaphoreType.DMA((17,)),
        ],
        compiler_params=pltpu.CompilerParams(
            collective_id=0, has_side_effects=True, vmem_limit_bytes=63 * 2**20
        ),
    )(
        segment,
        condition,
        b_ada.astype(f32).reshape(3, HALF),
        tokens,
        out_grad,
        w_ada.T,
        w_qkv.transpose(1, 2, 0).reshape(3 * QUARTER, D),
        w_proj.T,
        w_up,
        w_down,
    )
    mixed, tokens_grad, gown, gfar, mall, silu = out
    mixed, tokens_grad, wada, bada, gqkv, gproj, gup, gdown = pl.pallas_call(
        functools.partial(finish, step),
        name="finish",
        out_shape=(
            shape((OWN, D), bf16),
            shape((OWN, D), bf16),
            shape((BLK, 3 * HALF), f32),
            shape((1, 216), f32),
            shape((3, BLK, QUARTER), f32),
            shape((BLK, QUARTER), f32),
            shape((BLK, D), f32),
            shape((BLK, D), f32),
        ),
        in_specs=[hbm] * 6,
        out_specs=(hbm,) * 8,
        scratch_shapes=[
            V((3, BLK, D), bf16),
            V((3, BLK, D), bf16),
            V((8, 16, ATT), bf16),
            V((8, 16, D), bf16),
            V((OWN, D), bf16),
            V((OWN, D), bf16),
            V((BLK, 3 * HALF), f32),
            V((8, 14 * 128), f32),
            V((1, 216), f32),
            V((3, BLK, QUARTER), f32),
            V((BLK, QUARTER), f32),
            V((2, BLK, D), f32),
            pltpu.SemaphoreType.DMA((16,)),
        ],
        compiler_params=pltpu.CompilerParams(vmem_limit_bytes=63 * 2**20),
    )(mixed, tokens_grad, gown, gfar, mall, silu)
    gqkv = gqkv.transpose(1, 0, 2)
    place = lax.axis_index("wide")
    if gather_wide:
        w_ada_grad, b_ada_grad = wada, bada.reshape(216)
    else:
        silu_low = jax.nn.silu(condition.astype(f32)).astype(bf16)
        mine = lax.dynamic_index_in_dim(mall, place // step, keepdims=False)
        mod_grad = jnp.concatenate([mine[4 * i : 4 * i + 4, :HALF] for i in range(3)], axis=1)
        silu_wide = lax.all_gather(silu_low, "wide", axis=0, tiled=True)
        mod_wide = lax.all_gather(mod_grad, "wide", axis=0, tiled=True)
        left = lax.dynamic_slice_in_dim(silu_wide, place * (D // N), D // N, axis=1)
        w_ada_grad = jnp.einsum("id,ic->dc", left, mod_wide, preferred_element_type=f32)
        b_all = jnp.sum(mod_wide.astype(f32), axis=0)
        groups = [[i * step + r for r in range(step)] for i in range(8)]
        gqkv, gproj, gup, gdown = (
            lax.psum_scatter(g, "wide", scatter_dimension=0, axis_index_groups=groups, tiled=True)
            for g in (gqkv, gproj, gup, gdown)
        )
        part = b_all.shape[0] // N
        b_ada_grad = lax.dynamic_slice_in_dim(b_all, place * part, part)
    return (mixed, tokens_grad, w_ada_grad, b_ada_grad, gqkv, gproj, gup, gdown)


def solution(mesh):
    placed = (
        P(("wide", "narrow"), None),
        P("wide", None),
        P("wide"),
        P(None, "narrow"),
        P("narrow"),
        P(None, None, "narrow"),
        P(None, "narrow"),
        P(None, "narrow"),
        P("narrow", None),
        P(("wide", "narrow"), None),
    )
    return jax.shard_map(
        functools.partial(shards, mesh.shape["wide"]),
        mesh=mesh,
        in_specs=placed,
        out_specs=(
            P(("wide", "narrow"), None),
            P(("wide", "narrow"), None),
            P("wide", "narrow"),
            P(("narrow", "wide")),
            P("wide", None, "narrow"),
            P("wide", "narrow"),
            P("wide", "narrow"),
            P(("narrow", "wide"), None),
        ),
        check_vma=False,
    )
```

```python
import functools
import math

import jax
import jax.numpy as jnp
from jax import lax
from jax.experimental import pallas as pl
from jax.experimental.pallas import tpu as pltpu
from jax.sharding import PartitionSpec as P

D = 1152
HEAD = 72
HEADS_LOCAL = 4
QUARTER = 288
HALF = 576
BLK = 144
SUB_A = 80
SEG = 128
OWN = 256
GROUP = 512
ATT = 640
NEG = -1e30
EPS = 1e-6
FACTOR = HEAD ** -0.5
GELU_ONE = math.sqrt(2.0 / math.pi)
GELU_TWO = 0.044715

f32, bf16 = jnp.float32, jnp.bfloat16
MESH = pl.DeviceIdType.MESH
NN = (((1,), (0,)), ((), ()))
NT = (((1,), (1,)), ((), ()))
TN = (((0,), (0,)), ((), ()))
PAIRS = ((0, (0, 1)), (128, (2, 3)))


def dot(a, b, dims):
    return lax.dot_general(a, b, dims, preferred_element_type=f32)


def rows_at(start, size, align=16):
    return pl.ds(pl.multiple_of(start, align), size)


def mean_row(v):
    return jnp.sum(v, axis=-1, keepdims=True) * (1.0 / D)


def norm_parts(v):
    centred = v - mean_row(v)
    scale = lax.rsqrt(mean_row(centred * centred) + EPS)
    return centred * scale, scale


def norm_back(normal, scale, e):
    return scale * (e - mean_row(e) - normal * mean_row(e * normal))


def by_eight(v):
    return sum(v[i : i + 8, :] for i in range(0, v.shape[0], 8))


class Names:
    def __init__(self):
        self.ids = {}

    def __call__(self, *name):
        return self.ids.setdefault(name, len(self.ids))


SEMS = 83


def kernel(
    gather_wide, step,
    seg, cond, bada, tok_h, og_h, wada_h, wqkv_h, wproj_h, wup_h, wdown_h,
    mixed_o, tg_o, gown_o, gfar_o, mall_o, silu_o,
    wt, crecv, frecv, srecv, zrecv, tok, og, h1, qkv, heads, lse_t, attp, attr, h2, mlpg, big,
    mlpp, mlpr, seco, secr, mgrad, attg, hgrad, facc, keys_t, dq_t, firstr, modblk, modrecv, silu_all, msum, msum_one, mgs, mgr, mall, silu16,
    ssem, rsem, lsem,
):
    w = lax.axis_index("wide")
    n = lax.axis_index("narrow")
    b = w // step
    bits = (b % 2, (b // 2) % 2, b // 4)
    low, high = n % 2, n // 2

    def narrow_to(mask):
        m = n
        if mask & 1:
            m = m + 1 - 2 * low
        if mask & 2:
            m = m + 2 - 4 * high
        return (w, m)

    def wide_to(mask):
        m = w
        for k in range(3):
            if mask & (1 << k):
                m = m + step * (1 << k) * (1 - 2 * bits[k])
        return (m, n)

    def block_of(mask):
        m = b
        for k in range(3):
            if mask & (1 << k):
                m = m + (1 << k) * (1 - 2 * bits[k])
        return m

    names = Names()

    def remote(name, src, dst, dev):
        k = names(*name)
        return pltpu.make_async_remote_copy(
            src_ref=src, dst_ref=dst, send_sem=ssem.at[k], recv_sem=rsem.at[k], device_id=dev, device_id_type=MESH
        )

    sends = {}

    def send(name, src, dst, dev, group=None):
        remote(name, src, dst, dev).start()
        sends[name] = remote(name, src, dst, dev) if group is None else remote(name, group, group, dev)

    def recv(name, landing):
        remote(name, landing, landing, narrow_to(1)).wait_recv()

    def sent(prefix):
        for name in [s for s in sends if s[: len(prefix)] == prefix]:
            sends.pop(name).wait_send()

    locals_ = Names()

    def load(name, src, dst):
        copy = pltpu.make_async_copy(src, dst, lsem.at[locals_(name)])
        copy.start()
        return copy

    off = 128 * high
    own_at = off + OWN * low
    other_at = off + OWN * (1 - low)
    halo_at = GROUP * (1 - high)
    halo_there = GROUP * high

    load_m = load("m", wada_h, big.at[pl.ds(0, 3 * HALF)])
    load_a = load("a", wqkv_h, wt.at[0, pl.ds(0, 3 * QUARTER)])
    load_b = load("b", wproj_h, wt.at[0, pl.ds(3 * QUARTER, QUARTER)])
    load_t = load("t", tok_h, tok.at[rows_at(own_at, OWN)])
    load_u = load("u", wup_h, wt.at[1])
    load_d = load("d", wdown_h, wt.at[2])
    load_g = load("g", og_h, og.at[rows_at(OWN * low, OWN)])
    barrier = pltpu.get_barrier_semaphore()
    partners = [narrow_to(m) for m in (1, 2, 3)] + [wide_to(m) for m in (range(1, 8) if gather_wide else (1, 2, 4))]
    for dev in partners:
        pl.semaphore_signal(barrier, inc=1, device_id=dev, device_id_type=MESH)

    c = cond[...].astype(f32)
    silu = (c / (1.0 + jnp.exp(-c))).astype(bf16).astype(f32)
    silu16[...] = jnp.zeros((16, D), f32)
    for i in range(3):
        silu16[4 * i : 4 * i + 4, :] = silu
    silu_low = silu16[...].astype(bf16)
    silu_all[b] = silu_low
    load_m.wait()
    third = lax.broadcasted_iota(jnp.int32, (16, HALF), 0) // 4
    part = jnp.zeros((16, HALF), f32)
    for i in range(3):
        value = dot(silu_low, big[HALF * i : HALF * (i + 1), :], NT) + bada[pl.ds(HALF * i, HALF)].astype(f32).reshape(1, HALF)
        part = jnp.where(third == i, value, part)
    modrecv[n, :, 0:HALF] = part
    modrecv[n, :, HALF:ATT] = jnp.zeros((16, ATT - HALF), f32)
    modblk[...] = jnp.zeros((6, 8, D), f32)
    pl.semaphore_wait(barrier, len(partners))

    def block_rows(mask, part=None):
        base = block_of(mask) * BLK
        if part is None:
            return rows_at(base, BLK)
        return rows_at(base, SUB_A) if part == 0 else rows_at(base + SUB_A, BLK - SUB_A)

    def ag_z(m):
        r = block_rows(0)
        send(("ag", m, "z"), wt.at[m, r], wt.at[3 + m, r], narrow_to(2))

    def ag_pass(m, name, mask, axis, part=None):
        r = block_rows(mask, part)
        group = wt.at[3 + m, pl.ds(0, 4 * BLK)] if axis == 1 else None
        send(("ag", m) + name, wt.at[3 + m, r], wt.at[3 + m, r], wide_to(axis), group)

    def ag_take(m, name, mask, part=None):
        recv(("ag", m) + name, wt.at[3 + m, block_rows(mask, part)])

    def ag_one(m):
        ag_take(m, ("z",), 0)
        ag_pass(m, ("x",), 0, 2)
        ag_pass(m, ("y",), 0, 4)
        ag_pass(m, ("c",), 0, 1)

    def ag_two(m):
        ag_take(m, ("x",), 2)
        ag_pass(m, ("xy",), 2, 4, 0)
        ag_take(m, ("y",), 4)
        ag_pass(m, ("yx",), 4, 2, 1)
        ag_pass(m, ("c",), 2, 1)
        ag_pass(m, ("c",), 4, 1)

    def ag_three(m):
        ag_take(m, ("xy",), 6, 0)
        ag_take(m, ("yx",), 6, 1)
        ag_pass(m, ("c",), 6, 1)

    def ag_end(m):
        recv(("ag", m, "c"), wt.at[3 + m, pl.ds(0, 4 * BLK)])

    for mask in (1, 2, 3):
        send(("mod", mask), modrecv.at[n], modrecv.at[n], narrow_to(mask))
    send(("tok",), tok_h, tok.at[rows_at(own_at, OWN)], narrow_to(1))
    halo_first = remote(
        ("halo", 0), tok_h.at[rows_at(128 * (1 - high), SEG)], tok.at[rows_at(halo_there, SEG)], narrow_to(2)
    )
    halo_second = remote(
        ("halo", 1), tok.at[rows_at(halo_at, SEG)], tok.at[rows_at(halo_at, SEG)], narrow_to(1)
    )
    halo_source = low != high

    @pl.when(halo_source)
    def _():
        halo_first.start()

    load_a.wait()
    load_b.wait()
    ag_z(0)
    for mask in (1, 2, 3):
        m = narrow_to(mask)[1]
        recv(("mod", mask), modrecv.at[m])
    for k in range(6):
        halves = [modrecv[i // 3, i % 3 * 4 : i % 3 * 4 + 4, :] for i in (2 * k, 2 * k + 1)]
        first, second = halves[0], pltpu.roll(halves[1], 64, 1)
        modblk[k, 0:4, 0:512] = first[:, 0:512]
        modblk[k, 0:4, 512:640] = first[:, 512:640] + second[:, 0:128]
        modblk[k, 0:4, 640:D] = second[:, 128:640]

    def mod_row(k, shard_block):
        return modblk[k, pl.ds(seg[shard_block * SEG], 1), :]

    def first_norm(base, size):
        def body(t, carry):
            r = rows_at(base + t * 32, 32, 32)
            block = 3 * high + (base + t * 32) // SEG
            normal, _ = norm_parts(tok[r, :].astype(f32))
            h1[r, :] = (normal * (1.0 + mod_row(1, block)) + mod_row(0, block)).astype(bf16)
            return carry

        lax.fori_loop(0, size // 32, body, 0)

    def project(s, base=0, size=ATT):
        r = rows_at(base, size, SEG)

        def body(i, carry):
            qkv[s, i, r, :] = dot(h1[r, :], wt[3 * s, rows_at(QUARTER * i, 384), :], NT).astype(bf16)
            return carry

        lax.fori_loop(0, 3, body, 0)

    load_t.wait()
    first_norm(own_at, OWN)

    @pl.when(jnp.logical_not(halo_source))
    def _():
        halo_first.wait_recv()
        halo_second.start()

    project(0, own_at, OWN)
    ag_one(0)
    load_u.wait()
    ag_z(1)
    recv(("tok",), tok.at[rows_at(other_at, OWN)])
    load_g.wait()
    send(("og",), og_h, og.at[rows_at(OWN * low, OWN)], narrow_to(1))
    first_norm(other_at, OWN)

    @pl.when(halo_source)
    def _():
        halo_second.wait_recv()
        halo_first.wait_send()

    project(0, other_at, OWN)
    first_norm(halo_at, SEG)

    @pl.when(jnp.logical_not(halo_source))
    def _():
        halo_second.wait_send()

    def key_bias(j, k0, count):
        mine = seg[SEG * (j + 3 * high)]
        return [jnp.where(seg[SEG * (k0 + i + 3 * high)] == mine, 0.0, NEG) for i in range(count)]

    lane_pair = lax.broadcasted_iota(jnp.int32, (SEG, 256), 1)
    pair_masks = [
        [(lane_pair >= HEAD * hd - a) & (lane_pair < HEAD * (hd + 1) - a) for hd in hds] for a, hds in PAIRS
    ]

    def stacked(value, masks):
        value = value.astype(f32)
        return jnp.concatenate([jnp.where(m, value, 0.0).astype(bf16) for m in masks], axis=0)

    def attend(s, j, k0, count):
        r = rows_at(j * SEG, SEG, SEG)
        keys = slice(k0 * SEG, (k0 + count) * SEG)
        bias = key_bias(j, k0, count)
        out = [jnp.zeros((SEG, 128), f32) for _ in range(3)]
        lse = jnp.zeros((SEG, 128), f32)
        lane = lax.broadcasted_iota(jnp.int32, (SEG, 128), 1)
        for (a, hds), masks in zip(PAIRS, pair_masks):
            cols = slice(a, a + 256)
            scores = dot(stacked(qkv[s, 0, r, cols], masks), qkv[s, 1, keys, cols], NT) * FACTOR
            scores = jnp.concatenate(
                [scores[:, i * SEG : (i + 1) * SEG] + bias[i] for i in range(count)], axis=1
            )
            top = jnp.max(scores, axis=1, keepdims=True)
            weights = jnp.exp(scores - top)
            total = jnp.sum(weights, axis=1, keepdims=True)
            prob = (weights * (1.0 / total)).astype(bf16)
            res = dot(prob, qkv[s, 2, keys, cols], NN)
            log_total = top + jnp.log(total)
            for i, hd in enumerate(hds):
                part = jnp.where(masks[i], res[i * SEG : (i + 1) * SEG, :], 0.0)
                out[a // 128] += part[:, 0:128]
                out[a // 128 + 1] += part[:, 128:256]
                lse = jnp.where(lane == hd, log_total[i * SEG : (i + 1) * SEG, :], lse)
        for i in range(3):
            heads[s, r, i * 128 : (i + 1) * 128] = out[i].astype(bf16)
        lse_t[s, :, r] = lse.T[0:8, :]

    def for_blocks(fn, between=()):
        fn(0, 0, 2)
        for hook in between[0:1]:
            hook()
        fn(1, 0, 5)
        for hook in between[1:2]:
            hook()

        def body(j, carry):
            fn(j, 1, 4)
            return carry

        lax.fori_loop(2, 5, body, 0)

    load_d.wait()
    ag_two(0)
    ag_z(2)
    project(0, halo_at, SEG)
    for_blocks(functools.partial(attend, 0), (lambda: None, lambda: ag_three(0)))
    ag_one(1)
    ag_end(0)
    project(1)
    for_blocks(functools.partial(attend, 1))
    ag_two(1)
    def order(i):
        return 1 - high if i == 0 else high

    if gather_wide:
        for mask in range(1, 8):
            send(("silu",), silu_all.at[b], silu_all.at[b], wide_to(mask), silu_all.at[pl.ds(0, 7)])
    for i in range(2):
        cc = order(i)
        src = rows_at(off + OWN * cc, OWN)
        dst = rows_at(OWN * cc, OWN)

        def body(t, carry):
            cols = pl.ds(pl.multiple_of(t * 384, 128), 384)
            part = dot(heads[0, src, 0:QUARTER], wt[0, 3 * QUARTER : D, cols], NN)
            part += dot(heads[1, src, 0:QUARTER], wt[3, 3 * QUARTER : D, cols], NN)
            attp[dst, cols] = part.astype(bf16)
            return carry

        lax.fori_loop(0, 3, body, 0)
        if i == 0:
            send(("att", i), attp.at[dst], attr.at[dst], narrow_to(1))

    ag_three(1)
    ag_one(2)
    ag_two(2)
    recv(("og",), og.at[rows_at(OWN * (1 - low), OWN)])

    for i in range(2):
        cc = order(i)
        chunk = rows_at(OWN * cc, OWN)
        recv(("att", i), attr.at[chunk])
        if i == 0:
            dst = rows_at(OWN * order(1), OWN)
            send(("att", 1), attp.at[dst], attr.at[dst], narrow_to(1))

        def second_norm(t, carry):
            r = rows_at(OWN * cc + t * 32, 32, 32)
            ra = rows_at(off + OWN * cc + t * 32, 32, 32)
            block = 4 * high + 2 * cc + t // 4
            branch = attp[r, :].astype(f32) + attr[r, :].astype(f32)
            middle = tok[ra, :].astype(f32) + mod_row(2, block) * branch
            normal, _ = norm_parts(middle)
            h2[r, :] = (normal * (1.0 + mod_row(4, block)) + mod_row(3, block)).astype(bf16)
            mlpg[r, :] = (mod_row(5, block) * og[r, :].astype(f32)).astype(bf16)
            return carry

        lax.fori_loop(0, OWN // 32, second_norm, 0)
        if i == 0:
            ag_end(1)

        def units(k, carry):
            s, t = k // 3, k % 3
            cols = pl.ds(pl.multiple_of(t * 384, 128), 384)
            up = dot(h2[chunk, :], wt[3 * s + 1, :, cols], NN)
            grad = dot(mlpg[chunk, :], wt[3 * s + 2, cols, :], NT)
            square = up * up
            th = jnp.tanh(GELU_ONE * (up + GELU_TWO * up * square))
            half_one = 0.5 * (1.0 + th)
            act = up * half_one
            slope = half_one + 0.5 * up * (1.0 - th * th) * (GELU_ONE * (1.0 + 3.0 * GELU_TWO * square))
            big[rows_at(GROUP * s + OWN * cc, OWN), cols] = act.astype(bf16)
            big[rows_at(2 * GROUP + GROUP * s + OWN * cc, OWN), cols] = (grad * slope).astype(bf16)
            return carry

        if i == 0:
            lax.fori_loop(0, 3, units, 0)
            ag_three(2)
            ag_end(2)
            lax.fori_loop(3, 6, units, 0)
        else:
            lax.fori_loop(0, 6, units, 0)

        def inputs_back(t, carry):
            cols = pl.ds(pl.multiple_of(t * 384, 128), 384)
            part = dot(big[rows_at(2 * GROUP + OWN * cc, OWN), :], wt[1, cols, :], NT)
            part += dot(big[rows_at(3 * GROUP + OWN * cc, OWN), :], wt[4, cols, :], NT)
            seco[chunk, cols] = part.astype(bf16)
            return carry

        lax.fori_loop(0, 3, inputs_back, 0)
        send(("sec", i), seco.at[chunk], secr.at[chunk], narrow_to(1))

    sent(("ag",))

    def pieces(m):
        return ((pl.ds(0, 640), 2, 4), (pl.ds(640, 512), 4, 2))

    def part(m, mask, cols=slice(None), start=0, size=BLK):
        k = block_of(mask)
        if m == 3:
            return crecv.at[4 + k // 4, rows_at(k % 4 * BLK + start, size), cols]
        return wt.at[m, rows_at(k * BLK + start, size), cols]

    def rs_core(m):
        for i, mask in enumerate((0, 2, 4, 6)):
            send(("rs", m, "c"), part(m, mask ^ 1), crecv.at[m, pl.ds(i * BLK, BLK)], wide_to(1), crecv.at[m])

    def add_into(m, mask, ref, at, cols):
        def body(t, carry):
            mine = part(m, mask, cols, t * 48, 48)
            mine[...] = mine[...] + ref[m, rows_at(at + t * 48, 48), cols]
            return carry

        lax.fori_loop(0, BLK // 48, body, 0)

    def rs_one(m):
        recv(("rs", m, "c"), crecv.at[m])
        for p, (cols, first, second) in enumerate(pieces(m)):
            for mask in (first, 6):
                add_into(m, mask, crecv, mask // 2 * BLK, cols)
            for i, mask in enumerate((0, second)):
                send(
                    ("rs", m, "f", p, i), part(m, mask ^ first, cols), frecv.at[m, pl.ds(i * BLK, BLK), cols],
                    wide_to(first),
                )
        for p, (cols, first, second) in enumerate(pieces(m)):
            for mask in (0, second):
                add_into(m, mask, crecv, mask // 2 * BLK, cols)

    def rs_two(m):
        for p, (cols, first, second) in enumerate(pieces(m)):
            recv(("rs", m, "f", p, 1), frecv.at[m, pl.ds(BLK, BLK), cols])
            add_into(m, second, frecv, BLK, cols)
            send(("rs", m, "s", p), part(m, second, cols), srecv.at[m, :, cols], wide_to(second))
        for p, (cols, first, second) in enumerate(pieces(m)):
            recv(("rs", m, "f", p, 0), frecv.at[m, pl.ds(0, BLK), cols])
            add_into(m, 0, frecv, 0, cols)

    outs = []

    def rs_copy(m):
        return remote(("rs", m, "z"), part(m, 0), zrecv.at[m - 3], narrow_to(2))

    def rs_start(m, here):
        @pl.when(here)
        def _():
            rs_copy(m).start()

    def rs_three(m):
        for p, (cols, _, _) in enumerate(pieces(m)):
            recv(("rs", m, "s", p), srecv.at[m, :, cols])
            add_into(m, 0, srecv, 0, cols)
        if m >= 3:
            sends["rs", m, "z"] = rs_copy(m)
            if m > 3:
                rs_start(m, halo_source)
        else:
            outs.append(load(("own", m), part(m, 0), gown_o.at[m]))

    def rs_four(m):
        recv(("rs", m + 3, "z"), zrecv.at[m])
        outs.append(load(("far", m), zrecv.at[m], gfar_o.at[m]))

    def down(t, carry):
        cols = pl.ds(pl.multiple_of(t * 384, 128), 384)
        part = dot(big[0:GROUP, :], wt[2, :, cols], NN)
        part += dot(big[GROUP : 2 * GROUP, :], wt[5, :, cols], NN)
        mlpp[:, :, cols] = part.astype(bf16).reshape(2, OWN, 384)
        return carry

    def by_columns(fn, count=5):
        def body(t, carry):
            fn(pl.ds(pl.multiple_of(jnp.minimum(t * 256, D - 256), 128), 256))
            return carry

        lax.fori_loop(0, count, body, 0)

    def down_grad(s):
        def tile(cols):
            wt[3 * s + 2, :, cols] = dot(big[pl.ds(GROUP * s, GROUP), :], mlpg[:, cols], TN).astype(bf16)

        by_columns(tile)

    def up_grad(s):
        def tile(cols):
            wt[3 * s + 1, :, cols] = dot(h2[...], big[pl.ds(2 * GROUP + GROUP * s, GROUP), cols], TN).astype(bf16)

        by_columns(tile)

    up_grad(1)
    rs_core(4)
    msum[...] = jnp.zeros((2, 4, 8, D), f32)
    msum_one[...] = jnp.zeros((4, 2, 8, D), f32)
    for i in range(2):
        cc = order(i)
        chunk = rows_at(OWN * cc, OWN)
        recv(("sec", i), secr.at[chunk])

        def parts(t):
            r = rows_at(OWN * cc + t * 32, 32, 32)
            ra = rows_at(off + OWN * cc + t * 32, 32, 32)
            block = 4 * high + 2 * cc + t // 4
            branch = attp[r, :].astype(f32) + attr[r, :].astype(f32)
            gate = mod_row(2, block)
            normal, scale = norm_parts(tok[ra, :].astype(f32) + gate * branch)
            grad = seco[r, :].astype(f32) + secr[r, :].astype(f32)
            mid = og[r, :].astype(f32) + norm_back(normal, scale, grad * (1.0 + mod_row(4, block)))
            attg[ra, :] = (gate * mid).astype(bf16)
            return branch, normal, grad, mid

        @pl.when(cc == low)
        def _():
            def body(t, carry):
                branch, normal, grad, mid = parts(t)
                mgrad[rows_at(t * 32, 32, 32), :] = mid
                at = t // 4
                for k, v in ((2, mid * branch), (3, grad), (4, grad * normal)):
                    msum[at, k - 2] += by_eight(v)
                return carry

            lax.fori_loop(0, OWN // 32, body, 0)

        @pl.when(cc != low)
        def _():
            def body(t, carry):
                parts(t)
                return carry

            lax.fori_loop(0, OWN // 32, body, 0)

        if i == 0:
            r = rows_at(off + 384 * (1 - high) + 64 * low, 64)
            send(("ahalo", 0), attg.at[r], attg.at[rows_at(halo_there + 64 * low, 64)], narrow_to(2))
            rs_one(4)
            lax.fori_loop(0, 3, down, 0)
            down_grad(1)
            rs_core(5)
            down_grad(0)
            rs_core(2)
            rs_two(4)
            rs_one(5)
            r = rows_at(halo_at + 64 * low, 64)
            recv(("ahalo", 0), attg.at[r])
            send(("ahalo", 1), attg.at[r], attg.at[r], narrow_to(1))
            send(("mlp",), mlpp.at[1 - low], mlpr, narrow_to(1))

    def mix(t, carry):
        r = rows_at(OWN * low + t * 32, 32, 32)
        ra = rows_at(own_at + t * 32, 32, 32)
        rr = rows_at(t * 32, 32, 32)
        block = 4 * high + 2 * low + t // 4
        branch = attp[r, :].astype(f32) + attr[r, :].astype(f32)
        middle = tok[ra, :].astype(f32) + mod_row(2, block) * branch
        mlp = mlpp[low, rr, :].astype(f32) + mlpr[rr, :].astype(f32)
        mlpr[rr, :] = (middle + mod_row(5, block) * mlp).astype(bf16)
        msum[t // 4, 3] += by_eight(og[r, :].astype(f32) * mlp)
        return carry

    def attend_back(s, j, k0, count):
        r = rows_at(j * SEG, SEG, SEG)
        keys = slice(k0 * SEG, (k0 + count) * SEG)
        bias = key_bias(j, k0, count)
        row = lax.broadcasted_iota(jnp.int32, (256, SEG), 0)
        for (a, hds), masks in zip(PAIRS, pair_masks):
            cols = slice(a, a + 256)
            q = stacked(qkv[s, 0, r, cols], masks)
            hg = stacked(hgrad[r, cols], masks)
            top = jnp.concatenate([lse_t[s, hd : hd + 1, r] for hd in hds], axis=1)
            scores = dot(qkv[s, 1, keys, cols], q, NT) * FACTOR
            prob = jnp.exp(
                jnp.concatenate(
                    [scores[i * SEG : (i + 1) * SEG, :] - (top - bias[i]) for i in range(count)], axis=0
                )
            )
            prob_grad = dot(qkv[s, 2, keys, cols], hg, NT)
            inner = jnp.sum(prob * prob_grad, axis=0, keepdims=True)
            score_grad = (prob * (prob_grad - inner)).astype(bf16)
            facc[0, keys, cols] += dot(score_grad, q, NN)
            facc[1, keys, cols] += dot(prob.astype(bf16), hg, NN)
            res = dot(keys_t[a : a + 256, keys], score_grad, NN)
            total = jnp.zeros((256, SEG), f32)
            for i, hd in enumerate(hds):
                mine = (row >= HEAD * hd - a) & (row < HEAD * (hd + 1) - a)
                total += jnp.where(mine, res[:, i * SEG : (i + 1) * SEG], 0.0)
            dq_t[a : a + 256, r] += total

    def pack(s):
        lane = lax.broadcasted_iota(jnp.int32, (128, 384), 1)

        def body(t, carry):
            ra = rows_at(off + t * 128, 128, 128)
            rg = rows_at(GROUP * s + t * 128, 128, 128)
            q = jnp.where(lane < QUARTER, dq_t[:, ra].T * FACTOR, 0.0)
            k = pltpu.roll(jnp.where(lane < QUARTER, facc[0, ra, :] * FACTOR, 0.0), 32, 1)
            v = pltpu.roll(jnp.where(lane < QUARTER, facc[1, ra, :], 0.0), 64, 1)
            hd = pltpu.roll(heads[s, ra, :].astype(f32), 96, 1)
            tiles = [
                q[:, 0:128],
                q[:, 128:256],
                q[:, 256:384] + k[:, 0:128],
                k[:, 128:256],
                k[:, 256:384] + v[:, 0:128],
                v[:, 128:256],
                v[:, 256:384],
            ]
            for i, tile in enumerate(tiles):
                big[rg, i * 128 : (i + 1) * 128] = tile.astype(bf16)
            heads[s, ra, :] = hd.astype(bf16)
            return carry

        lax.fori_loop(0, GROUP // 128, body, 0)

    def first_back(half, at):
        def tile(cols):
            total = dot(big[rows_at(OWN * half, OWN), 0 : 3 * QUARTER], wt[0, 0 : 3 * QUARTER, cols], NN)
            total += dot(big[rows_at(GROUP + OWN * half, OWN), 0 : 3 * QUARTER], wt[3, 0 : 3 * QUARTER, cols], NN)
            seco[pl.ds(at, OWN), cols] = total.astype(bf16)

        by_columns(tile)

    def attn_grad(s):
        rg = rows_at(off, GROUP)

        def put(cols, value):
            value = value.astype(bf16)
            if s == 0:
                wt[0, :, cols] = value
            else:
                crecv[4, :, cols] = value[: 4 * BLK, :]
                crecv[5, :, cols] = value[4 * BLK :, :]

        def tile(cols):
            put(cols, dot(h1[rg, :], big[pl.ds(GROUP * s, GROUP), cols], TN))

        by_columns(tile, 3)
        value = dot(h1[rg, :], big[pl.ds(GROUP * s, GROUP), 768:896], TN)
        value += dot(attg[rg, :], heads[s, rg, 0:128], TN)
        put(slice(768, 896), value)
        put(slice(896, D), dot(attg[rg, :], heads[s, rg, 128:384], TN))

    def heads_rows(s, r):
        hgrad[r, 0:QUARTER] = dot(attg[r, :], wt[3 * s, 3 * QUARTER : D, :], NT).astype(bf16)

    def heads_back(s, early, middle):
        heads_rows(s, rows_at(off, GROUP))
        facc[...] = jnp.zeros((2, ATT, 384), f32)
        dq_t[...] = jnp.zeros((384, ATT), f32)
        for i in range(5):
            keys_t[:, i * 128 : (i + 1) * 128] = qkv[s, 1, i * 128 : (i + 1) * 128, :].T
        attend_back(s, 1, 0, 5)
        early()

        def body(j, carry):
            attend_back(s, j, 1, 4)
            return carry

        lax.fori_loop(2, 4, body, 0)
        middle()
        heads_rows(s, rows_at(halo_at, SEG))
        attend_back(s, 0, 0, 2)
        attend_back(s, 4, 1, 4)
        pack(s)

    def middle_far():
        recv(("ahalo", 1), attg.at[rows_at(halo_at + 64 * (1 - low), 64)])
        rs_start(4, jnp.logical_not(halo_source))
        rs_two(5)


    rs_three(4)
    heads_back(1, lambda: None, middle_far)
    rs_one(2)
    attn_grad(1)
    rs_core(3)
    rs_three(5)
    up_grad(0)
    rs_core(1)
    rs_one(3)
    rs_start(5, jnp.logical_not(halo_source))
    heads_back(0, lambda: None, lambda: (rs_two(2), rs_one(1)))
    sent(("sec",))
    first_back(1 - low, 0)
    send(("first",), seco.at[pl.ds(0, OWN)], firstr, narrow_to(1))
    first_back(low, OWN)
    rs_two(3)
    attn_grad(0)
    rs_core(0)
    rs_three(2)
    recv(("mlp",), mlpr)
    lax.fori_loop(0, OWN // 32, mix, 0)
    outs.append(load("mixed", mlpr, mixed_o))

    def first_sums(t, carry):
        half = 1 - low + t // 8 * (2 * low - 1)
        normal, _ = norm_parts(tok[rows_at(off + OWN * half + t % 8 * 32, 32, 32), :].astype(f32))
        grad = seco[rows_at(t * 32, 32, 32), :].astype(f32)
        msum_one[t // 4, 0] += by_eight(grad)
        msum_one[t // 4, 1] += by_eight(grad * normal)
        return carry

    lax.fori_loop(0, GROUP // 32, first_sums, 0)
    sent(("mod",))
    row = lax.broadcasted_iota(jnp.int32, (8, D), 0)
    lane = lax.broadcasted_iota(jnp.int32, (8, ATT), 1)
    for k in range(6):
        total = jnp.zeros((8, D), f32)
        for i in range(4 if k < 2 else 2):
            half, value = (low, msum[i, k - 2]) if k > 1 else (low if i > 1 else 1 - low, msum_one[i, k])
            slot = seg[SEG * (4 * high + 2 * half + i % 2)]
            total += jnp.where((row == slot) & (row < 4), jnp.sum(value, axis=0, keepdims=True), 0.0)
        for i, value in ((2 * k, total[:, 0:ATT]), (2 * k + 1, pltpu.roll(total[:, 512:D], HALF, 1))):
            modrecv[i // 3, i % 3 * 4 : i % 3 * 4 + 4, :] = jnp.where(lane < HALF, value, 0.0)[0:4, :]
    for i in range(4):
        modrecv[i, 12:16, :] = jnp.zeros((4, ATT), f32)
        mgs[i] = modrecv[i].astype(bf16)
    for mask in (1, 2, 3):
        m = narrow_to(mask)[1]
        send(("mg", mask), mgs.at[m], mgr.at[mask - 1], narrow_to(mask))
    rs_one(0)
    rs_three(3)
    rs_start(3, jnp.logical_not(halo_source))
    rs_two(1)

    recv(("first",), firstr)
    rs_start(3, halo_source)

    def tokens_back(t, carry):
        ra = rows_at(own_at + t * 32, 32, 32)
        rr = rows_at(t * 32, 32, 32)
        block = 4 * high + 2 * low + t // 4
        normal, scale = norm_parts(tok[ra, :].astype(f32))
        grad = seco[rows_at(OWN + t * 32, 32, 32), :].astype(f32) + firstr[rr, :].astype(f32)
        res = mgrad[rr, :] + norm_back(normal, scale, grad * (1.0 + mod_row(1, block)))
        firstr[rr, :] = res.astype(bf16)
        return carry

    lax.fori_loop(0, OWN // 32, tokens_back, 0)
    outs.append(load("tg", firstr, tg_o))
    for mask in (1, 2, 3):
        recv(("mg", mask), mgr.at[mask - 1])
    total = modrecv[n] + mgr[0].astype(f32) + mgr[1].astype(f32) + mgr[2].astype(f32)
    mall[b] = total.astype(bf16)
    if gather_wide:
        for mask in range(1, 8):
            send(("mall",), mall.at[b], mall.at[b], wide_to(mask), mall.at[pl.ds(0, 7)])

    rs_two(0)
    rs_three(1)
    rs_four(2)
    rs_four(1)
    rs_three(0)
    rs_four(0)
    if gather_wide:
        recv(("silu",), silu_all.at[pl.ds(0, 7)])
        recv(("mall",), mall.at[pl.ds(0, 7)])
    outs.append(load("mall", mall, mall_o))
    outs.append(load("silu", silu_all, silu_o))
    for copy in outs:
        copy.wait()
    sent(())


def finish(
    step, mixed_h, tg_h, gown_h, gfar_h, mall_h, silu_h,
    mixed_o, tg_o, wada_o, bada_o, gqkv_o, gproj_o, gup_o, gdown_o,
    gown, gfar, mall, silu, mixed, tg, wada, sums, bada, gqkv, gproj, gffn, sem,
):
    ids = Names()

    def move(src, dst):
        copy = pltpu.make_async_copy(src, dst, sem.at[ids(len(ids.ids))])
        copy.start()
        return copy

    ins = [move(mall_h, mall), move(silu_h, silu), move(gown_h, gown), move(gfar_h, gfar)]
    outs = []
    rows = [move(mixed_h, mixed), move(tg_h, tg)]
    b = lax.axis_index("wide") // step
    ins[0].wait()
    ins[1].wait()
    pick_row = lax.broadcasted_iota(jnp.int32, (BLK, D), 0) + b * BLK
    pick_col = lax.broadcasted_iota(jnp.int32, (BLK, D), 1)
    pick = jnp.where(pick_row == pick_col, 1.0, 0.0).astype(bf16)
    left = dot(pick, silu[...].reshape(128, D), NT).astype(bf16)
    third = lax.broadcasted_iota(jnp.int32, (BLK, 128), 1) % 16 // 4
    right = mall[...].reshape(128, ATT)
    for i in range(3):
        part = dot(jnp.where(third == i, left, 0), right, NN)
        total = dot(jnp.where(third[0:8] == i, 1.0, 0.0).astype(bf16), right, NN)
        if i == 1:
            part, total = pltpu.roll(part, 64, 1), pltpu.roll(total, 64, 1)
            wada[:, 512:640] += part[:, 0:128]
            wada[:, 640:D] = part[:, 128:640]
            sums[:, 512:640] += total[:, 0:128]
            sums[:, 640:D] = total[:, 128:640]
        else:
            at = i * HALF
            wada[:, at : at + HALF] = part[:, 0:HALF]
            sums[:, at : at + ATT] = total
            if i == 0:
                wada[:, HALF:640] = jnp.zeros((BLK, 64), f32)
    place = lax.axis_index("wide")
    bada[...] = pltpu.roll(sums[...], 14 * 128 - place * 216, 1)[0:1, 0:216]
    outs.append(move(wada, wada_o))
    outs.append(move(bada, bada_o))
    ins[2].wait()
    ins[3].wait()
    for m in range(3):
        total = gown[m].astype(f32) + gfar[m].astype(f32)
        if m == 0:
            gqkv[0] = total[:, 0:QUARTER]
            gqkv[1] = pltpu.roll(total[:, 256:640], 352, 1)[:, 0:QUARTER]
            gqkv[2] = pltpu.roll(total[:, 512:896], 320, 1)[:, 0:QUARTER]
            gproj[...] = pltpu.roll(total[:, 768:D], 288, 1)[:, 0:QUARTER]
            outs.append(move(gqkv, gqkv_o))
            outs.append(move(gproj, gproj_o))
        else:
            gffn[m - 1] = total
            outs.append(move(gffn.at[m - 1], (gup_o, gdown_o)[m - 1]))
    rows[0].wait()
    outs.append(move(mixed, mixed_o))
    rows[1].wait()
    outs.append(move(tg, tg_o))
    for copy in outs:
        copy.wait()


def shards(N, tokens, condition, segment, w_ada, b_ada, w_qkv, w_proj, w_up, w_down, out_grad):
    step = N // 8
    gather_wide = N == 8
    anywhere = pl.BlockSpec(memory_space=pl.ANY)
    hbm = pl.BlockSpec(memory_space=pltpu.HBM)
    vmem = pl.BlockSpec(memory_space=pltpu.VMEM)
    smem = pl.BlockSpec(memory_space=pltpu.SMEM)
    shape = jax.ShapeDtypeStruct
    V = pltpu.VMEM
    out = pl.pallas_call(
        functools.partial(kernel, gather_wide, step),
        name="block",
        out_shape=(
            shape((OWN, D), bf16),
            shape((OWN, D), bf16),
            shape((3, BLK, D), bf16),
            shape((3, BLK, D), bf16),
            shape((8, 16, ATT), bf16),
            shape((8, 16, D), bf16),
        ),
        in_specs=[smem, vmem, vmem] + [anywhere] * 7,
        out_specs=(anywhere,) * 6,
        scratch_shapes=[
            V((6, D, D), bf16),
            V((6, 4 * BLK, D), bf16),
            V((6, 2 * BLK, D), bf16),
            V((6, BLK, D), bf16),
            V((3, BLK, D), bf16),
            V((ATT, D), bf16),
            V((GROUP, D), bf16),
            V((ATT, D), bf16),
            V((2, 3, ATT, 384), bf16),
            V((2, ATT, 384), bf16),
            V((2, 8, ATT), f32),
            V((GROUP, D), bf16),
            V((GROUP, D), bf16),
            V((GROUP, D), bf16),
            V((GROUP, D), bf16),
            V((4 * GROUP, D), bf16),
            V((2, OWN, D), bf16),
            V((OWN, D), bf16),
            V((GROUP, D), bf16),
            V((GROUP, D), bf16),
            V((OWN, D), f32),
            V((ATT, D), bf16),
            V((ATT, 384), bf16),
            V((2, ATT, 384), f32),
            V((384, ATT), bf16),
            V((384, ATT), f32),
            V((OWN, D), bf16),
            V((6, 8, D), f32),
            V((4, 16, ATT), f32),
            V((8, 16, D), bf16),
            V((2, 4, 8, D), f32),
            V((4, 2, 8, D), f32),
            V((4, 16, ATT), bf16),
            V((3, 16, ATT), bf16),
            V((8, 16, ATT), bf16),
            V((16, D), f32),
            pltpu.SemaphoreType.DMA((SEMS,)),
            pltpu.SemaphoreType.DMA((SEMS,)),
            pltpu.SemaphoreType.DMA((17,)),
        ],
        compiler_params=pltpu.CompilerParams(
            collective_id=0, has_side_effects=True, vmem_limit_bytes=63 * 2**20
        ),
    )(
        segment,
        condition,
        b_ada,
        tokens,
        out_grad,
        w_ada.T,
        w_qkv.transpose(1, 2, 0).reshape(3 * QUARTER, D),
        w_proj.T,
        w_up,
        w_down,
    )
    mixed, tokens_grad, gown, gfar, mall, silu = out
    mixed, tokens_grad, wada, bada, gqkv, gproj, gup, gdown = pl.pallas_call(
        functools.partial(finish, step),
        name="finish",
        out_shape=(
            shape((OWN, D), bf16),
            shape((OWN, D), bf16),
            shape((BLK, 3 * HALF), f32),
            shape((1, 216), f32),
            shape((3, BLK, QUARTER), f32),
            shape((BLK, QUARTER), f32),
            shape((BLK, D), f32),
            shape((BLK, D), f32),
        ),
        in_specs=[hbm] * 6,
        out_specs=(hbm,) * 8,
        scratch_shapes=[
            V((3, BLK, D), bf16),
            V((3, BLK, D), bf16),
            V((8, 16, ATT), bf16),
            V((8, 16, D), bf16),
            V((OWN, D), bf16),
            V((OWN, D), bf16),
            V((BLK, 3 * HALF), f32),
            V((8, 14 * 128), f32),
            V((1, 216), f32),
            V((3, BLK, QUARTER), f32),
            V((BLK, QUARTER), f32),
            V((2, BLK, D), f32),
            pltpu.SemaphoreType.DMA((16,)),
        ],
        compiler_params=pltpu.CompilerParams(vmem_limit_bytes=63 * 2**20),
    )(mixed, tokens_grad, gown, gfar, mall, silu)
    gqkv = gqkv.transpose(1, 0, 2)
    place = lax.axis_index("wide")
    if gather_wide:
        w_ada_grad, b_ada_grad = wada, bada.reshape(216)
    else:
        silu_low = jax.nn.silu(condition.astype(f32)).astype(bf16)
        mine = lax.dynamic_index_in_dim(mall, place // step, keepdims=False)
        mod_grad = jnp.concatenate([mine[4 * i : 4 * i + 4, :HALF] for i in range(3)], axis=1)
        silu_wide = lax.all_gather(silu_low, "wide", axis=0, tiled=True)
        mod_wide = lax.all_gather(mod_grad, "wide", axis=0, tiled=True)
        left = lax.dynamic_slice_in_dim(silu_wide, place * (D // N), D // N, axis=1)
        w_ada_grad = jnp.einsum("id,ic->dc", left, mod_wide, preferred_element_type=f32)
        b_all = jnp.sum(mod_wide.astype(f32), axis=0)
        groups = [[i * step + r for r in range(step)] for i in range(8)]
        gqkv, gproj, gup, gdown = (
            lax.psum_scatter(g, "wide", scatter_dimension=0, axis_index_groups=groups, tiled=True)
            for g in (gqkv, gproj, gup, gdown)
        )
        part = b_all.shape[0] // N
        b_ada_grad = lax.dynamic_slice_in_dim(b_all, place * part, part)
    return (mixed, tokens_grad, w_ada_grad, b_ada_grad, gqkv, gproj, gup, gdown)


def solution(mesh):
    placed = (
        P(("wide", "narrow"), None),
        P("wide", None),
        P("wide"),
        P(None, "narrow"),
        P("narrow"),
        P(None, None, "narrow"),
        P(None, "narrow"),
        P(None, "narrow"),
        P("narrow", None),
        P(("wide", "narrow"), None),
    )
    return jax.shard_map(
        functools.partial(shards, mesh.shape["wide"]),
        mesh=mesh,
        in_specs=placed,
        out_specs=(
            P(("wide", "narrow"), None),
            P(("wide", "narrow"), None),
            P("wide", "narrow"),
            P(("narrow", "wide")),
            P("wide", None, "narrow"),
            P("wide", "narrow"),
            P("wide", "narrow"),
            P(("narrow", "wide"), None),
        ),
        check_vma=False,
    )
```

```python
import functools
import math

import jax
import jax.numpy as jnp
from jax import lax
from jax.experimental import pallas as pl
from jax.experimental.pallas import tpu as pltpu
from jax.sharding import PartitionSpec as P

D = 1152
HEAD = 72
HEADS_LOCAL = 4
QUARTER = 288
HALF = 576
BLK = 144
SUB_A = 80
SEG = 128
OWN = 256
GROUP = 512
ATT = 640
NEG = -1e30
EPS = 1e-6
FACTOR = HEAD ** -0.5
GELU_ONE = math.sqrt(2.0 / math.pi)
GELU_TWO = 0.044715

f32, bf16 = jnp.float32, jnp.bfloat16
MESH = pl.DeviceIdType.MESH
NN = (((1,), (0,)), ((), ()))
NT = (((1,), (1,)), ((), ()))
TN = (((0,), (0,)), ((), ()))
PAIRS = ((0, (0, 1)), (128, (2, 3)))


def dot(a, b, dims):
    return lax.dot_general(a, b, dims, preferred_element_type=f32)


def rows_at(start, size, align=16):
    return pl.ds(pl.multiple_of(start, align), size)


def mean_row(v):
    return jnp.sum(v, axis=-1, keepdims=True) * (1.0 / D)


def norm_parts(v):
    centred = v - mean_row(v)
    scale = lax.rsqrt(mean_row(centred * centred) + EPS)
    return centred * scale, scale


def norm_back(normal, scale, e):
    return scale * (e - mean_row(e) - normal * mean_row(e * normal))


def by_eight(v):
    return sum(v[i : i + 8, :] for i in range(0, v.shape[0], 8))


class Names:
    def __init__(self):
        self.ids = {}

    def __call__(self, *name):
        return self.ids.setdefault(name, len(self.ids))


SEMS = 83


def kernel(
    gather_wide, step,
    seg, cond, bada, tok_h, og_h, wada_h, wqkv_h, wproj_h, wup_h, wdown_h,
    mixed_o, tg_o, gown_o, gfar_o, mall_o, silu_o,
    wt, crecv, frecv, srecv, zrecv, tok, og, h1, qkv, heads, lse_t, attp, attr, h2, mlpg, big,
    mlpp, mlpr, seco, secr, mgrad, attg, hgrad, facc, keys_t, dq_t, firstr, modblk, modrecv, silu_all, msum, msum_one, mgs, mgr, mall, silu16,
    ssem, rsem, lsem,
):
    w = lax.axis_index("wide")
    n = lax.axis_index("narrow")
    b = w // step
    bits = (b % 2, (b // 2) % 2, b // 4)
    low, high = n % 2, n // 2

    def narrow_to(mask):
        m = n
        if mask & 1:
            m = m + 1 - 2 * low
        if mask & 2:
            m = m + 2 - 4 * high
        return (w, m)

    def wide_to(mask):
        m = w
        for k in range(3):
            if mask & (1 << k):
                m = m + step * (1 << k) * (1 - 2 * bits[k])
        return (m, n)

    def block_of(mask):
        m = b
        for k in range(3):
            if mask & (1 << k):
                m = m + (1 << k) * (1 - 2 * bits[k])
        return m

    names = Names()

    def remote(name, src, dst, dev):
        k = names(*name)
        return pltpu.make_async_remote_copy(
            src_ref=src, dst_ref=dst, send_sem=ssem.at[k], recv_sem=rsem.at[k], device_id=dev, device_id_type=MESH
        )

    sends = {}

    def send(name, src, dst, dev, group=None):
        remote(name, src, dst, dev).start()
        sends[name] = remote(name, src, dst, dev) if group is None else remote(name, group, group, dev)

    def recv(name, landing):
        remote(name, landing, landing, narrow_to(1)).wait_recv()

    def sent(prefix):
        for name in [s for s in sends if s[: len(prefix)] == prefix]:
            sends.pop(name).wait_send()

    locals_ = Names()

    def load(name, src, dst):
        copy = pltpu.make_async_copy(src, dst, lsem.at[locals_(name)])
        copy.start()
        return copy

    off = 128 * high
    own_at = off + OWN * low
    other_at = off + OWN * (1 - low)
    halo_at = GROUP * (1 - high)
    halo_there = GROUP * high

    load_m = load("m", wada_h, big.at[pl.ds(0, 3 * HALF)])
    load_a = load("a", wqkv_h, wt.at[0, pl.ds(0, 3 * QUARTER)])
    load_b = load("b", wproj_h, wt.at[0, pl.ds(3 * QUARTER, QUARTER)])
    load_t = load("t", tok_h, tok.at[rows_at(own_at, OWN)])
    load_u = load("u", wup_h, wt.at[1])
    load_d = load("d", wdown_h, wt.at[2])
    load_g = load("g", og_h, og.at[rows_at(OWN * low, OWN)])
    barrier = pltpu.get_barrier_semaphore()
    partners = [narrow_to(m) for m in (1, 2, 3)] + [wide_to(m) for m in (range(1, 8) if gather_wide else (1, 2, 4))]
    for dev in partners:
        pl.semaphore_signal(barrier, inc=1, device_id=dev, device_id_type=MESH)

    c = cond[...].astype(f32)
    silu = (c / (1.0 + jnp.exp(-c))).astype(bf16).astype(f32)
    silu16[...] = jnp.zeros((16, D), f32)
    for i in range(3):
        silu16[4 * i : 4 * i + 4, :] = silu
    silu_low = silu16[...].astype(bf16)
    silu_all[b] = silu_low
    load_m.wait()
    third = lax.broadcasted_iota(jnp.int32, (16, HALF), 0) // 4
    part = jnp.zeros((16, HALF), f32)
    for i in range(3):
        value = dot(silu_low, big[HALF * i : HALF * (i + 1), :], NT) + bada[pl.ds(HALF * i, HALF)].astype(f32).reshape(1, HALF)
        part = jnp.where(third == i, value, part)
    modrecv[n, :, 0:HALF] = part
    modrecv[n, :, HALF:ATT] = jnp.zeros((16, ATT - HALF), f32)
    modblk[...] = jnp.zeros((6, 8, D), f32)
    pl.semaphore_wait(barrier, len(partners))

    def block_rows(mask, part=None):
        base = block_of(mask) * BLK
        if part is None:
            return rows_at(base, BLK)
        return rows_at(base, SUB_A) if part == 0 else rows_at(base + SUB_A, BLK - SUB_A)

    def ag_z(m):
        r = block_rows(0)
        send(("ag", m, "z"), wt.at[m, r], wt.at[3 + m, r], narrow_to(2))

    def ag_pass(m, name, mask, axis, part=None):
        r = block_rows(mask, part)
        group = wt.at[3 + m, pl.ds(0, 4 * BLK)] if axis == 1 else None
        send(("ag", m) + name, wt.at[3 + m, r], wt.at[3 + m, r], wide_to(axis), group)

    def ag_take(m, name, mask, part=None):
        recv(("ag", m) + name, wt.at[3 + m, block_rows(mask, part)])

    def ag_one(m):
        ag_take(m, ("z",), 0)
        ag_pass(m, ("x",), 0, 2)
        ag_pass(m, ("y",), 0, 4)
        ag_pass(m, ("c",), 0, 1)

    def ag_two(m):
        ag_take(m, ("x",), 2)
        ag_pass(m, ("xy",), 2, 4, 0)
        ag_take(m, ("y",), 4)
        ag_pass(m, ("yx",), 4, 2, 1)
        ag_pass(m, ("c",), 2, 1)
        ag_pass(m, ("c",), 4, 1)

    def ag_three(m):
        ag_take(m, ("xy",), 6, 0)
        ag_take(m, ("yx",), 6, 1)
        ag_pass(m, ("c",), 6, 1)

    def ag_end(m):
        recv(("ag", m, "c"), wt.at[3 + m, pl.ds(0, 4 * BLK)])

    for mask in (1, 2, 3):
        send(("mod", mask), modrecv.at[n], modrecv.at[n], narrow_to(mask))
    send(("tok",), tok_h, tok.at[rows_at(own_at, OWN)], narrow_to(1))
    halo_first = remote(
        ("halo", 0), tok_h.at[rows_at(128 * (1 - high), SEG)], tok.at[rows_at(halo_there, SEG)], narrow_to(2)
    )
    halo_second = remote(
        ("halo", 1), tok.at[rows_at(halo_at, SEG)], tok.at[rows_at(halo_at, SEG)], narrow_to(1)
    )
    halo_source = low != high

    @pl.when(halo_source)
    def _():
        halo_first.start()

    load_a.wait()
    load_b.wait()
    ag_z(0)
    for mask in (1, 2, 3):
        m = narrow_to(mask)[1]
        recv(("mod", mask), modrecv.at[m])
    for k in range(6):
        halves = [modrecv[i // 3, i % 3 * 4 : i % 3 * 4 + 4, :] for i in (2 * k, 2 * k + 1)]
        first, second = halves[0], pltpu.roll(halves[1], 64, 1)
        modblk[k, 0:4, 0:512] = first[:, 0:512]
        modblk[k, 0:4, 512:640] = first[:, 512:640] + second[:, 0:128]
        modblk[k, 0:4, 640:D] = second[:, 128:640]

    def mod_row(k, shard_block):
        return modblk[k, pl.ds(seg[shard_block * SEG], 1), :]

    def first_norm(base, size):
        def body(t, carry):
            r = rows_at(base + t * 32, 32, 32)
            block = 3 * high + (base + t * 32) // SEG
            normal, _ = norm_parts(tok[r, :].astype(f32))
            h1[r, :] = (normal * (1.0 + mod_row(1, block)) + mod_row(0, block)).astype(bf16)
            return carry

        lax.fori_loop(0, size // 32, body, 0)

    def project(s, base=0, size=ATT):
        r = rows_at(base, size, SEG)

        def body(i, carry):
            qkv[s, i, r, :] = dot(h1[r, :], wt[3 * s, rows_at(QUARTER * i, 384), :], NT).astype(bf16)
            return carry

        lax.fori_loop(0, 3, body, 0)

    load_t.wait()
    first_norm(own_at, OWN)

    @pl.when(jnp.logical_not(halo_source))
    def _():
        halo_first.wait_recv()
        halo_second.start()

    project(0, own_at, OWN)
    ag_one(0)
    load_u.wait()
    ag_z(1)
    recv(("tok",), tok.at[rows_at(other_at, OWN)])
    load_g.wait()
    send(("og",), og_h, og.at[rows_at(OWN * low, OWN)], narrow_to(1))
    first_norm(other_at, OWN)

    @pl.when(halo_source)
    def _():
        halo_second.wait_recv()
        halo_first.wait_send()

    project(0, other_at, OWN)
    first_norm(halo_at, SEG)

    @pl.when(jnp.logical_not(halo_source))
    def _():
        halo_second.wait_send()

    def key_bias(j, k0, count):
        mine = seg[SEG * (j + 3 * high)]
        return [jnp.where(seg[SEG * (k0 + i + 3 * high)] == mine, 0.0, NEG) for i in range(count)]

    lane_pair = lax.broadcasted_iota(jnp.int32, (SEG, 256), 1)
    pair_masks = [
        [(lane_pair >= HEAD * hd - a) & (lane_pair < HEAD * (hd + 1) - a) for hd in hds] for a, hds in PAIRS
    ]

    def stacked(value, masks):
        value = value.astype(f32)
        return jnp.concatenate([jnp.where(m, value, 0.0).astype(bf16) for m in masks], axis=0)

    def attend(s, j, k0, count):
        r = rows_at(j * SEG, SEG, SEG)
        keys = slice(k0 * SEG, (k0 + count) * SEG)
        bias = key_bias(j, k0, count)
        out = [jnp.zeros((SEG, 128), f32) for _ in range(3)]
        lse = jnp.zeros((SEG, 128), f32)
        lane = lax.broadcasted_iota(jnp.int32, (SEG, 128), 1)
        for (a, hds), masks in zip(PAIRS, pair_masks):
            cols = slice(a, a + 256)
            scores = dot(stacked(qkv[s, 0, r, cols], masks), qkv[s, 1, keys, cols], NT) * FACTOR
            scores = jnp.concatenate(
                [scores[:, i * SEG : (i + 1) * SEG] + bias[i] for i in range(count)], axis=1
            )
            top = jnp.max(scores, axis=1, keepdims=True)
            weights = jnp.exp(scores - top)
            total = jnp.sum(weights, axis=1, keepdims=True)
            prob = (weights * (1.0 / total)).astype(bf16)
            res = dot(prob, qkv[s, 2, keys, cols], NN)
            log_total = top + jnp.log(total)
            for i, hd in enumerate(hds):
                part = jnp.where(masks[i], res[i * SEG : (i + 1) * SEG, :], 0.0)
                out[a // 128] += part[:, 0:128]
                out[a // 128 + 1] += part[:, 128:256]
                lse = jnp.where(lane == hd, log_total[i * SEG : (i + 1) * SEG, :], lse)
        for i in range(3):
            heads[s, r, i * 128 : (i + 1) * 128] = out[i].astype(bf16)
        lse_t[s, :, r] = lse.T[0:8, :]

    def for_blocks(fn, between=()):
        fn(0, 0, 2)
        for hook in between[0:1]:
            hook()
        fn(1, 0, 5)
        for hook in between[1:2]:
            hook()

        def body(j, carry):
            fn(j, 1, 4)
            return carry

        lax.fori_loop(2, 5, body, 0)

    load_d.wait()
    ag_two(0)
    ag_z(2)
    project(0, halo_at, SEG)
    for_blocks(functools.partial(attend, 0), (lambda: None, lambda: ag_three(0)))
    ag_one(1)
    ag_end(0)
    project(1)
    for_blocks(functools.partial(attend, 1))
    ag_two(1)
    def order(i):
        return 1 - high if i == 0 else high

    if gather_wide:
        for mask in range(1, 8):
            send(("silu",), silu_all.at[b], silu_all.at[b], wide_to(mask), silu_all.at[pl.ds(0, 7)])
    for i in range(2):
        cc = order(i)
        src = rows_at(off + OWN * cc, OWN)
        dst = rows_at(OWN * cc, OWN)

        def body(t, carry):
            cols = pl.ds(pl.multiple_of(t * 384, 128), 384)
            part = dot(heads[0, src, 0:QUARTER], wt[0, 3 * QUARTER : D, cols], NN)
            part += dot(heads[1, src, 0:QUARTER], wt[3, 3 * QUARTER : D, cols], NN)
            attp[dst, cols] = part.astype(bf16)
            return carry

        lax.fori_loop(0, 3, body, 0)
        if i == 0:
            send(("att", i), attp.at[dst], attr.at[dst], narrow_to(1))

    ag_three(1)
    ag_one(2)
    ag_two(2)
    recv(("og",), og.at[rows_at(OWN * (1 - low), OWN)])

    for i in range(2):
        cc = order(i)
        chunk = rows_at(OWN * cc, OWN)
        recv(("att", i), attr.at[chunk])
        if i == 0:
            dst = rows_at(OWN * order(1), OWN)
            send(("att", 1), attp.at[dst], attr.at[dst], narrow_to(1))

        def second_norm(t, carry):
            r = rows_at(OWN * cc + t * 32, 32, 32)
            ra = rows_at(off + OWN * cc + t * 32, 32, 32)
            block = 4 * high + 2 * cc + t // 4
            branch = attp[r, :].astype(f32) + attr[r, :].astype(f32)
            middle = tok[ra, :].astype(f32) + mod_row(2, block) * branch
            normal, _ = norm_parts(middle)
            h2[r, :] = (normal * (1.0 + mod_row(4, block)) + mod_row(3, block)).astype(bf16)
            mlpg[r, :] = (mod_row(5, block) * og[r, :].astype(f32)).astype(bf16)
            return carry

        lax.fori_loop(0, OWN // 32, second_norm, 0)
        if i == 0:
            ag_end(1)

        def units(k, carry):
            s, t = k // 3, k % 3
            cols = pl.ds(pl.multiple_of(t * 384, 128), 384)
            up = dot(h2[chunk, :], wt[3 * s + 1, :, cols], NN)
            grad = dot(mlpg[chunk, :], wt[3 * s + 2, cols, :], NT)
            square = up * up
            th = jnp.tanh(GELU_ONE * (up + GELU_TWO * up * square))
            half_one = 0.5 * (1.0 + th)
            act = up * half_one
            slope = half_one + 0.5 * up * (1.0 - th * th) * (GELU_ONE * (1.0 + 3.0 * GELU_TWO * square))
            big[rows_at(GROUP * s + OWN * cc, OWN), cols] = act.astype(bf16)
            big[rows_at(2 * GROUP + GROUP * s + OWN * cc, OWN), cols] = (grad * slope).astype(bf16)
            return carry

        if i == 0:
            lax.fori_loop(0, 3, units, 0)
            ag_three(2)
            ag_end(2)
            lax.fori_loop(3, 6, units, 0)
        else:
            lax.fori_loop(0, 6, units, 0)

        def inputs_back(t, carry):
            cols = pl.ds(pl.multiple_of(t * 384, 128), 384)
            part = dot(big[rows_at(2 * GROUP + OWN * cc, OWN), :], wt[1, cols, :], NT)
            part += dot(big[rows_at(3 * GROUP + OWN * cc, OWN), :], wt[4, cols, :], NT)
            seco[chunk, cols] = part.astype(bf16)
            return carry

        lax.fori_loop(0, 3, inputs_back, 0)
        send(("sec", i), seco.at[chunk], secr.at[chunk], narrow_to(1))

    sent(("ag",))

    def pieces(m):
        return ((pl.ds(0, 640), 2, 4), (pl.ds(640, 512), 4, 2))

    def part(m, mask, cols=slice(None), start=0, size=BLK):
        k = block_of(mask)
        if m == 3:
            return crecv.at[4 + k // 4, rows_at(k % 4 * BLK + start, size), cols]
        return wt.at[m, rows_at(k * BLK + start, size), cols]

    def rs_core(m):
        for i, mask in enumerate((0, 2, 4, 6)):
            send(("rs", m, "c"), part(m, mask ^ 1), crecv.at[m, pl.ds(i * BLK, BLK)], wide_to(1), crecv.at[m])

    def add_into(m, mask, ref, at, cols):
        def body(t, carry):
            mine = part(m, mask, cols, t * 48, 48)
            mine[...] = mine[...] + ref[m, rows_at(at + t * 48, 48), cols]
            return carry

        lax.fori_loop(0, BLK // 48, body, 0)

    def rs_one(m):
        recv(("rs", m, "c"), crecv.at[m])
        for p, (cols, first, second) in enumerate(pieces(m)):
            for mask in (first, 6):
                add_into(m, mask, crecv, mask // 2 * BLK, cols)
            for i, mask in enumerate((0, second)):
                send(
                    ("rs", m, "f", p, i), part(m, mask ^ first, cols), frecv.at[m, pl.ds(i * BLK, BLK), cols],
                    wide_to(first),
                )
        for p, (cols, first, second) in enumerate(pieces(m)):
            for mask in (0, second):
                add_into(m, mask, crecv, mask // 2 * BLK, cols)

    def rs_two(m):
        for p, (cols, first, second) in enumerate(pieces(m)):
            recv(("rs", m, "f", p, 1), frecv.at[m, pl.ds(BLK, BLK), cols])
            add_into(m, second, frecv, BLK, cols)
            send(("rs", m, "s", p), part(m, second, cols), srecv.at[m, :, cols], wide_to(second))
        for p, (cols, first, second) in enumerate(pieces(m)):
            recv(("rs", m, "f", p, 0), frecv.at[m, pl.ds(0, BLK), cols])
            add_into(m, 0, frecv, 0, cols)

    outs = []

    def rs_copy(m):
        return remote(("rs", m, "z"), part(m, 0), zrecv.at[m - 3], narrow_to(2))

    def rs_start(m, here):
        @pl.when(here)
        def _():
            rs_copy(m).start()

    def rs_three(m):
        for p, (cols, _, _) in enumerate(pieces(m)):
            recv(("rs", m, "s", p), srecv.at[m, :, cols])
            add_into(m, 0, srecv, 0, cols)
        if m >= 3:
            sends["rs", m, "z"] = rs_copy(m)
            if m > 3:
                rs_start(m, halo_source)
        else:
            outs.append(load(("own", m), part(m, 0), gown_o.at[m]))

    def rs_four(m):
        recv(("rs", m + 3, "z"), zrecv.at[m])
        outs.append(load(("far", m), zrecv.at[m], gfar_o.at[m]))

    def down(t, carry):
        cols = pl.ds(pl.multiple_of(t * 384, 128), 384)
        part = dot(big[0:GROUP, :], wt[2, :, cols], NN)
        part += dot(big[GROUP : 2 * GROUP, :], wt[5, :, cols], NN)
        mlpp[:, :, cols] = part.astype(bf16).reshape(2, OWN, 384)
        return carry

    def by_columns(fn, count=5):
        def body(t, carry):
            fn(pl.ds(pl.multiple_of(jnp.minimum(t * 256, D - 256), 128), 256))
            return carry

        lax.fori_loop(0, count, body, 0)

    def down_grad(s):
        def tile(cols):
            wt[3 * s + 2, :, cols] = dot(big[pl.ds(GROUP * s, GROUP), :], mlpg[:, cols], TN).astype(bf16)

        by_columns(tile)

    def up_grad(s):
        def tile(cols):
            wt[3 * s + 1, :, cols] = dot(h2[...], big[pl.ds(2 * GROUP + GROUP * s, GROUP), cols], TN).astype(bf16)

        by_columns(tile)

    up_grad(1)
    rs_core(4)
    msum[...] = jnp.zeros((2, 4, 8, D), f32)
    msum_one[...] = jnp.zeros((4, 2, 8, D), f32)
    for i in range(2):
        cc = order(i)
        chunk = rows_at(OWN * cc, OWN)
        recv(("sec", i), secr.at[chunk])

        def parts(t):
            r = rows_at(OWN * cc + t * 32, 32, 32)
            ra = rows_at(off + OWN * cc + t * 32, 32, 32)
            block = 4 * high + 2 * cc + t // 4
            branch = attp[r, :].astype(f32) + attr[r, :].astype(f32)
            gate = mod_row(2, block)
            normal, scale = norm_parts(tok[ra, :].astype(f32) + gate * branch)
            grad = seco[r, :].astype(f32) + secr[r, :].astype(f32)
            mid = og[r, :].astype(f32) + norm_back(normal, scale, grad * (1.0 + mod_row(4, block)))
            attg[ra, :] = (gate * mid).astype(bf16)
            return branch, normal, grad, mid

        @pl.when(cc == low)
        def _():
            def body(t, carry):
                branch, normal, grad, mid = parts(t)
                mgrad[rows_at(t * 32, 32, 32), :] = mid
                at = t // 4
                for k, v in ((2, mid * branch), (3, grad), (4, grad * normal)):
                    msum[at, k - 2] += by_eight(v)
                return carry

            lax.fori_loop(0, OWN // 32, body, 0)

        @pl.when(cc != low)
        def _():
            def body(t, carry):
                parts(t)
                return carry

            lax.fori_loop(0, OWN // 32, body, 0)

        if i == 0:
            r = rows_at(off + 384 * (1 - high) + 64 * low, 64)
            send(("ahalo", 0), attg.at[r], attg.at[rows_at(halo_there + 64 * low, 64)], narrow_to(2))
            rs_one(4)
            lax.fori_loop(0, 3, down, 0)
            down_grad(1)
            rs_core(5)
            down_grad(0)
            rs_core(2)
            rs_two(4)
            rs_one(5)
            r = rows_at(halo_at + 64 * low, 64)
            recv(("ahalo", 0), attg.at[r])
            send(("ahalo", 1), attg.at[r], attg.at[r], narrow_to(1))
            send(("mlp",), mlpp.at[1 - low], mlpr, narrow_to(1))

    def mix(t, carry):
        r = rows_at(OWN * low + t * 32, 32, 32)
        ra = rows_at(own_at + t * 32, 32, 32)
        rr = rows_at(t * 32, 32, 32)
        block = 4 * high + 2 * low + t // 4
        branch = attp[r, :].astype(f32) + attr[r, :].astype(f32)
        middle = tok[ra, :].astype(f32) + mod_row(2, block) * branch
        mlp = mlpp[low, rr, :].astype(f32) + mlpr[rr, :].astype(f32)
        mlpr[rr, :] = (middle + mod_row(5, block) * mlp).astype(bf16)
        msum[t // 4, 3] += by_eight(og[r, :].astype(f32) * mlp)
        return carry

    def attend_back(s, j, k0, count):
        r = rows_at(j * SEG, SEG, SEG)
        keys = slice(k0 * SEG, (k0 + count) * SEG)
        bias = key_bias(j, k0, count)
        row = lax.broadcasted_iota(jnp.int32, (256, SEG), 0)
        for (a, hds), masks in zip(PAIRS, pair_masks):
            cols = slice(a, a + 256)
            q = stacked(qkv[s, 0, r, cols], masks)
            hg = stacked(hgrad[r, cols], masks)
            top = jnp.concatenate([lse_t[s, hd : hd + 1, r] for hd in hds], axis=1)
            scores = dot(qkv[s, 1, keys, cols], q, NT) * FACTOR
            prob = jnp.exp(
                jnp.concatenate(
                    [scores[i * SEG : (i + 1) * SEG, :] - (top - bias[i]) for i in range(count)], axis=0
                )
            )
            prob_grad = dot(qkv[s, 2, keys, cols], hg, NT)
            inner = jnp.sum(prob * prob_grad, axis=0, keepdims=True)
            score_grad = (prob * (prob_grad - inner)).astype(bf16)
            facc[0, keys, cols] += dot(score_grad, q, NN)
            facc[1, keys, cols] += dot(prob.astype(bf16), hg, NN)
            res = dot(keys_t[a : a + 256, keys], score_grad, NN)
            total = jnp.zeros((256, SEG), f32)
            for i, hd in enumerate(hds):
                mine = (row >= HEAD * hd - a) & (row < HEAD * (hd + 1) - a)
                total += jnp.where(mine, res[:, i * SEG : (i + 1) * SEG], 0.0)
            dq_t[a : a + 256, r] += total

    def pack(s):
        lane = lax.broadcasted_iota(jnp.int32, (128, 384), 1)

        def body(t, carry):
            ra = rows_at(off + t * 128, 128, 128)
            rg = rows_at(GROUP * s + t * 128, 128, 128)
            q = jnp.where(lane < QUARTER, dq_t[:, ra].T * FACTOR, 0.0)
            k = pltpu.roll(jnp.where(lane < QUARTER, facc[0, ra, :] * FACTOR, 0.0), 32, 1)
            v = pltpu.roll(jnp.where(lane < QUARTER, facc[1, ra, :], 0.0), 64, 1)
            hd = pltpu.roll(heads[s, ra, :].astype(f32), 96, 1)
            tiles = [
                q[:, 0:128],
                q[:, 128:256],
                q[:, 256:384] + k[:, 0:128],
                k[:, 128:256],
                k[:, 256:384] + v[:, 0:128],
                v[:, 128:256],
                v[:, 256:384],
            ]
            for i, tile in enumerate(tiles):
                big[rg, i * 128 : (i + 1) * 128] = tile.astype(bf16)
            heads[s, ra, :] = hd.astype(bf16)
            return carry

        lax.fori_loop(0, GROUP // 128, body, 0)

    def first_back(half, at):
        def tile(cols):
            total = dot(big[rows_at(OWN * half, OWN), 0 : 3 * QUARTER], wt[0, 0 : 3 * QUARTER, cols], NN)
            total += dot(big[rows_at(GROUP + OWN * half, OWN), 0 : 3 * QUARTER], wt[3, 0 : 3 * QUARTER, cols], NN)
            seco[pl.ds(at, OWN), cols] = total.astype(bf16)

        by_columns(tile)

    def attn_grad(s):
        rg = rows_at(off, GROUP)

        def put(cols, value):
            value = value.astype(bf16)
            if s == 0:
                wt[0, :, cols] = value
            else:
                crecv[4, :, cols] = value[: 4 * BLK, :]
                crecv[5, :, cols] = value[4 * BLK :, :]

        def tile(cols):
            put(cols, dot(h1[rg, :], big[pl.ds(GROUP * s, GROUP), cols], TN))

        by_columns(tile, 3)
        value = dot(h1[rg, :], big[pl.ds(GROUP * s, GROUP), 768:896], TN)
        value += dot(attg[rg, :], heads[s, rg, 0:128], TN)
        put(slice(768, 896), value)
        put(slice(896, D), dot(attg[rg, :], heads[s, rg, 128:384], TN))

    def heads_rows(s, r):
        hgrad[r, 0:QUARTER] = dot(attg[r, :], wt[3 * s, 3 * QUARTER : D, :], NT).astype(bf16)

    def heads_back(s, early, middle):
        heads_rows(s, rows_at(off, GROUP))
        facc[...] = jnp.zeros((2, ATT, 384), f32)
        dq_t[...] = jnp.zeros((384, ATT), f32)
        for i in range(5):
            keys_t[:, i * 128 : (i + 1) * 128] = qkv[s, 1, i * 128 : (i + 1) * 128, :].T
        attend_back(s, 1, 0, 5)
        early()

        def body(j, carry):
            attend_back(s, j, 1, 4)
            return carry

        lax.fori_loop(2, 4, body, 0)
        middle()
        heads_rows(s, rows_at(halo_at, SEG))
        attend_back(s, 0, 0, 2)
        attend_back(s, 4, 1, 4)
        pack(s)

    def middle_far():
        recv(("ahalo", 1), attg.at[rows_at(halo_at + 64 * (1 - low), 64)])
        rs_start(4, jnp.logical_not(halo_source))
        rs_two(5)


    rs_three(4)
    heads_back(1, lambda: None, middle_far)
    rs_one(2)
    attn_grad(1)
    rs_core(3)
    rs_three(5)
    up_grad(0)
    rs_core(1)
    rs_one(3)
    rs_start(5, jnp.logical_not(halo_source))
    heads_back(0, lambda: None, lambda: (rs_two(2), rs_one(1)))
    sent(("sec",))
    first_back(1 - low, 0)
    send(("first",), seco.at[pl.ds(0, OWN)], firstr, narrow_to(1))
    first_back(low, OWN)
    rs_two(3)
    attn_grad(0)
    rs_core(0)
    rs_three(2)
    recv(("mlp",), mlpr)
    lax.fori_loop(0, OWN // 32, mix, 0)
    outs.append(load("mixed", mlpr, mixed_o))

    def first_sums(t, carry):
        half = 1 - low + t // 8 * (2 * low - 1)
        normal, _ = norm_parts(tok[rows_at(off + OWN * half + t % 8 * 32, 32, 32), :].astype(f32))
        grad = seco[rows_at(t * 32, 32, 32), :].astype(f32)
        msum_one[t // 4, 0] += by_eight(grad)
        msum_one[t // 4, 1] += by_eight(grad * normal)
        return carry

    lax.fori_loop(0, GROUP // 32, first_sums, 0)
    sent(("mod",))
    row = lax.broadcasted_iota(jnp.int32, (8, D), 0)
    lane = lax.broadcasted_iota(jnp.int32, (8, ATT), 1)
    for k in range(6):
        total = jnp.zeros((8, D), f32)
        for i in range(4 if k < 2 else 2):
            half, value = (low, msum[i, k - 2]) if k > 1 else (low if i > 1 else 1 - low, msum_one[i, k])
            slot = seg[SEG * (4 * high + 2 * half + i % 2)]
            total += jnp.where((row == slot) & (row < 4), jnp.sum(value, axis=0, keepdims=True), 0.0)
        for i, value in ((2 * k, total[:, 0:ATT]), (2 * k + 1, pltpu.roll(total[:, 512:D], HALF, 1))):
            modrecv[i // 3, i % 3 * 4 : i % 3 * 4 + 4, :] = jnp.where(lane < HALF, value, 0.0)[0:4, :]
    for i in range(4):
        modrecv[i, 12:16, :] = jnp.zeros((4, ATT), f32)
        mgs[i] = modrecv[i].astype(bf16)
    for mask in (1, 2, 3):
        m = narrow_to(mask)[1]
        send(("mg", mask), mgs.at[m], mgr.at[mask - 1], narrow_to(mask))
    rs_one(0)
    rs_three(3)
    rs_start(3, jnp.logical_not(halo_source))
    rs_two(1)
    rs_start(3, halo_source)
    rs_two(0)
    for mask in (1, 2, 3):
        recv(("mg", mask), mgr.at[mask - 1])
    total = modrecv[n] + mgr[0].astype(f32) + mgr[1].astype(f32) + mgr[2].astype(f32)
    mall[b] = total.astype(bf16)
    if gather_wide:
        for mask in range(1, 8):
            send(("mall",), mall.at[b], mall.at[b], wide_to(mask), mall.at[pl.ds(0, 7)])

    recv(("first",), firstr)

    def tokens_back(t, carry):
        ra = rows_at(own_at + t * 32, 32, 32)
        rr = rows_at(t * 32, 32, 32)
        block = 4 * high + 2 * low + t // 4
        normal, scale = norm_parts(tok[ra, :].astype(f32))
        grad = seco[rows_at(OWN + t * 32, 32, 32), :].astype(f32) + firstr[rr, :].astype(f32)
        res = mgrad[rr, :] + norm_back(normal, scale, grad * (1.0 + mod_row(1, block)))
        firstr[rr, :] = res.astype(bf16)
        return carry

    lax.fori_loop(0, OWN // 32, tokens_back, 0)
    outs.append(load("tg", firstr, tg_o))
    rs_three(1)
    rs_four(2)
    rs_four(1)
    rs_three(0)
    rs_four(0)
    if gather_wide:
        recv(("silu",), silu_all.at[pl.ds(0, 7)])
        recv(("mall",), mall.at[pl.ds(0, 7)])
    outs.append(load("mall", mall, mall_o))
    outs.append(load("silu", silu_all, silu_o))
    for copy in outs:
        copy.wait()
    sent(())


def finish(
    step, mixed_h, tg_h, gown_h, gfar_h, mall_h, silu_h,
    mixed_o, tg_o, wada_o, bada_o, gqkv_o, gproj_o, gup_o, gdown_o,
    gown, gfar, mall, silu, mixed, tg, wada, sums, bada, gqkv, gproj, gffn, sem,
):
    ids = Names()

    def move(src, dst):
        copy = pltpu.make_async_copy(src, dst, sem.at[ids(len(ids.ids))])
        copy.start()
        return copy

    ins = [move(gown_h, gown), move(gfar_h, gfar), move(mall_h, mall), move(silu_h, silu)]
    outs = []
    rows = [move(mixed_h, mixed), move(tg_h, tg)]
    b = lax.axis_index("wide") // step
    ins[0].wait()
    ins[1].wait()
    for m in range(3):
        total = gown[m].astype(f32) + gfar[m].astype(f32)
        if m == 0:
            gqkv[0] = total[:, 0:QUARTER]
            gqkv[1] = pltpu.roll(total[:, 256:640], 352, 1)[:, 0:QUARTER]
            gqkv[2] = pltpu.roll(total[:, 512:896], 320, 1)[:, 0:QUARTER]
            gproj[...] = pltpu.roll(total[:, 768:D], 288, 1)[:, 0:QUARTER]
            outs.append(move(gqkv, gqkv_o))
            outs.append(move(gproj, gproj_o))
        else:
            gffn[m - 1] = total
            outs.append(move(gffn.at[m - 1], (gup_o, gdown_o)[m - 1]))
    rows[0].wait()
    outs.append(move(mixed, mixed_o))
    rows[1].wait()
    outs.append(move(tg, tg_o))
    ins[2].wait()
    ins[3].wait()
    pick_row = lax.broadcasted_iota(jnp.int32, (BLK, D), 0) + b * BLK
    pick_col = lax.broadcasted_iota(jnp.int32, (BLK, D), 1)
    pick = jnp.where(pick_row == pick_col, 1.0, 0.0).astype(bf16)
    left = dot(pick, silu[...].reshape(128, D), NT).astype(bf16)
    third = lax.broadcasted_iota(jnp.int32, (BLK, 128), 1) % 16 // 4
    right = mall[...].reshape(128, ATT)
    for i in range(3):
        part = dot(jnp.where(third == i, left, 0), right, NN)
        total = dot(jnp.where(third[0:8] == i, 1.0, 0.0).astype(bf16), right, NN)
        if i == 1:
            part, total = pltpu.roll(part, 64, 1), pltpu.roll(total, 64, 1)
            wada[:, 512:640] += part[:, 0:128]
            wada[:, 640:D] = part[:, 128:640]
            sums[:, 512:640] += total[:, 0:128]
            sums[:, 640:D] = total[:, 128:640]
        else:
            at = i * HALF
            wada[:, at : at + HALF] = part[:, 0:HALF]
            sums[:, at : at + ATT] = total
            if i == 0:
                wada[:, HALF:640] = jnp.zeros((BLK, 64), f32)
    place = lax.axis_index("wide")
    bada[...] = pltpu.roll(sums[...], 14 * 128 - place * 216, 1)[0:1, 0:216]
    outs.append(move(wada, wada_o))
    outs.append(move(bada, bada_o))
    for copy in outs:
        copy.wait()


def shards(N, tokens, condition, segment, w_ada, b_ada, w_qkv, w_proj, w_up, w_down, out_grad):
    step = N // 8
    gather_wide = N == 8
    anywhere = pl.BlockSpec(memory_space=pl.ANY)
    hbm = pl.BlockSpec(memory_space=pltpu.HBM)
    vmem = pl.BlockSpec(memory_space=pltpu.VMEM)
    smem = pl.BlockSpec(memory_space=pltpu.SMEM)
    shape = jax.ShapeDtypeStruct
    V = pltpu.VMEM
    out = pl.pallas_call(
        functools.partial(kernel, gather_wide, step),
        name="block",
        out_shape=(
            shape((OWN, D), bf16),
            shape((OWN, D), bf16),
            shape((3, BLK, D), bf16),
            shape((3, BLK, D), bf16),
            shape((8, 16, ATT), bf16),
            shape((8, 16, D), bf16),
        ),
        in_specs=[smem, vmem, vmem] + [anywhere] * 7,
        out_specs=(anywhere,) * 6,
        scratch_shapes=[
            V((6, D, D), bf16),
            V((6, 4 * BLK, D), bf16),
            V((6, 2 * BLK, D), bf16),
            V((6, BLK, D), bf16),
            V((3, BLK, D), bf16),
            V((ATT, D), bf16),
            V((GROUP, D), bf16),
            V((ATT, D), bf16),
            V((2, 3, ATT, 384), bf16),
            V((2, ATT, 384), bf16),
            V((2, 8, ATT), f32),
            V((GROUP, D), bf16),
            V((GROUP, D), bf16),
            V((GROUP, D), bf16),
            V((GROUP, D), bf16),
            V((4 * GROUP, D), bf16),
            V((2, OWN, D), bf16),
            V((OWN, D), bf16),
            V((GROUP, D), bf16),
            V((GROUP, D), bf16),
            V((OWN, D), f32),
            V((ATT, D), bf16),
            V((ATT, 384), bf16),
            V((2, ATT, 384), f32),
            V((384, ATT), bf16),
            V((384, ATT), f32),
            V((OWN, D), bf16),
            V((6, 8, D), f32),
            V((4, 16, ATT), f32),
            V((8, 16, D), bf16),
            V((2, 4, 8, D), f32),
            V((4, 2, 8, D), f32),
            V((4, 16, ATT), bf16),
            V((3, 16, ATT), bf16),
            V((8, 16, ATT), bf16),
            V((16, D), f32),
            pltpu.SemaphoreType.DMA((SEMS,)),
            pltpu.SemaphoreType.DMA((SEMS,)),
            pltpu.SemaphoreType.DMA((17,)),
        ],
        compiler_params=pltpu.CompilerParams(
            collective_id=0, has_side_effects=True, vmem_limit_bytes=63 * 2**20
        ),
    )(
        segment,
        condition,
        b_ada,
        tokens,
        out_grad,
        w_ada.T,
        w_qkv.transpose(1, 2, 0).reshape(3 * QUARTER, D),
        w_proj.T,
        w_up,
        w_down,
    )
    mixed, tokens_grad, gown, gfar, mall, silu = out
    mixed, tokens_grad, wada, bada, gqkv, gproj, gup, gdown = pl.pallas_call(
        functools.partial(finish, step),
        name="finish",
        out_shape=(
            shape((OWN, D), bf16),
            shape((OWN, D), bf16),
            shape((BLK, 3 * HALF), f32),
            shape((1, 216), f32),
            shape((3, BLK, QUARTER), f32),
            shape((BLK, QUARTER), f32),
            shape((BLK, D), f32),
            shape((BLK, D), f32),
        ),
        in_specs=[hbm] * 6,
        out_specs=(hbm,) * 8,
        scratch_shapes=[
            V((3, BLK, D), bf16),
            V((3, BLK, D), bf16),
            V((8, 16, ATT), bf16),
            V((8, 16, D), bf16),
            V((OWN, D), bf16),
            V((OWN, D), bf16),
            V((BLK, 3 * HALF), f32),
            V((8, 14 * 128), f32),
            V((1, 216), f32),
            V((3, BLK, QUARTER), f32),
            V((BLK, QUARTER), f32),
            V((2, BLK, D), f32),
            pltpu.SemaphoreType.DMA((16,)),
        ],
        compiler_params=pltpu.CompilerParams(vmem_limit_bytes=63 * 2**20),
    )(mixed, tokens_grad, gown, gfar, mall, silu)
    gqkv = gqkv.transpose(1, 0, 2)
    place = lax.axis_index("wide")
    if gather_wide:
        w_ada_grad, b_ada_grad = wada, bada.reshape(216)
    else:
        silu_low = jax.nn.silu(condition.astype(f32)).astype(bf16)
        mine = lax.dynamic_index_in_dim(mall, place // step, keepdims=False)
        mod_grad = jnp.concatenate([mine[4 * i : 4 * i + 4, :HALF] for i in range(3)], axis=1)
        silu_wide = lax.all_gather(silu_low, "wide", axis=0, tiled=True)
        mod_wide = lax.all_gather(mod_grad, "wide", axis=0, tiled=True)
        left = lax.dynamic_slice_in_dim(silu_wide, place * (D // N), D // N, axis=1)
        w_ada_grad = jnp.einsum("id,ic->dc", left, mod_wide, preferred_element_type=f32)
        b_all = jnp.sum(mod_wide.astype(f32), axis=0)
        groups = [[i * step + r for r in range(step)] for i in range(8)]
        gqkv, gproj, gup, gdown = (
            lax.psum_scatter(g, "wide", scatter_dimension=0, axis_index_groups=groups, tiled=True)
            for g in (gqkv, gproj, gup, gdown)
        )
        part = b_all.shape[0] // N
        b_ada_grad = lax.dynamic_slice_in_dim(b_all, place * part, part)
    return (mixed, tokens_grad, w_ada_grad, b_ada_grad, gqkv, gproj, gup, gdown)


def solution(mesh):
    placed = (
        P(("wide", "narrow"), None),
        P("wide", None),
        P("wide"),
        P(None, "narrow"),
        P("narrow"),
        P(None, None, "narrow"),
        P(None, "narrow"),
        P(None, "narrow"),
        P("narrow", None),
        P(("wide", "narrow"), None),
    )
    return jax.shard_map(
        functools.partial(shards, mesh.shape["wide"]),
        mesh=mesh,
        in_specs=placed,
        out_specs=(
            P(("wide", "narrow"), None),
            P(("wide", "narrow"), None),
            P("wide", "narrow"),
            P(("narrow", "wide")),
            P("wide", None, "narrow"),
            P("wide", "narrow"),
            P("wide", "narrow"),
            P(("narrow", "wide"), None),
        ),
        check_vma=False,
    )
```
